512 devices in a mesh: band: 16 (over y, core), fft: 32 (over z, x).
Axes of the slice: x: 4, y: 8, z: 8, core: 2. Of those that a mesh axis runs over, the one named last changes fastest.
Arguments:
- orbitals: float32 [2, 16, 65536], P(None, 'band', 'fft'), may hold values from -6 to 6
- stick_columns: int32 [1024], P('fft'), may hold values from 0 to 32400, as said below
- stick_depths: int32 [1024, 64], P('fft'), may hold values from 0 to 96, as said below
- potential: float32 [96, 32400], P('fft'), may hold values from -1.5 to 1.5
- projectors: float32 [2, 16, 65536], P(None, None, 'fft'), may hold values from -0.1875 to 0.1875
- atom_projectors: int32 [2, 8], replicated, may hold values from 0 to 15, as said below
- couplings: float32 [2, 8, 8], replicated, may hold values from -0.9 to 0.9
- slab_orbitals: float32 [2, 64, 65536], P(None, 'band', 'fft'), may hold values from -0.0234375 to 0.0234375
Outputs:
- applied: float32 [2, 16, 65536], P(None, 'band', 'fft')
- projected_h: float32 [2, 16, 64], P(None, 'band')
- projected_correlation: float32 [2, 16, 64], P(None, 'band')
The draws below stay inside these ranges and needn't reach their ends.
Inputs may be any that keep to these rules, and one draw needn't show every extreme that they name: `stick_columns`: each device's block of 32 slots holds its sticks first and then empty slots marked 32400; every device holds 16 sticks or more, and some device exactly 32. The columns of all sticks are distinct and lie in the disk fx^2 + fy^2 <= 45^2 of signed frequencies about (0, 0); where the slots in all suffice, every column of the disk is a stick. `stick_depths`: A stick with l G-vectors lists the z indices -(l // 2), ..., l - 1 - l // 2 modulo 96, then 96 in the other slots, with l from 32 to 64; the first stick of every device has l = 64; empty stick slots hold only 96. `atom_projectors`: every projector index appears once.
All inputs are finite; a program needn't handle non-finite values.
Results may differ from the reference program's by a relative error of at most 0.000078.
Values sent between devices are 32-bit elements; how exact they have to be, the bound alone decides.
A program may use at most 128 MiB of HBM per device.

```python
import jax
import jax.numpy as jnp
from jax import lax

NX = 180
NY = 180
NZ = 96
GZ = 64
RADIUS = 45
PROJ_ATOM = 8
S_CAP = 32
ATOMS = 2
NXY = 32400
STICKS = 1024
GVECS = 65536
BLOCK = 16
SLAB = 64
NPROJ = 16
N_FFT = 32


def disk_order(key):
    shuffled = jax.random.permutation(key, NXY).astype(jnp.int32)
    column_x = shuffled // NY
    column_y = shuffled % NY
    freq_x = jnp.where(column_x < (NX + 1) // 2, column_x, column_x - NX)
    freq_y = jnp.where(column_y < (NY + 1) // 2, column_y, column_y - NY)
    inside = freq_x * freq_x + freq_y * freq_y <= RADIUS * RADIUS
    order = jnp.argsort(jnp.where(inside, 0, 1), stable=True)
    return (shuffled[order], jnp.sum(inside.astype(jnp.int32)))


def stick_usage(key):
    perm_key, full_key, disk_key = jax.random.split(key, 3)
    devices = STICKS // S_CAP
    half = S_CAP // 2
    sorted_columns, disk_count = disk_order(disk_key)
    total = jnp.minimum(disk_count, STICKS)
    extra = total - devices * half
    fullest = jax.random.randint(full_key, (), 0, devices)
    units = jnp.arange(devices * half, dtype=jnp.int32)
    unit_device = units // half
    priority = jax.random.permutation(perm_key, devices * half).astype(jnp.int32)
    score = jnp.where(unit_device == fullest, 0, devices * half) + priority
    position = jnp.argsort(jnp.argsort(score, stable=True), stable=True)
    chosen_units = (position < extra).astype(jnp.int32)
    counts = half + chosen_units.reshape(devices, half).sum(axis=1)
    slots = jnp.arange(STICKS)
    used = slots % S_CAP < counts[slots // S_CAP]
    return (used, sorted_columns)


def draw_stick_columns(key, part):
    used, sorted_columns = stick_usage(key)
    rank = jnp.cumsum(used.astype(jnp.int32)) - 1
    rank = jnp.clip(rank, 0, NXY - 1)
    chosen = sorted_columns[rank]
    return jnp.where(used, chosen, NXY).astype(jnp.int32)


def draw_stick_depths(key, part):
    used, sorted_columns = stick_usage(key)
    key = jax.random.fold_in(key, 12)
    lengths = jax.random.randint(key, (STICKS,), GZ // 2, GZ + 1)
    lengths = jnp.where(jnp.arange(STICKS) % S_CAP == 0, GZ, lengths)
    offsets = jnp.arange(GZ)[None, :]
    depths = (offsets - lengths[:, None] // 2) % NZ
    live = (offsets < lengths[:, None]) & used[:, None]
    return jnp.where(live, depths, NZ).astype(jnp.int32)


def draw_atom_projectors(key, part):
    key = jax.random.fold_in(key, 13)
    return jax.random.permutation(key, NPROJ).reshape(ATOMS, PROJ_ATOM).astype(jnp.int32)


def block_levels(key, shape, shards, low, largest):
    level, own = 1.0, jax.random.fold_in(key, 6)
    for dim, blocks in shards:
        heights = jnp.exp(jax.random.uniform(jax.random.fold_in(own, dim), (blocks,), jnp.float32, low / len(shards), largest / len(shards)))
        level = level * jnp.repeat(heights, shape[dim] // blocks).reshape([-1 if axis == dim else 1 for axis in range(len(shape))])
    return level


def normal_values(own_key, shape, width, most, cuts=(), kind=jnp.bfloat16):
    drawn = jax.random.normal(own_key, shape, jnp.float32) * width
    if len(cuts) > 0:
        drawn = block_levels(own_key, shape, cuts, -0.22, 0.18) * drawn
    return jnp.clip(drawn, min=-most, max=most).astype(kind)


def setup_inputs(seed: int = 0) -> dict:
    streams_of = jax.random.split(jax.random.key(seed), 9)
    return {
        "orbitals": normal_values(streams_of[0], (2, BLOCK, GVECS), 1.0, 6.0, ((1, 16), (2, 32)), jnp.float32),
        "stick_columns": draw_stick_columns(jax.random.fold_in(streams_of[8], 71), 0),
        "stick_depths": draw_stick_depths(jax.random.fold_in(streams_of[8], 71), 0),
        "potential": jnp.clip(jax.random.uniform(streams_of[3], (NZ, NXY), jnp.float32, -1.5, 1.5) * block_levels(streams_of[3], (NZ, NXY), ((0, 32),), -0.4, 0.0), -1.5, 1.5),
        "projectors": normal_values(streams_of[4], (2, NPROJ, GVECS), (N_FFT * S_CAP * GZ // 64) ** -0.5, 0.1875, ((2, 32),), jnp.float32),
        "atom_projectors": draw_atom_projectors(jax.random.fold_in(streams_of[8], 71), 0),
        "couplings": normal_values(streams_of[6], (ATOMS, PROJ_ATOM, PROJ_ATOM), 0.15, 0.9, (), jnp.float32),
        "slab_orbitals": normal_values(streams_of[7], (2, SLAB, GVECS), (N_FFT * S_CAP * GZ) ** -0.5, 0.0234375, ((1, 16), (2, 32)), jnp.float32),
    }


def signed_freq(index, length):
    return jnp.where(index < (length + 1) // 2, index, index - length)


def kinetic_factor(stick_columns, stick_depths):
    column_x = signed_freq(stick_columns // NY, NX)
    column_y = signed_freq(stick_columns % NY, NY)
    depth = signed_freq(stick_depths, NZ)
    squared = (column_x * column_x + column_y * column_y)[:, None] + depth * depth
    return (0.5 / (RADIUS * RADIUS)) * squared.astype(jnp.float32)


def conj_correlation(vectors, reference_rows):
    highest = lax.Precision.HIGHEST
    real_out = jnp.einsum("ng,mg->nm", vectors[0], reference_rows[0], precision=highest) + jnp.einsum("ng,mg->nm", vectors[1], reference_rows[1], precision=highest)
    imag_out = jnp.einsum("ng,mg->nm", vectors[1], reference_rows[0], precision=highest) - jnp.einsum("ng,mg->nm", vectors[0], reference_rows[1], precision=highest)
    return jnp.stack([real_out, imag_out])


def reference(orbitals, stick_columns, stick_depths, potential, projectors, atom_projectors, couplings, slab_orbitals):
    highest = lax.Precision.HIGHEST
    plane_size = NX * NY
    valid = (stick_depths < NZ) & (stick_columns[:, None] < plane_size)
    mask = valid.reshape(-1).astype(jnp.float32)
    places = jnp.where(valid, stick_depths * plane_size + stick_columns[:, None], NZ * plane_size).reshape(-1).astype(jnp.int32)
    masked = orbitals * mask
    field_potential = potential.reshape(NZ, NX, NY)

    def one_band(coefs):
        empty = jnp.zeros((NZ * plane_size + 1,), jnp.float32)
        grid_real = empty.at[places].add(coefs[0])
        grid_imag = empty.at[places].add(coefs[1])
        grid = (grid_real[:-1] + 1j * grid_imag[:-1]).reshape(NZ, NX, NY)
        field = jnp.fft.ifftn(grid) * field_potential
        spectrum = jnp.fft.fftn(field).reshape(-1)
        spectrum = jnp.concatenate([spectrum, jnp.zeros((1,), spectrum.dtype)])[places]
        return jnp.stack([jnp.real(spectrum), jnp.imag(spectrum)]).astype(jnp.float32)

    local = lax.map(one_band, jnp.transpose(masked, (1, 0, 2)))
    local = jnp.transpose(local, (1, 0, 2)) * mask
    kinetic = kinetic_factor(stick_columns, stick_depths).reshape(-1) * mask
    proj = conj_correlation(masked, projectors)
    owner = (atom_projectors[:, :, None] == jnp.arange(NPROJ, dtype=jnp.int32)[None, None, :]).astype(jnp.float32)
    dfull = jnp.einsum("aip,ail,alq->pq", owner, couplings, owner, precision=highest)
    coupled = jnp.einsum("cbq,pq->cbp", proj, dfull, precision=highest)
    first = jnp.einsum("bp,pg->bg", coupled[0], projectors[0], precision=highest)
    second = jnp.einsum("bp,pg->bg", coupled[1], projectors[1], precision=highest)
    third = jnp.einsum("bp,pg->bg", coupled[0], projectors[1], precision=highest)
    fourth = jnp.einsum("bp,pg->bg", coupled[1], projectors[0], precision=highest)
    nonlocal_term = jnp.stack([first - second, third + fourth]) * mask
    applied = kinetic * masked + local + nonlocal_term
    projected_h = conj_correlation(applied, slab_orbitals)
    projected_correlation = conj_correlation(masked, slab_orbitals)
    return applied, projected_h, projected_correlation
```

```python
import functools
import math

import jax
import jax.numpy as jnp
import numpy as np
from jax import lax
from jax.experimental import pallas as pl
from jax.experimental.pallas import tpu as pltpu
from jax.sharding import PartitionSpec as P

NX = 180
NY = 180
NZ = 96
GZ = 64
RADIUS = 45
NXY = NX * NY
NF = 32
STK = 32
KX = 96
KY = 128
U = 192
V = 256
PLANES = 3

MESH = pl.DeviceIdType.MESH
HIGH = lax.Precision.HIGH
HIGHEST = lax.Precision.HIGHEST
F32 = jnp.float32
BF16 = jnp.bfloat16
NN = (((1,), (0,)), ((), ()))
NT = (((1,), (1,)), ((), ()))


def mm(a, b, dims=NN, precision=HIGH):
    return lax.dot_general(a, b, dims, precision=precision, preferred_element_type=F32)


@functools.lru_cache(maxsize=None)
def tables():
    tau = 2.0 * math.pi
    j = np.arange(GZ)
    t1 = np.zeros((NF, 8, 2, GZ))
    t2 = np.zeros((NF, 8, 2, GZ))
    tb = np.zeros((2, GZ, 2, NF, 8))
    turn = np.zeros((2, NF, 8, 128))
    depth = np.arange(NZ + 1)
    for d in range(NF):
        for zz in range(PLANES):
            z = PLANES * d + zz
            th = tau * (j * z % NZ) / NZ
            c, s = np.cos(th), np.sin(th)
            t1[d, 2 * zz, 0], t1[d, 2 * zz, 1] = c, -s
            t1[d, 2 * zz + 1, 0], t1[d, 2 * zz + 1, 1] = s, c
            t2[d, 2 * zz, 0], t2[d, 2 * zz, 1] = -s, -c
            t2[d, 2 * zz + 1, 0], t2[d, 2 * zz + 1, 1] = c, -s
            tb[0, :, 0, d, 2 * zz], tb[0, :, 0, d, 2 * zz + 1] = c, s
            tb[0, :, 1, d, 2 * zz], tb[0, :, 1, d, 2 * zz + 1] = -s, c
            tb[1, :, 0, d, 2 * zz], tb[1, :, 0, d, 2 * zz + 1] = -s, c
            tb[1, :, 1, d, 2 * zz], tb[1, :, 1, d, 2 * zz + 1] = -c, -s
            ph = tau * (depth * z % NZ) / NZ
            turn[0, d, 2 * zz : 2 * zz + 2, : NZ + 1] = np.cos(ph)
            turn[1, d, 2 * zz : 2 * zz + 2, : NZ + 1] = np.sin(ph)
    t1, t2 = t1 / NZ, t2 / NZ
    k = np.arange(2 * RADIUS + 1) - RADIUS
    g = np.arange(NX)
    ang = tau * ((k[:, None] * g[None, :]) % NX) / NX
    c, s = np.cos(ang), np.sin(ang)
    n = 2 * RADIUS + 1
    wiy = np.zeros((2, KY, 2, V))
    wiy[0, :n, 0, :NY], wiy[0, :n, 1, :NY] = c / NY, s / NY
    wiy[1, :n, 0, :NY], wiy[1, :n, 1, :NY] = -s / NY, c / NY
    wix = np.zeros((2, U, 2, KX))
    wix[0, :NX, 0, :n], wix[0, :NX, 1, :n] = c.T / NX, -s.T / NX
    wix[1, :NX, 0, :n], wix[1, :NX, 1, :n] = s.T / NX, c.T / NX
    wfy = np.zeros((2, V, 2, KY))
    wfy[0, :NY, 0, :n], wfy[0, :NY, 1, :n] = c.T, -s.T
    wfy[1, :NY, 0, :n], wfy[1, :NY, 1, :n] = s.T, c.T
    wfx = np.zeros((2, KX, 2, U))
    wfx[0, :n, 0, :NX], wfx[0, :n, 1, :NX] = c, s
    wfx[1, :n, 0, :NX], wfx[1, :n, 1, :NX] = -s, c
    out = (
        t1.reshape(256, 128),
        t2.reshape(256, 128),
        turn.reshape(2, 256, 128),
        wiy.reshape(2 * KY, 2 * V),
        wix.reshape(2 * U, 2 * KX),
        wfy.reshape(2 * V, 2 * KY),
        wfx.reshape(2 * KX, 2 * U),
        tb.transpose(0, 1, 2, 3, 4).reshape(2, GZ, 2, 256),
    )
    back = out[7]
    back = np.transpose(back, (2, 1, 0, 3)).reshape(2 * GZ, 512)
    return tuple(np.asarray(x, np.float32) for x in out[:7]) + (np.asarray(back, np.float32),)


def kernel(
    orb, cols, deps, pot, proj, atoms, coup, slab,
    t1, t2, turn, wiy, wix, wfy, wfx, tback,
    out, out_h, out_s,
    mine, got, tiles, ret, pool, red, work, nonl, rows_s,
    sa, ra, sb, rb, ss, rs, sf, rf, sr, rr,
):
    me = lax.axis_index("fft")
    band = lax.axis_index("band")
    core = lax.rem(band, 2)
    row = band // 2
    twin = band + 1 - 2 * core

    barrier = pltpu.get_barrier_semaphore()

    def greet_fft(k, _):
        pl.semaphore_signal(barrier, inc=1, device_id={"fft": lax.rem(me + k, NF)}, device_id_type=MESH)
        return 0

    def greet_band(k, _):
        pl.semaphore_signal(barrier, inc=1, device_id={"band": lax.rem(band + 2 * k, 16)}, device_id_type=MESH)
        return 0

    lax.fori_loop(1, NF, greet_fft, 0)
    lax.fori_loop(1, 8, greet_band, 0)
    pl.semaphore_signal(barrier, inc=1, device_id={"band": twin}, device_id_type=MESH)

    pool[core, row] = jnp.concatenate([slab[0], slab[1]], axis=0)

    dep_even = deps[pl.ds(0, 16, stride=2), :]
    dep_odd = deps[pl.ds(1, 16, stride=2), :]
    dep16 = jnp.concatenate([dep_even, dep_odd], axis=1)
    mask = dep16 < NZ
    m_re = jnp.where(mask, orb[0], 0.0)
    m_im = jnp.where(mask, orb[1], 0.0)
    x2 = jnp.concatenate(
        [
            jnp.concatenate([m_re[:, :GZ], m_im[:, :GZ]], axis=1),
            jnp.concatenate([m_re[:, GZ:], m_im[:, GZ:]], axis=1),
        ],
        axis=0,
    )
    x2 = jnp.concatenate([x2, jnp.zeros((96, 128), F32)], axis=0)
    d1 = mm(t1[...], x2, NT)
    d2 = mm(t2[...], x2, NT)

    dep32 = jnp.concatenate([dep_even, dep_odd], axis=0).astype(F32)
    first = (lax.broadcasted_iota(jnp.int32, (8, GZ), 1) == 0).astype(F32)
    dep0 = mm(first, dep32, NT)
    dep0 = jnp.concatenate([dep0, jnp.full((8, 96), -1.0, F32)], axis=1)
    hot = (lax.broadcasted_iota(jnp.int32, (128, 128), 0).astype(F32) == dep0[0:1, :]).astype(F32)
    cosp = mm(turn[0], hot)
    sinp = mm(turn[1], hot)

    colf = cols[...].astype(F32)
    qx = jnp.floor((colf + 0.5) * (1.0 / NY))
    qy = colf - NY * qx
    live = cols[...] < NXY
    kx = jnp.where(live, jnp.where(qx < 90.0, qx, qx - NX) + RADIUS, -1.0)
    ky = jnp.where(live, jnp.where(qy < 90.0, qy, qy - NY) + RADIUS, -1.0)
    si = lax.broadcasted_iota(jnp.int32, (STK, STK), 0)
    so = lax.broadcasted_iota(jnp.int32, (STK, STK), 1)
    perm = (si == 2 * lax.rem(so, 16) + so // 16).astype(F32)
    kxy = mm(jnp.concatenate([kx, ky, jnp.zeros((6, STK), F32)], axis=0), perm)

    acc_re = jnp.zeros((16, 128), F32)
    acc_im = jnp.zeros((16, 128), F32)
    for r in range(16):
        lanes = slice(128 * r, 128 * (r + 1))
        p_re, p_im = proj[0, :, lanes], proj[1, :, lanes]
        a, b = m_re[r : r + 1, :], m_im[r : r + 1, :]
        acc_re += a * p_re + b * p_im
        acc_im += b * p_re - a * p_im
    ones = jnp.ones((8, 128), F32)
    part = mm(ones, jnp.concatenate([acc_re, acc_im], axis=0), NT, HIGHEST)

    field = cosp * d1 + sinp * d2
    place = lax.rem(lax.broadcasted_iota(jnp.int32, (256, STK), 0), 8)
    field = jnp.where(
        place == 6,
        jnp.broadcast_to(kxy[0:1, :], (256, STK)),
        jnp.where(place == 7, jnp.broadcast_to(kxy[1:2, :], (256, STK)), field[:, :STK]),
    )
    message = jnp.concatenate(
        [field, jnp.broadcast_to(part[0:1, :], (256, STK)), jnp.zeros((256, 64), F32)], axis=1
    )
    mine[0] = message.reshape(NF, 8, 128)
    for b in range(1, 4):
        mine[b] = pltpu.roll(message, 32 * b, 1).reshape(NF, 8, 128)
    got[0] = mine[0, me]

    pl.semaphore_wait(barrier, NF - 1 + 7 + 1)

    def send_field(k, _):
        to = lax.rem(me + k, NF)
        pltpu.make_async_remote_copy(
            mine.at[lax.rem(k, 4), to], got.at[k], sa, ra, device_id={"fft": to}, device_id_type=MESH
        ).start()
        return 0

    lax.fori_loop(1, NF, send_field, 0)

    def send_slab(k, _):
        to = lax.rem(band + 2 * k, 16)
        pltpu.make_async_remote_copy(
            pool.at[core, row], pool.at[core, row], ss, rs, device_id={"band": to}, device_id_type=MESH
        ).start()
        return 0

    lax.fori_loop(1, 8, send_slab, 0)

    sr_i = lax.broadcasted_iota(jnp.int32, (16, STK), 1) // 2
    rr_i = lax.broadcasted_iota(jnp.int32, (16, STK), 0)
    s_i = lax.broadcasted_iota(jnp.int32, (STK, 128), 0)
    l_i = lax.broadcasted_iota(jnp.int32, (STK, 128), 1)
    half = (lax.rem(s_i, 2) == l_i // GZ).astype(F32)
    kx16 = mm(jnp.where(sr_i == rr_i, jnp.broadcast_to(kx, (16, STK)), 0.0), half) - RADIUS
    ky16 = mm(jnp.where(sr_i == rr_i, jnp.broadcast_to(ky, (16, STK)), 0.0), half) - RADIUS
    fz = jnp.where(dep16 < NZ // 2, dep16, dep16 - NZ).astype(F32)
    kin = (0.5 / (RADIUS * RADIUS)) * (kx16 * kx16 + ky16 * ky16 + fz * fz)

    dfull = jnp.zeros((16, 16), F32)
    p_i = lax.broadcasted_iota(jnp.int32, (16, 8), 0)
    for a in range(2):
        owner = (p_i == jnp.broadcast_to(atoms[a : a + 1, :], (16, 8))).astype(F32)
        dfull += mm(mm(owner, coup[a], NN, HIGHEST), owner, NT, HIGHEST)

    whole = pltpu.make_async_remote_copy(
        got.at[pl.ds(1, NF - 1)], got.at[pl.ds(1, NF - 1)], sa, ra, device_id={"fft": lax.rem(me + 1, NF)}, device_id_type=MESH
    )
    whole.wait_recv()
    lane = lax.broadcasted_iota(jnp.int32, (8, 128), 1) // 32
    sticks = []
    others = []
    for a in range(8):
        tile = jnp.zeros((8, 128), F32)
        for b in range(4):
            tile = jnp.where(lane == b, got[4 * a + b], tile)
        sticks.append(tile)
    total = jnp.zeros((8, 128), F32)
    for b in range(4):
        piece = jnp.zeros((8, 128), F32)
        for a in range(8):
            piece += got[4 * a + b]
        piece = jnp.where(lane == (b + 1) % 4, piece, 0.0)
        shift = (128 - 32 * (b + 1)) % 128
        total += pltpu.roll(piece, shift, 1) if shift else piece
    pr, pi = total[0:1, 0:16], total[0:1, 16:32]
    c_re = jnp.sum(dfull * pr, axis=1, keepdims=True)
    c_im = jnp.sum(dfull * pi, axis=1, keepdims=True)
    for r in range(16):
        lanes = slice(128 * r, 128 * (r + 1))
        p_re, p_im = proj[0, :, lanes], proj[1, :, lanes]
        nonl[0, r : r + 1, :] = jnp.sum(c_re * p_re - c_im * p_im, axis=0, keepdims=True)
        nonl[1, r : r + 1, :] = jnp.sum(c_re * p_im + c_im * p_re, axis=0, keepdims=True)

    ix = lax.broadcasted_iota(jnp.int32, (KX, 128), 0).astype(F32)
    iy = lax.broadcasted_iota(jnp.int32, (KY, 128), 0).astype(F32)
    grid = jnp.zeros((6 * KX, KY), F32)
    hot_y = []
    for a in range(8):
        tile = sticks[a]
        hot_y.append((iy == tile[7:8, :]).astype(F32).astype(BF16))
        on = ix == tile[6:7, :]
        hi = tile.astype(BF16).astype(F32)
        lo = tile - hi
        z_hi = jnp.concatenate([jnp.where(on, hi[p : p + 1, :], 0.0) for p in range(6)], axis=0)
        z_lo = jnp.concatenate([jnp.where(on, lo[p : p + 1, :], 0.0) for p in range(6)], axis=0)
        grid += mm(z_hi.astype(BF16), hot_y[a], NT, None) + mm(z_lo.astype(BF16), hot_y[a], NT, None)

    left = jnp.concatenate(
        [jnp.concatenate([grid[2 * z * KX : (2 * z + 1) * KX], grid[(2 * z + 1) * KX : (2 * z + 2) * KX]], axis=1) for z in range(PLANES)],
        axis=0,
    )
    inv_y = mm(left, wiy[...])
    fields = []
    for z in range(PLANES):
        rows = inv_y[z * KX : (z + 1) * KX]
        right = jnp.concatenate([rows[:, :V], rows[:, V:]], axis=0)
        grid_z = mm(wix[...], right)
        fields.append(jnp.concatenate([grid_z[:U] * pot[z], grid_z[U:] * pot[z]], axis=1))
    fwd_y = mm(jnp.concatenate(fields, axis=0), wfy[...])
    right = jnp.concatenate(
        [
            jnp.concatenate([fwd_y[z * U : (z + 1) * U, :KY], fwd_y[z * U : (z + 1) * U, KY:]], axis=0)
            for z in range(PLANES)
        ],
        axis=1,
    )
    back = mm(wfx[...], right)
    stack = jnp.concatenate(
        [back[c * KX : (c + 1) * KX, z * KY : (z + 1) * KY] for z in range(PLANES) for c in range(2)], axis=0
    )
    hi = stack.astype(BF16)
    lo = (stack - hi.astype(F32)).astype(BF16)
    both = jnp.concatenate([hi, lo], axis=1)
    for a in range(8):
        spread = mm(both, jnp.concatenate([hot_y[a], hot_y[a]], axis=0), NN, None)
        on = ix == sticks[a][6:7, :]
        rows = [
            jnp.sum(jnp.where(on, spread[p * KX : (p + 1) * KX], 0.0), axis=0, keepdims=True) for p in range(6)
        ]
        tile = jnp.concatenate(rows + [jnp.zeros((2, 128), F32)], axis=0)
        tiles[0, a] = tile
        for b in range(1, 4):
            tiles[b, a] = pltpu.roll(tile, 128 - 32 * b, 1)
    ret[me] = tiles[0, 0]

    def send_back(k, _):
        to = lax.rem(me + NF - k, NF)
        pltpu.make_async_remote_copy(
            tiles.at[lax.rem(k, 4), k // 4], ret.at[me], sb, rb, device_id={"fft": to}, device_id_type=MESH
        ).start()
        return 0

    lax.fori_loop(1, NF, send_back, 0)

    seven = pltpu.make_async_remote_copy(
        pool.at[0, pl.ds(0, 7)], pool.at[0, pl.ds(0, 7)], ss, rs, device_id={"band": twin}, device_id_type=MESH
    )
    seven.wait_recv()
    swap = pltpu.make_async_remote_copy(
        pool.at[core], pool.at[core], sf, rf, device_id={"band": twin}, device_id_type=MESH
    )
    swap.start()

    sign = jnp.where(lax.broadcasted_iota(jnp.int32, (8, 128), 0) < 4, 1.0, -1.0)

    def correlate(v_re, v_im, source):
        def step(k, _):
            u = jnp.zeros((8, 128), F32)
            w = jnp.zeros((8, 128), F32)
            for r in range(16):
                block = pool[lax.rem(k, 2), k // 2, :, 128 * r : 128 * (r + 1)]
                u += block * v_re[r : r + 1, :]
                w += block * v_im[r : r + 1, :]
            w = jnp.concatenate([w[4:8], w[0:4]], axis=0)
            source[k] = w + u * sign
            return 0

        lax.fori_loop(0, 16, step, 0)
        sums = mm(ones, source[...].reshape(128, 128), NT, HIGHEST)
        return sums[0:1, :]

    swap.wait_recv()
    s_row = correlate(m_re, m_im, work)

    every = pltpu.make_async_remote_copy(
        got.at[pl.ds(1, NF - 1)], ret.at[pl.ds(0, NF - 1)], sb, rb, device_id={"fft": lax.rem(me + 1, NF)}, device_id_type=MESH
    )
    every.wait_recv()
    came = ret[...].reshape(256, 128)
    ab = jnp.concatenate([came * cosp, came * sinp], axis=0)
    loc = mm(tback[...], ab).T
    loc_re = jnp.concatenate([loc[0:16, :GZ], loc[16:32, :GZ]], axis=1)
    loc_im = jnp.concatenate([loc[0:16, GZ:], loc[16:32, GZ:]], axis=1)
    a_re = jnp.where(mask, kin * m_re + loc_re + nonl[0], 0.0)
    a_im = jnp.where(mask, kin * m_im + loc_im + nonl[1], 0.0)
    out[0] = a_re
    out[1] = a_im
    h_row = correlate(a_re, a_im, work)
    red[me] = jnp.concatenate([h_row, s_row], axis=0)

    def send_sum(k, _):
        pltpu.make_async_remote_copy(
            red.at[me], red.at[me], sr, rr, device_id={"fft": lax.rem(me + k, NF)}, device_id_type=MESH
        ).start()
        return 0

    lax.fori_loop(1, NF, send_sum, 0)
    last = pltpu.make_async_remote_copy(
        red.at[pl.ds(0, NF - 1)], red.at[pl.ds(0, NF - 1)], sr, rr, device_id={"fft": lax.rem(me + 1, NF)}, device_id_type=MESH
    )
    last.wait_recv()
    both_rows = jnp.sum(red[...], axis=0)
    li = lax.broadcasted_iota(jnp.int32, (128, 128), 0)
    lo_ = lax.broadcasted_iota(jnp.int32, (128, 128), 1)
    want = (lax.rem(lo_, 64) // 4) * 8 + (lo_ // 64) * 4 + lax.rem(lo_, 4)
    order = (li == want).astype(F32)
    final = mm(jnp.concatenate([both_rows, jnp.zeros((6, 128), F32)], axis=0), order, NN, HIGHEST)
    out_h[0] = final[0:1, 0:64]
    out_h[1] = final[0:1, 64:128]
    out_s[0] = final[1:2, 0:64]
    out_s[1] = final[1:2, 64:128]

    whole.wait_send()
    seven.wait_send()
    swap.wait_send()
    every.wait_send()
    last.wait_send()


def shards(orbitals, stick_columns, stick_depths, potential, projectors, atom_projectors, couplings, slab_orbitals):
    pot = jnp.pad(potential.reshape(PLANES, NX, NY), ((0, 0), (0, U - NX), (0, V - NY)))
    args = (
        orbitals.reshape(2, 16, 128),
        stick_columns.reshape(1, STK),
        stick_depths,
        pot,
        projectors,
        atom_projectors,
        couplings,
        slab_orbitals,
    ) + tuple(jnp.asarray(t) for t in tables())
    vmem = pl.BlockSpec(memory_space=pltpu.VMEM)
    dma = pltpu.SemaphoreType.DMA
    applied, proj_h, proj_s = pl.pallas_call(
        kernel,
        out_shape=(
            jax.ShapeDtypeStruct((2, 16, 128), F32),
            jax.ShapeDtypeStruct((2, 1, 64), F32),
            jax.ShapeDtypeStruct((2, 1, 64), F32),
        ),
        in_specs=[vmem] * len(args),
        out_specs=(vmem, vmem, vmem),
        scratch_shapes=[
            pltpu.VMEM((4, NF, 8, 128), F32),
            pltpu.VMEM((NF, 8, 128), F32),
            pltpu.VMEM((4, 8, 8, 128), F32),
            pltpu.VMEM((NF, 8, 128), F32),
            pltpu.VMEM((2, 8, 8, 2048), F32),
            pltpu.VMEM((NF, 2, 128), F32),
            pltpu.VMEM((16, 8, 128), F32),
            pltpu.VMEM((2, 16, 128), F32),
            pltpu.VMEM((8, 128), F32),
        ]
        + [dma] * 10,
        compiler_params=pltpu.CompilerParams(
            collective_id=0, has_side_effects=True, vmem_limit_bytes=48 * 1024 * 1024
        ),
        name="davidson",
    )(*args)
    return applied.reshape(2, 1, 2048), proj_h, proj_s


def solution(mesh):
    in_specs = (
        P(None, "band", "fft"),
        P("fft"),
        P("fft", None),
        P("fft", None),
        P(None, None, "fft"),
        P(),
        P(),
        P(None, "band", "fft"),
    )
    out_specs = (P(None, "band", "fft"), P(None, "band", None), P(None, "band", None))
    return jax.shard_map(shards, mesh=mesh, in_specs=in_specs, out_specs=out_specs, check_vma=False)
```

```python
import functools
import math

import jax
import jax.numpy as jnp
import ml_dtypes
import numpy as np
from jax import lax
from jax.experimental import pallas as pl
from jax.experimental.pallas import tpu as pltpu
from jax.sharding import PartitionSpec as P

NX = 180
NY = 180
NZ = 96
GZ = 64
RADIUS = 45
NXY = NX * NY
NF = 32
STK = 32
KX = 96
KY = 128
U = 192
V = 256
PLANES = 3

MESH = pl.DeviceIdType.MESH
HIGHEST = lax.Precision.HIGHEST
F32 = jnp.float32
BF16 = jnp.bfloat16
NN = (((1,), (0,)), ((), ()))
NT = (((1,), (1,)), ((), ()))


def mm(a, b, dims=NN, precision=None):
    return lax.dot_general(a, b, dims, precision=precision, preferred_element_type=F32)


def split(x):
    hi = x.astype(BF16)
    return hi, (x - hi.astype(F32)).astype(BF16)


def mm_right(a, table, dims=NN):
    hi, lo = split(a)
    return mm(hi, table[0], dims) + (mm(lo, table[0], dims) + mm(hi, table[1], dims))


def mm_left(table, b, dims=NN):
    hi, lo = split(b)
    return mm(table[0], hi, dims) + (mm(table[0], lo, dims) + mm(table[1], hi, dims))


def far_first():
    hops = lambda o: min(o[0], 8 - o[0]) + min(o[1], 4 - o[1])
    every = [(dz, dx) for dz in range(8) for dx in range(4)]
    return sorted((o for o in every if o != (0, 0)), key=lambda o: (-hops(o), o))


OFFSETS = far_first()


@functools.lru_cache(maxsize=None)
def tables():
    tau = 2.0 * math.pi
    j = np.arange(GZ)
    depth = np.arange(NZ + 1)
    t1 = np.zeros((4, NF, 2, 2, GZ))
    t2 = np.zeros((4, NF, 2, 2, GZ))
    tb = np.zeros((2, GZ, 2, 4, NF, 2))
    turn = np.zeros((2, 4, NF, 2, 128))
    for d in range(NF):
        for p in range(2 * PLANES):
            h, q = p // 4, p % 4
            z = PLANES * d + p // 2
            th = tau * (j * z % NZ) / NZ
            c, s = np.cos(th), np.sin(th)
            if p % 2 == 0:
                t1[q, d, h] = c, -s
                t2[q, d, h] = -s, -c
                tb[0, :, 0, q, d, h], tb[0, :, 1, q, d, h] = c, -s
                tb[1, :, 0, q, d, h], tb[1, :, 1, q, d, h] = -s, -c
            else:
                t1[q, d, h] = s, c
                t2[q, d, h] = c, -s
                tb[0, :, 0, q, d, h], tb[0, :, 1, q, d, h] = s, c
                tb[1, :, 0, q, d, h], tb[1, :, 1, q, d, h] = c, -s
            ph = tau * (depth * z % NZ) / NZ
            turn[0, q, d, h, : NZ + 1] = np.cos(ph)
            turn[1, q, d, h, : NZ + 1] = np.sin(ph)
    n = 2 * RADIUS + 1
    k = np.arange(n) - RADIUS
    g = np.arange(NX)
    ang = tau * ((k[:, None] * g[None, :]) % NX) / NX
    c, s = np.cos(ang), np.sin(ang)
    wiy = np.zeros((2, KY, 2, V))
    wiy[0, :n, 0, :NY], wiy[0, :n, 1, :NY] = c / NY, s / NY
    wiy[1, :n, 0, :NY], wiy[1, :n, 1, :NY] = -s / NY, c / NY
    wix = np.zeros((2, U, 2, KX))
    wix[0, :NX, 0, :n], wix[0, :NX, 1, :n] = c.T / NX, -s.T / NX
    wix[1, :NX, 0, :n], wix[1, :NX, 1, :n] = s.T / NX, c.T / NX
    wfy = np.zeros((2, V, 2, KY))
    wfy[0, :NY, 0, :n], wfy[0, :NY, 1, :n] = c.T, -s.T
    wfy[1, :NY, 0, :n], wfy[1, :NY, 1, :n] = s.T, c.T
    wfx = np.zeros((2, KX, 2, U))
    wfx[0, :n, 0, :NX], wfx[0, :n, 1, :NX] = c, s
    wfx[1, :n, 0, :NX], wfx[1, :n, 1, :NX] = -s, c
    back = np.transpose(tb.reshape(2, GZ, 2, 256), (2, 1, 0, 3)).reshape(2 * GZ, 512)
    tz = np.concatenate([t1.reshape(256, 128), t2.reshape(256, 128)], axis=0) / NZ

    def parts(x):
        x = np.asarray(x, np.float32)
        hi = x.astype(ml_dtypes.bfloat16)
        lo = (x - hi.astype(np.float32)).astype(ml_dtypes.bfloat16)
        return np.stack([hi, lo])

    return (
        parts(tz),
        parts(turn.reshape(512, 128)),
        parts(wiy.reshape(2 * KY, 2 * V)),
        parts(wix.reshape(2 * U, 2 * KX)),
        parts(wfy.reshape(2 * V, 2 * KY)),
        parts(wfx.reshape(2 * KX, 2 * U)),
        parts(back),
    )


def kernel(
    orb_h, cols_h, deps_h, pot_h, proj_h, atoms_h, coup_h, slab_h, tz_h, turn_h, wiy_h, wix_h, wfy_h, wfx_h, tback_h,
    out, out_sums,
    orb, cols, deps, pot, proj, atoms, coup, slab, tz, turn, wiy, wix, wfy, wfx, tback,
    mine, got, tiles, ret, pool, red, nonl, vecs, field_pot,
    loads, sa, ra, sb, rb, near_s, near_r, far_s, far_r, sf, rf, sr, rr,
):
    me = lax.axis_index("fft")
    band = lax.axis_index("band")
    my_z, my_x = me // 4, lax.rem(me, 4)
    core = lax.rem(band, 2)
    row = band // 2
    twin = band + 1 - 2 * core

    def fft_at(dz, dx):
        return lax.rem(my_z + dz, 8) * 4 + lax.rem(my_x + dx, 4)

    def band_at(dy):
        return lax.rem(band + 2 * dy, 16)

    barrier = pltpu.get_barrier_semaphore()
    for dz, dx in OFFSETS:
        pl.semaphore_signal(barrier, inc=1, device_id={"fft": fft_at(dz, dx)}, device_id_type=MESH)
    for dy in (2, 6, 1, 7):
        pl.semaphore_signal(barrier, inc=1, device_id={"band": band_at(dy)}, device_id_type=MESH)
    pl.semaphore_signal(barrier, inc=1, device_id={"band": twin}, device_id_type=MESH)

    pairs = (
        (orb_h, orb), (deps_h, deps), (cols_h, cols), (tz_h, tz), (turn_h, turn), (proj_h, proj), (slab_h, slab),
        (pot_h, pot), (atoms_h, atoms), (coup_h, coup), (wiy_h, wiy), (wix_h, wix), (wfy_h, wfy), (wfx_h, wfx),
        (tback_h, tback),
    )
    copies = [pltpu.make_async_copy(a, b, loads.at[i]) for i, (a, b) in enumerate(pairs)]
    for c in copies:
        c.start()
    for c in copies[:5]:
        c.wait()

    dep_even = deps[pl.ds(0, 16, stride=2), :]
    dep_odd = deps[pl.ds(1, 16, stride=2), :]
    dep16 = jnp.concatenate([dep_even, dep_odd], axis=1)
    mask = dep16 < NZ
    m_re = jnp.where(mask, orb[0], 0.0)
    m_im = jnp.where(mask, orb[1], 0.0)
    x2 = jnp.concatenate(
        [
            jnp.concatenate([m_re[:, :GZ], m_im[:, :GZ]], axis=1),
            jnp.concatenate([m_re[:, GZ:], m_im[:, GZ:]], axis=1),
        ],
        axis=0,
    )
    x2 = jnp.concatenate([x2] * 4, axis=0)
    d12 = mm_left(tz, x2, NT)

    dep32 = jnp.concatenate([dep_even, dep_odd] * 4, axis=0).astype(F32)
    first = (lax.broadcasted_iota(jnp.int32, (8, GZ), 1) == 0).astype(F32)
    dep0 = mm(first, dep32, NT)
    hot = (lax.broadcasted_iota(jnp.int32, (128, 128), 0).astype(F32) == dep0[0:1, :]).astype(F32).astype(BF16)
    phase = mm(turn[0], hot) + mm(turn[1], hot)
    cosp, sinp = phase[:256], phase[256:]

    colf = cols[...].astype(F32)
    qx = jnp.floor((colf + 0.5) * (1.0 / NY))
    qy = colf - NY * qx
    live = cols[...] < NXY
    kx = jnp.where(live, jnp.where(qx < 90.0, qx, qx - NX) + (RADIUS + 1), 0.0)
    ky = jnp.where(live, jnp.where(qy < 90.0, qy, qy - NY) + (RADIUS + 1), 0.0)
    si = lax.broadcasted_iota(jnp.int32, (STK, 128), 0)
    so = lax.rem(lax.broadcasted_iota(jnp.int32, (STK, 128), 1), 32)
    perm = (si == 2 * lax.rem(so, 16) + so // 16).astype(F32)
    kxy = mm(jnp.concatenate([kx, ky, jnp.zeros((6, STK), F32)], axis=0), perm)
    code = kxy[0:1, :] * 128.0 + kxy[1:2, :]

    copies[5].wait()
    acc_re = jnp.zeros((16, 128), F32)
    acc_im = jnp.zeros((16, 128), F32)
    for r in range(16):
        lanes = slice(128 * r, 128 * (r + 1))
        p_re, p_im = proj[0, :, lanes], proj[1, :, lanes]
        a, b = m_re[r : r + 1, :], m_im[r : r + 1, :]
        acc_re += a * p_re + b * p_im
        acc_im += b * p_re - a * p_im
    ones = jnp.ones((8, 128), F32)
    part = mm(ones, jnp.concatenate([acc_re, acc_im] * 4, axis=0), NT, HIGHEST)

    field = cosp * d12[:256] + sinp * d12[256:]
    group = lax.broadcasted_iota(jnp.int32, (64, 128), 1) // 32
    odd = lax.rem(lax.broadcasted_iota(jnp.int32, (64, 128), 0), 2) == 1
    message = jnp.where(
        group == 0,
        field[0:64],
        jnp.where(
            group == 1,
            field[64:128],
            jnp.where(
                group == 2,
                jnp.where(odd, jnp.broadcast_to(code, (64, 128)), field[128:192]),
                jnp.where(odd, jnp.broadcast_to(part[0:1, :], (64, 128)), field[192:256]),
            ),
        ),
    )
    for d in range(NF):
        mine[d] = message[2 * d : 2 * d + 2]
    got[0] = mine[me]

    copies[6].wait()
    pool[core, row] = jnp.concatenate([slab[0], slab[1]], axis=0)

    pl.semaphore_wait(barrier, NF - 1 + 4 + 1)

    for dz, dx in OFFSETS:
        to = fft_at(dz, dx)
        pltpu.make_async_remote_copy(
            mine.at[to], got.at[4 * dz + dx], sa, ra, device_id={"fft": to}, device_id_type=MESH
        ).start()

    def to_band(src, dst, send, recv, dy):
        return pltpu.make_async_remote_copy(
            src, dst, send, recv, device_id={"band": band_at(dy)}, device_id_type=MESH
        )

    own = pool.at[core, row]
    near = [to_band(own, own, near_s.at[i], near_r.at[i], dy) for i, dy in enumerate((2, 6, 1, 7))]
    for c in near:
        c.start()

    sr_i = lax.broadcasted_iota(jnp.int32, (16, STK), 1) // 2
    rr_i = lax.broadcasted_iota(jnp.int32, (16, STK), 0)
    s_i = lax.broadcasted_iota(jnp.int32, (STK, 128), 0)
    l_i = lax.broadcasted_iota(jnp.int32, (STK, 128), 1)
    half = (lax.rem(s_i, 2) == l_i // GZ).astype(F32)
    kx16 = mm(jnp.where(sr_i == rr_i, jnp.broadcast_to(kx, (16, STK)), 0.0), half) - (RADIUS + 1)
    ky16 = mm(jnp.where(sr_i == rr_i, jnp.broadcast_to(ky, (16, STK)), 0.0), half) - (RADIUS + 1)
    fz = jnp.where(dep16 < NZ // 2, dep16, dep16 - NZ).astype(F32)
    kin = (0.5 / (RADIUS * RADIUS)) * (kx16 * kx16 + ky16 * ky16 + fz * fz)

    for c in copies[7:]:
        c.wait()

    dfull = jnp.zeros((16, 16), F32)
    p_i = lax.broadcasted_iota(jnp.int32, (16, 8), 0)
    for a in range(2):
        owner = (p_i == jnp.broadcast_to(atoms[a : a + 1, :], (16, 8))).astype(F32)
        dfull += mm(mm(owner, coup[a], NN, HIGHEST), owner, NT, HIGHEST)

    field_pot[...] = jnp.zeros_like(field_pot)
    for x in range(NX):
        field_pot[0, 4 * x : 4 * x + PLANES, :] = pot[:, NY * x : NY * x + 128]
        field_pot[1, 4 * x : 4 * x + PLANES, 0 : NY - 128] = pot[:, NY * x + 128 : NY * x + NY]

    ahead = pool.at[core, lax.rem(row + 6, 8)]
    behind = pool.at[core, lax.rem(row + 2, 8)]
    first_half, second_half = pl.ds(0, 1024), pl.ds(1024, 1024)
    far = (
        to_band(ahead, ahead, far_s.at[0], far_r.at[0], 1),
        to_band(ahead.at[:, first_half], ahead.at[:, first_half], far_s.at[1], far_r.at[1], 2),
        to_band(behind, behind, far_s.at[2], far_r.at[2], 7),
        to_band(behind.at[:, second_half], behind.at[:, second_half], far_s.at[3], far_r.at[3], 6),
    )

    whole = pltpu.make_async_remote_copy(
        got.at[pl.ds(1, NF - 1)], got.at[pl.ds(1, NF - 1)], sa, ra, device_id={"fft": fft_at(0, 1)}, device_id_type=MESH
    )
    whole.wait_recv()
    near[0].wait_recv()
    far[0].start()
    far[1].start()
    near[1].wait_recv()
    far[2].start()
    far[3].start()

    lane = lax.broadcasted_iota(jnp.int32, (8, 128), 1) // 32
    parts = [[None] * 4 for _ in range(2)]
    for h in range(2):
        for b in range(4):
            rows = jnp.concatenate([got[4 * a + b, h : h + 1, :] for a in range(8)], axis=0)
            for q in range(4):
                shift = 32 * ((b - q) % 4)
                turned = pltpu.roll(rows, shift, 1) if shift else rows
                parts[h][q] = turned if b == 0 else jnp.where(lane == b, turned, parts[h][q])
    fields = [parts[p // 4][p % 4] for p in range(6)]
    code = parts[1][2]
    kx_at = jnp.floor(code * (1.0 / 128.0))
    ky_at = code - 128.0 * kx_at
    kx_at -= 1.0
    ky_at -= 1.0

    ix = lax.broadcasted_iota(jnp.int32, (KX, 128), 0).astype(F32)
    iy = lax.broadcasted_iota(jnp.int32, (KY, 128), 0).astype(F32)
    his = [f.astype(BF16).astype(F32) for f in fields]
    los = [f - h for f, h in zip(fields, his)]
    on = [ix == kx_at[a : a + 1, :] for a in range(8)]
    hot_y = [(iy == ky_at[a : a + 1, :]).astype(F32).astype(BF16) for a in range(8)]
    grid = jnp.zeros((6 * KX, KY), F32)
    for a in range(0, 8, 2):
        wide = jnp.concatenate([hot_y[a], hot_y[a + 1]], axis=1)
        for values in (his, los):
            placed = jnp.concatenate(
                [
                    jnp.concatenate(
                        [jnp.where(on[i], values[p][i : i + 1, :], 0.0).astype(BF16) for i in (a, a + 1)], axis=1
                    )
                    for p in range(6)
                ],
                axis=0,
            )
            grid += mm(placed, wide, NT)

    left = jnp.concatenate(
        [
            jnp.concatenate([grid[2 * z * KX : (2 * z + 1) * KX], grid[(2 * z + 1) * KX : (2 * z + 2) * KX]], axis=1)
            for z in range(PLANES)
        ],
        axis=0,
    )
    inv_y = mm_right(left, wiy)
    planes = []
    for z in range(PLANES):
        rows = inv_y[z * KX : (z + 1) * KX]
        right = jnp.concatenate([rows[:, :V], rows[:, V:]], axis=0)
        grid_z = mm_left(wix, right)
        value = jnp.concatenate(
            [
                jnp.concatenate([field_pot[i, pl.ds(32 * x + z, 8, stride=4), :] for i in range(2)], axis=1)
                for x in range(U // 8)
            ],
            axis=0,
        )
        planes.append(jnp.concatenate([grid_z[:U] * value, grid_z[U:] * value], axis=1))
    fwd_y = mm_right(jnp.concatenate(planes, axis=0), wfy)
    right = jnp.concatenate(
        [
            jnp.concatenate([fwd_y[z * U : (z + 1) * U, :KY], fwd_y[z * U : (z + 1) * U, KY:]], axis=0)
            for z in range(PLANES)
        ],
        axis=1,
    )
    back = mm_left(wfx, right)
    stack = jnp.concatenate(
        [back[c * KX : (c + 1) * KX, z * KY : (z + 1) * KY] for z in range(PLANES) for c in range(2)], axis=0
    )
    both = jnp.concatenate(split(stack), axis=1)
    picked = [[] for _ in range(6)]
    for a in range(0, 8, 2):
        wide = jnp.concatenate([hot_y[a], hot_y[a + 1]], axis=1)
        spread = mm(both, jnp.concatenate([wide, wide], axis=0))
        for i in range(2):
            for p in range(6):
                block = spread[p * KX : (p + 1) * KX, 128 * i : 128 * (i + 1)]
                picked[p].append(jnp.sum(jnp.where(on[a + i], block, 0.0), axis=0, keepdims=True))
    picked = [jnp.concatenate(rows, axis=0) for rows in picked] + [jnp.zeros((8, 128), F32)] * 2
    for h in range(2):
        for b in range(4):
            rows = None
            for q in range(4):
                shift = 32 * ((q - b) % 4)
                turned = pltpu.roll(picked[4 * h + q], shift, 1) if shift else picked[4 * h + q]
                rows = turned if q == 0 else jnp.where(lane == q, turned, rows)
            for a in range(8):
                tiles[4 * a + b, h : h + 1, :] = rows[a : a + 1, :]
    ret[me] = tiles[0]

    for dz, dx in OFFSETS:
        pltpu.make_async_remote_copy(
            tiles.at[4 * dz + dx], ret.at[me], sb, rb, device_id={"fft": fft_at(8 - dz, 4 - dx)}, device_id_type=MESH
        ).start()

    total = jnp.sum(parts[1][3], axis=0, keepdims=True)
    total = total + pltpu.roll(total, 64, 1)
    total = total + pltpu.roll(total, 32, 1)
    c_re = jnp.sum(dfull * total[:, 0:16], axis=1, keepdims=True)
    c_im = jnp.sum(dfull * total[:, 16:32], axis=1, keepdims=True)
    for r in range(16):
        lanes = slice(128 * r, 128 * (r + 1))
        p_re, p_im = proj[0, :, lanes], proj[1, :, lanes]
        nonl[0, r : r + 1, :] = jnp.sum(c_re * p_re - c_im * p_im, axis=0, keepdims=True)
        nonl[1, r : r + 1, :] = jnp.sum(c_re * p_im + c_im * p_re, axis=0, keepdims=True)

    near[2].wait_recv()
    near[3].wait_recv()
    for c in far:
        c.wait_recv()
    swap = pltpu.make_async_remote_copy(
        pool.at[core], pool.at[core], sf, rf, device_id={"band": twin}, device_id_type=MESH
    )
    swap.start()

    sign = jnp.where(lax.broadcasted_iota(jnp.int32, (8, 128), 0) < 4, 1.0, -1.0)

    def correlate(at):
        def step(r, carry):
            u, w = carry
            block = pool[:, :, :, pl.ds(pl.multiple_of(128 * r, 128), 128)]
            u = u + block * vecs[at, pl.ds(r, 1), :]
            w = w + block * vecs[at + 1, pl.ds(r, 1), :]
            return u, w

        zero = jnp.zeros((2, 8, 8, 128), F32)
        u, w = lax.fori_loop(0, 16, step, (zero, zero))
        pieces = []
        for k in range(16):
            x = w[k % 2, k // 2]
            pieces.append(jnp.concatenate([x[4:8], x[0:4]], axis=0) + u[k % 2, k // 2] * sign)
        return mm(ones, jnp.concatenate(pieces, axis=0), NT, HIGHEST)[0:1, :]

    vecs[0] = m_re
    vecs[1] = m_im
    base_re = kin * m_re + nonl[0]
    base_im = kin * m_im + nonl[1]
    swap.wait_recv()
    s_row = correlate(0)

    every = pltpu.make_async_remote_copy(
        tiles.at[pl.ds(1, NF - 1)], ret.at[pl.ds(0, NF - 1)], sb, rb, device_id={"fft": fft_at(0, 1)}, device_id_type=MESH
    )
    every.wait_recv()
    came = jnp.concatenate([ret[d] for d in range(NF)], axis=0)
    came = jnp.concatenate([came] + [pltpu.roll(came, 128 - 32 * q, 1) for q in range(1, 4)], axis=0)
    loc = mm_left(tback, jnp.concatenate([came * cosp, came * sinp], axis=0)).T
    loc_re = jnp.concatenate([loc[0:16, :GZ], loc[16:32, :GZ]], axis=1)
    loc_im = jnp.concatenate([loc[0:16, GZ:], loc[16:32, GZ:]], axis=1)
    a_re = jnp.where(mask, base_re + loc_re, 0.0)
    a_im = jnp.where(mask, base_im + loc_im, 0.0)
    vecs[2] = a_re
    vecs[3] = a_im
    out[0] = a_re
    out[1] = a_im
    h_row = correlate(2)
    red[me] = jnp.concatenate([h_row, s_row], axis=0)
    for dz, dx in OFFSETS:
        pltpu.make_async_remote_copy(
            red.at[me], red.at[me], sr, rr, device_id={"fft": fft_at(dz, dx)}, device_id_type=MESH
        ).start()

    whole.wait_send()
    every.wait_send()
    for c in near:
        c.wait_send()
    for c in far:
        c.wait_send()
    swap.wait_send()
    last = pltpu.make_async_remote_copy(
        red.at[pl.ds(0, NF - 1)], red.at[pl.ds(0, NF - 1)], sr, rr, device_id={"fft": fft_at(0, 1)}, device_id_type=MESH
    )
    last.wait_recv()
    out_sums[...] = jnp.concatenate([jnp.sum(red[...], axis=0), jnp.zeros((6, 128), F32)], axis=0)
    last.wait_send()


def finish(applied, sums, out, out_h, out_s):
    out[...] = applied[...]
    li = lax.broadcasted_iota(jnp.int32, (128, 128), 0)
    lo = lax.broadcasted_iota(jnp.int32, (128, 128), 1)
    want = (lax.rem(lo, 64) // 4) * 8 + (lo // 64) * 4 + lax.rem(lo, 4)
    final = mm(sums[...], (li == want).astype(F32), NN, HIGHEST)
    out_h[0] = final[0:1, 0:64]
    out_h[1] = final[0:1, 64:128]
    out_s[0] = final[1:2, 0:64]
    out_s[1] = final[1:2, 64:128]


def shards(orbitals, stick_columns, stick_depths, potential, projectors, atom_projectors, couplings, slab_orbitals):
    args = (
        orbitals.reshape(2, 16, 128),
        stick_columns.reshape(1, STK),
        stick_depths,
        potential,
        projectors,
        atom_projectors,
        couplings,
        slab_orbitals,
    ) + tuple(jnp.asarray(t) for t in tables())
    vmem = pl.BlockSpec(memory_space=pltpu.VMEM)
    hbm = pl.BlockSpec(memory_space=pltpu.HBM)
    dma = pltpu.SemaphoreType.DMA
    applied, sums = pl.pallas_call(
        kernel,
        out_shape=(jax.ShapeDtypeStruct((2, 16, 128), F32), jax.ShapeDtypeStruct((8, 128), F32)),
        in_specs=[hbm] * len(args),
        out_specs=(vmem, vmem),
        scratch_shapes=[pltpu.VMEM(a.shape, a.dtype) for a in args]
        + [
            pltpu.VMEM((NF, 2, 128), F32),
            pltpu.VMEM((NF, 2, 128), F32),
            pltpu.VMEM((NF, 2, 128), F32),
            pltpu.VMEM((NF, 2, 128), F32),
            pltpu.VMEM((2, 8, 8, 2048), F32),
            pltpu.VMEM((NF, 2, 128), F32),
            pltpu.VMEM((2, 16, 128), F32),
            pltpu.VMEM((4, 16, 128), F32),
            pltpu.VMEM((2, 4 * U, 128), F32),
            dma((len(args),)),
        ]
        + [dma] * 4
        + [dma((4,))] * 4
        + [dma] * 4,
        compiler_params=pltpu.CompilerParams(
            collective_id=0, has_side_effects=True, vmem_limit_bytes=64 * 1024 * 1024
        ),
        name="davidson",
    )(*args)
    applied, proj_h, proj_s = pl.pallas_call(
        finish,
        out_shape=(
            jax.ShapeDtypeStruct((2, 16, 128), F32),
            jax.ShapeDtypeStruct((2, 1, 64), F32),
            jax.ShapeDtypeStruct((2, 1, 64), F32),
        ),
        in_specs=[vmem, vmem],
        out_specs=(vmem, vmem, vmem),
        name="finish",
    )(applied, sums)
    return applied.reshape(2, 1, 2048), proj_h, proj_s


def solution(mesh):
    in_specs = (
        P(None, "band", "fft"),
        P("fft"),
        P("fft", None),
        P("fft", None),
        P(None, None, "fft"),
        P(),
        P(),
        P(None, "band", "fft"),
    )
    out_specs = (P(None, "band", "fft"), P(None, "band", None), P(None, "band", None))
    return jax.shard_map(shards, mesh=mesh, in_specs=in_specs, out_specs=out_specs, check_vma=False)
```

```python
import functools
import math

import jax
import jax.numpy as jnp
import ml_dtypes
import numpy as np
from jax import lax
from jax.experimental import pallas as pl
from jax.experimental.pallas import tpu as pltpu
from jax.sharding import PartitionSpec as P

NX = 180
NY = 180
NZ = 96
GZ = 64
RADIUS = 45
NXY = NX * NY
NF = 32
STK = 32
KA = 48
KB = 64
U = 96
V = 256
PLANES = 3

MESH = pl.DeviceIdType.MESH
HIGHEST = lax.Precision.HIGHEST
F32 = jnp.float32
BF16 = jnp.bfloat16
NN = (((1,), (0,)), ((), ()))
NT = (((1,), (1,)), ((), ()))


def mm(a, b, dims=NN, precision=None):
    return lax.dot_general(a, b, dims, precision=precision, preferred_element_type=F32)


def split(x):
    hi = x.astype(BF16)
    return hi, (x - hi.astype(F32)).astype(BF16)


def mm_right(a, table, dims=NN):
    hi, lo = split(a)
    return mm(hi, table[0], dims) + (mm(lo, table[0], dims) + mm(hi, table[1], dims))


def mm_left(table, b, dims=NN):
    hi, lo = split(b)
    return mm(table[0], hi, dims) + (mm(table[0], lo, dims) + mm(table[1], hi, dims))


def far_first():
    hops = lambda o: min(o[0], 8 - o[0]) + min(o[1], 4 - o[1])
    every = [(dz, dx) for dz in range(8) for dx in range(4)]
    return sorted((o for o in every if o != (0, 0)), key=lambda o: (-hops(o), o))


OFFSETS = far_first()


@functools.lru_cache(maxsize=None)
def tables():
    tau = 2.0 * math.pi
    j = np.arange(GZ)
    depth = np.arange(NZ + 1)
    t1 = np.zeros((4, NF, 2, 2, GZ))
    t2 = np.zeros((4, NF, 2, 2, GZ))
    tb = np.zeros((2, GZ, 2, 4, NF, 2))
    turn = np.zeros((2, 4, NF, 2, 128))
    for d in range(NF):
        for p in range(2 * PLANES):
            h, q = p // 4, p % 4
            z = PLANES * d + p // 2
            th = tau * (j * z % NZ) / NZ
            c, s = np.cos(th), np.sin(th)
            if p % 2 == 0:
                t1[q, d, h] = c, -s
                t2[q, d, h] = -s, -c
                tb[0, :, 0, q, d, h], tb[0, :, 1, q, d, h] = c, -s
                tb[1, :, 0, q, d, h], tb[1, :, 1, q, d, h] = -s, -c
            else:
                t1[q, d, h] = s, c
                t2[q, d, h] = c, -s
                tb[0, :, 0, q, d, h], tb[0, :, 1, q, d, h] = s, c
                tb[1, :, 0, q, d, h], tb[1, :, 1, q, d, h] = c, -s
            ph = tau * (depth * z % NZ) / NZ
            turn[0, q, d, h, : NZ + 1] = np.cos(ph)
            turn[1, q, d, h, : NZ + 1] = np.sin(ph)
    n = RADIUS + 1
    k = np.arange(n)
    ang = tau * ((k[:, None] * np.arange(NY)[None, :]) % NY) / NY
    wiy = np.zeros((2, KB, V))
    wiy[0, :n, :NY], wiy[1, :n, :NY] = np.cos(ang) / NY, np.sin(ang) / NY
    wfy = np.zeros((V, 2, KB))
    wfy[:NY, 0, :n], wfy[:NY, 1, :n] = np.cos(ang).T, np.sin(ang).T
    g = np.arange(NX // 2 + 1)
    ang = tau * ((k[:, None] * g[None, :]) % NX) / NX
    c, s = np.cos(ang), np.sin(ang)
    wix = np.zeros((2, U, KA))
    wix[0, : len(g), :n], wix[1, : len(g), :n] = c.T / NX, s.T / NX
    wfx = np.zeros((2, KA, 2, U))
    wfx[0, :n, 0, : len(g)], wfx[0, :n, 1, : len(g)] = c, c
    wfx[1, :n, 0, : len(g)], wfx[1, :n, 1, : len(g)] = s, -s
    back = np.transpose(tb.reshape(2, GZ, 2, 256), (2, 1, 0, 3)).reshape(2 * GZ, 512)
    tz = np.concatenate([t1.reshape(256, 128), t2.reshape(256, 128)], axis=0) / NZ

    def parts(x):
        x = np.asarray(x, np.float32)
        hi = x.astype(ml_dtypes.bfloat16)
        lo = (x - hi.astype(np.float32)).astype(ml_dtypes.bfloat16)
        return np.stack([hi, lo])

    yh, yl = parts(wiy.reshape(2 * KB, V))
    xh, xl = parts(wix)
    fh, fl = parts(wfy.reshape(V, 2 * KB))
    gh, gl = parts(wfx.reshape(2 * KA, 2 * U))
    return (
        parts(tz),
        parts(turn.reshape(512, 128)),
        np.concatenate([yh, yh, yl], axis=0),
        np.concatenate([xh, xh, xl], axis=2),
        np.concatenate([fh, fl], axis=1),
        np.concatenate([gh, gl], axis=0),
        parts(back),
    )


def kernel(
    orb_h, cols_h, deps_h, pot_h, proj_h, atoms_h, coup_h, slab_h, tz_h, turn_h, wiy_h, wix_h, wfy_h, wfx_h, tback_h,
    out, out_sums,
    orb, cols, deps, pot, proj, atoms, coup, slab, tz, turn, wiy, wix, wfy, wfx, tback,
    mine, got, tiles, ret, pool, red, nonl, vecs, field_pot,
    loads, keep, sa, ra, sb, rb, near_s, near_r, far_s, far_r, sf, rf, sr, rr,
):
    me = lax.axis_index("fft")
    band = lax.axis_index("band")
    my_z, my_x = me // 4, lax.rem(me, 4)
    core = lax.rem(band, 2)
    row = band // 2
    twin = band + 1 - 2 * core

    def fft_at(dz, dx):
        return lax.rem(my_z + dz, 8) * 4 + lax.rem(my_x + dx, 4)

    def band_at(dy):
        return lax.rem(band + 2 * dy, 16)

    barrier = pltpu.get_barrier_semaphore()
    for dz, dx in OFFSETS:
        pl.semaphore_signal(barrier, inc=1, device_id={"fft": fft_at(dz, dx)}, device_id_type=MESH)
    for dy in (2, 6, 1, 7):
        pl.semaphore_signal(barrier, inc=1, device_id={"band": band_at(dy)}, device_id_type=MESH)
    pl.semaphore_signal(barrier, inc=1, device_id={"band": twin}, device_id_type=MESH)

    pairs = (
        (orb_h, orb), (deps_h, deps), (cols_h, cols), (tz_h, tz), (turn_h, turn), (proj_h, proj), (slab_h, slab),
        (pot_h, pot), (atoms_h, atoms), (coup_h, coup), (wiy_h, wiy), (wix_h, wix), (wfy_h, wfy), (wfx_h, wfx),
        (tback_h, tback),
    )
    copies = [pltpu.make_async_copy(a, b, loads.at[i]) for i, (a, b) in enumerate(pairs)]
    for c in copies:
        c.start()
    for c in copies[:5]:
        c.wait()

    dep_even = deps[pl.ds(0, 16, stride=2), :]
    dep_odd = deps[pl.ds(1, 16, stride=2), :]
    dep16 = jnp.concatenate([dep_even, dep_odd], axis=1)
    mask = dep16 < NZ
    m_re = jnp.where(mask, orb[0], 0.0)
    m_im = jnp.where(mask, orb[1], 0.0)
    x2 = jnp.concatenate(
        [
            jnp.concatenate([m_re[:, :GZ], m_im[:, :GZ]], axis=1),
            jnp.concatenate([m_re[:, GZ:], m_im[:, GZ:]], axis=1),
        ],
        axis=0,
    )
    x2 = jnp.concatenate([x2] * 4, axis=0)
    d12 = mm_left(tz, x2, NT)

    dep32 = jnp.concatenate([dep_even, dep_odd] * 4, axis=0).astype(F32)
    first = (lax.broadcasted_iota(jnp.int32, (8, GZ), 1) == 0).astype(F32)
    dep0 = mm(first, dep32, NT)
    hot = (lax.broadcasted_iota(jnp.int32, (128, 128), 0).astype(F32) == dep0[0:1, :]).astype(F32).astype(BF16)
    phase = mm(turn[0], hot) + mm(turn[1], hot)
    cosp, sinp = phase[:256], phase[256:]

    colf = cols[...].astype(F32)
    qx = jnp.floor((colf + 0.5) * (1.0 / NY))
    qy = colf - NY * qx
    live = cols[...] < NXY
    far_x, far_y = qx >= 90.0, qy >= 90.0
    kx = jnp.where(live, jnp.where(far_x, NX - qx, qx), 63.0)
    ky = jnp.where(live, jnp.where(far_y, NY - qy, qy), 0.0)
    col = ky + jnp.where(far_x, 2.0 * KB, 0.0) + jnp.where(far_y, 1.0 * KB, 0.0)
    si = lax.broadcasted_iota(jnp.int32, (STK, 128), 0)
    so = lax.rem(lax.broadcasted_iota(jnp.int32, (STK, 128), 1), 32)
    perm = (si == 2 * lax.rem(so, 16) + so // 16).astype(F32)
    kxy = mm(jnp.concatenate([kx, col, jnp.zeros((6, STK), F32)], axis=0), perm)
    code = kxy[0:1, :] * 256.0 + kxy[1:2, :]

    copies[5].wait()
    acc_re = jnp.zeros((16, 128), F32)
    acc_im = jnp.zeros((16, 128), F32)
    for r in range(16):
        lanes = slice(128 * r, 128 * (r + 1))
        p_re, p_im = proj[0, :, lanes], proj[1, :, lanes]
        a, b = m_re[r : r + 1, :], m_im[r : r + 1, :]
        acc_re += a * p_re + b * p_im
        acc_im += b * p_re - a * p_im
    ones = jnp.ones((8, 128), F32)
    part = mm(ones, jnp.concatenate([acc_re, acc_im] * 4, axis=0), NT, HIGHEST)

    field = cosp * d12[:256] + sinp * d12[256:]
    group = lax.broadcasted_iota(jnp.int32, (64, 128), 1) // 32
    odd = lax.rem(lax.broadcasted_iota(jnp.int32, (64, 128), 0), 2) == 1
    message = jnp.where(
        group == 0,
        field[0:64],
        jnp.where(
            group == 1,
            field[64:128],
            jnp.where(
                group == 2,
                jnp.where(odd, jnp.broadcast_to(code, (64, 128)), field[128:192]),
                jnp.where(odd, jnp.broadcast_to(part[0:1, :], (64, 128)), field[192:256]),
            ),
        ),
    )
    for d in range(NF):
        mine[d] = message[2 * d : 2 * d + 2]
    got[0] = mine[me]

    copies[6].wait()
    pool[core, row] = jnp.concatenate([slab[0], slab[1]], axis=0)

    pl.semaphore_wait(barrier, NF - 1 + 4 + 1)

    for dz, dx in OFFSETS:
        to = fft_at(dz, dx)
        pltpu.make_async_remote_copy(
            mine.at[to], got.at[4 * dz + dx], sa, ra, device_id={"fft": to}, device_id_type=MESH
        ).start()

    def to_band(src, dst, send, recv, dy):
        return pltpu.make_async_remote_copy(
            src, dst, send, recv, device_id={"band": band_at(dy)}, device_id_type=MESH
        )

    own = pool.at[core, row]
    first_half, second_half = pl.ds(0, 1024), pl.ds(1024, 1024)
    near = [
        to_band(src, src, near_s.at[i], near_r.at[i], dy)
        for i, (src, dy) in enumerate(
            (
                (own.at[:, first_half], 2),
                (own.at[:, second_half], 6),
                (own.at[:, second_half], 2),
                (own.at[:, first_half], 6),
                (own, 1),
                (own, 7),
            )
        )
    ]
    for c in near:
        c.start()

    sr_i = lax.broadcasted_iota(jnp.int32, (16, STK), 1) // 2
    rr_i = lax.broadcasted_iota(jnp.int32, (16, STK), 0)
    s_i = lax.broadcasted_iota(jnp.int32, (STK, 128), 0)
    l_i = lax.broadcasted_iota(jnp.int32, (STK, 128), 1)
    half = (lax.rem(s_i, 2) == l_i // GZ).astype(F32)
    kx16 = mm(jnp.where(sr_i == rr_i, jnp.broadcast_to(kx, (16, STK)), 0.0), half)
    ky16 = mm(jnp.where(sr_i == rr_i, jnp.broadcast_to(ky, (16, STK)), 0.0), half)
    fz = jnp.where(dep16 < NZ // 2, dep16, dep16 - NZ).astype(F32)
    kin = (0.5 / (RADIUS * RADIUS)) * (kx16 * kx16 + ky16 * ky16 + fz * fz)

    for c in copies[7:]:
        c.wait()

    dfull = jnp.zeros((16, 16), F32)
    p_i = lax.broadcasted_iota(jnp.int32, (16, 8), 0)
    for a in range(2):
        owner = (p_i == jnp.broadcast_to(atoms[a : a + 1, :], (16, 8))).astype(F32)
        dfull += mm(mm(owner, coup[a], NN, HIGHEST), owner, NT, HIGHEST)

    field_pot[...] = jnp.zeros_like(field_pot)
    for x in range(NX):
        r = 4 * (x if x <= NX // 2 else U + NX - x)
        field_pot[0, r : r + PLANES, :] = pot[:, NY * x : NY * x + 128]
        field_pot[1, r : r + PLANES, 0 : NY - 128] = pot[:, NY * x + 128 : NY * x + NY]

    ahead = pool.at[core, lax.rem(row + 6, 8)]
    behind = pool.at[core, lax.rem(row + 2, 8)]
    far = [
        to_band(src, src, far_s.at[i], far_r.at[i], dy)
        for i, (src, dy) in enumerate(
            (
                (ahead.at[:, first_half], 2),
                (ahead.at[:, first_half], 1),
                (behind.at[:, second_half], 6),
                (behind.at[:, second_half], 7),
                (ahead.at[:, second_half], 1),
                (behind.at[:, first_half], 7),
            )
        )
    ]
    near[0].wait_recv()
    far[0].start()
    far[1].start()
    near[1].wait_recv()
    far[2].start()
    far[3].start()
    near[2].wait_recv()
    far[4].start()
    near[3].wait_recv()
    far[5].start()

    whole = pltpu.make_async_remote_copy(
        got.at[pl.ds(1, NF - 1)], got.at[pl.ds(1, NF - 1)], sa, ra, device_id={"fft": fft_at(0, 1)}, device_id_type=MESH
    )
    whole.wait_recv()

    lane = lax.broadcasted_iota(jnp.int32, (8, 128), 1) // 32
    parts = [[None] * 4 for _ in range(2)]
    for h in range(2):
        for b in range(4):
            rows = jnp.concatenate([got[4 * a + b, h : h + 1, :] for a in range(8)], axis=0)
            for q in range(4):
                shift = 32 * ((b - q) % 4)
                turned = pltpu.roll(rows, shift, 1) if shift else rows
                parts[h][q] = turned if b == 0 else jnp.where(lane == b, turned, parts[h][q])
    fields = [parts[p // 4][p % 4] for p in range(6)]
    code = parts[1][2]
    kx_at = jnp.floor(code * (1.0 / 256.0))
    col_at = code - 256.0 * kx_at

    ix = lax.broadcasted_iota(jnp.int32, (KA, 128), 0).astype(F32)
    iy = lax.broadcasted_iota(jnp.int32, (4 * KB, 128), 0).astype(F32)
    his = [f.astype(BF16).astype(F32) for f in fields]
    los = [f - h for f, h in zip(fields, his)]
    on = [ix == kx_at[a : a + 1, :] for a in range(8)]
    hot_y = [(iy == col_at[a : a + 1, :]).astype(F32).astype(BF16) for a in range(8)]
    wide = [jnp.concatenate(hot_y[a : a + 2], axis=1) for a in range(0, 8, 2)]
    grid = jnp.zeros((6 * KA, 4 * KB), F32)
    for a in range(0, 8, 2):
        for values in (his, los):
            placed = jnp.concatenate(
                [
                    jnp.concatenate(
                        [jnp.where(on[i], values[p][i : i + 1, :], 0.0).astype(BF16) for i in (a, a + 1)], axis=1
                    )
                    for p in range(6)
                ],
                axis=0,
            )
            grid += mm(placed, wide[a // 2], NT)

    low = lax.broadcasted_iota(jnp.int32, (KA, 2 * KB), 1) < KB
    rows = []
    for z in range(PLANES):
        real, imag = grid[2 * z * KA : (2 * z + 1) * KA], grid[(2 * z + 1) * KA : (2 * z + 2) * KA]
        pair = []
        for s in range(2):
            re, im = real[:, 128 * s : 128 * (s + 1)], imag[:, 128 * s : 128 * (s + 1)]
            re_t, im_t = pltpu.roll(re, KB, 1), pltpu.roll(im, KB, 1)
            pair.append((jnp.where(low, re + re_t, im - im_t), jnp.where(low, im + im_t, re_t - re)))
        rows += [pair[0][0], pair[1][0], pair[0][1], pair[1][1]]
    hi, lo = split(jnp.concatenate(rows, axis=0))
    inv_y = mm(jnp.concatenate([hi, lo], axis=1), wiy[0:256, :]) + mm(hi, wiy[256:384, :])

    planes = []
    for z in range(PLANES):
        part4 = [inv_y[(4 * z + i) * KA : (4 * z + i + 1) * KA] for i in range(4)]
        even = jnp.concatenate([part4[0] + part4[1], part4[2] + part4[3]], axis=1)
        odd = jnp.concatenate([part4[2] - part4[3], part4[0] - part4[1]], axis=1)
        made = []
        for t, values in enumerate((even, odd)):
            hi, lo = split(values)
            made.append(mm(wix[t], jnp.concatenate([hi, lo, hi], axis=0)))
        value = [
            jnp.concatenate(
                [
                    jnp.concatenate([field_pot[i, pl.ds(32 * x + z, 8, stride=4), :] for i in range(2)], axis=1)
                    for x in range(f * U // 8, (f + 1) * U // 8)
                ],
                axis=0,
            )
            for f in range(2)
        ]
        e_re, e_im, o_im, o_re = made[0][:, :V], made[0][:, V:], made[1][:, :V], made[1][:, V:]
        planes += [
            (e_re - o_im) * value[0],
            (e_re + o_im) * value[1],
            (e_im + o_re) * value[0],
            (e_im - o_re) * value[1],
        ]
    hi, lo = split(jnp.concatenate(planes, axis=0))
    fwd_y = mm(hi, wfy[...]) + mm(lo, wfy[...])
    fwd_y = fwd_y[:, :128] + fwd_y[:, 128:]
    stack = []
    for z in range(PLANES):
        right = jnp.concatenate([fwd_y[4 * z * U : (4 * z + 2) * U], fwd_y[(4 * z + 2) * U : (4 * z + 4) * U]], axis=1)
        hi, lo = split(right)
        all_hi = mm(wfx[...], hi)
        sums = all_hi[: 2 * KA] + (all_hi[2 * KA :] + mm(wfx[0 : 2 * KA, :], lo))
        c_re, c_im, s_re, s_im = sums[:KA, :128], sums[:KA, 128:], sums[KA:, :128], sums[KA:, 128:]
        real, imag = [], []
        for p, q in ((c_re + s_im, c_im - s_re), (c_re - s_im, c_im + s_re)):
            m, n = jnp.where(low, p, q), jnp.where(low, q, -p)
            m_t, n_t = pltpu.roll(m, KB, 1), pltpu.roll(n, KB, 1)
            real.append(jnp.where(low, m + m_t, m_t - m))
            imag.append(jnp.where(low, n + n_t, n_t - n))
        stack += [jnp.concatenate(real, axis=1), jnp.concatenate(imag, axis=1)]
    hi, lo = split(jnp.concatenate(stack, axis=0))
    picked = [[] for _ in range(6)]
    for a in range(0, 8, 2):
        spread = mm(hi, wide[a // 2]) + mm(lo, wide[a // 2])
        for i in range(2):
            for p in range(6):
                block = spread[p * KA : (p + 1) * KA, 128 * i : 128 * (i + 1)]
                picked[p].append(jnp.sum(jnp.where(on[a + i], block, 0.0), axis=0, keepdims=True))
    picked = [jnp.concatenate(rows, axis=0) for rows in picked] + [jnp.zeros((8, 128), F32)] * 2
    for h in range(2):
        for b in range(4):
            rows = None
            for q in range(4):
                shift = 32 * ((q - b) % 4)
                turned = pltpu.roll(picked[4 * h + q], shift, 1) if shift else picked[4 * h + q]
                rows = turned if q == 0 else jnp.where(lane == q, turned, rows)
            for a in range(8):
                tiles[4 * a + b, h : h + 1, :] = rows[a : a + 1, :]
    ret[me] = tiles[0]

    for dz, dx in OFFSETS:
        pltpu.make_async_remote_copy(
            tiles.at[4 * dz + dx], ret.at[me], sb, rb, device_id={"fft": fft_at(8 - dz, 4 - dx)}, device_id_type=MESH
        ).start()

    total = jnp.sum(parts[1][3], axis=0, keepdims=True)
    total = total + pltpu.roll(total, 64, 1)
    total = total + pltpu.roll(total, 32, 1)
    c_re = jnp.sum(dfull * total[:, 0:16], axis=1, keepdims=True)
    c_im = jnp.sum(dfull * total[:, 16:32], axis=1, keepdims=True)
    for r in range(16):
        lanes = slice(128 * r, 128 * (r + 1))
        p_re, p_im = proj[0, :, lanes], proj[1, :, lanes]
        nonl[0, r : r + 1, :] = jnp.sum(c_re * p_re - c_im * p_im, axis=0, keepdims=True)
        nonl[1, r : r + 1, :] = jnp.sum(c_re * p_im + c_im * p_re, axis=0, keepdims=True)

    def pass_on(k):
        block = pool.at[core, lax.rem(row + k, 8)]
        pltpu.make_async_remote_copy(block, block, sf, rf, device_id={"band": twin}, device_id_type=MESH).start()

    near[4].wait_recv()
    near[5].wait_recv()
    for k in (0, 1, 2, 6, 7):
        pass_on(k)
    for c in far:
        c.wait_recv()
    for k in (3, 4, 5):
        pass_on(k)
    swap = pltpu.make_async_remote_copy(
        pool.at[core], pool.at[core], sf, rf, device_id={"band": twin}, device_id_type=MESH
    )

    def correlate(at):
        def step(r, carry):
            u, w = carry
            block = pool[:, :, :, pl.ds(pl.multiple_of(128 * r, 128), 128)]
            u = u + block * vecs[at, pl.ds(r, 1), :]
            w = w + block * vecs[at + 1, pl.ds(r, 1), :]
            return u, w

        zero = jnp.zeros((2, 8, 8, 128), F32)
        u, w = lax.fori_loop(0, 16, step, (zero, zero))
        real = [u[k % 2, k // 2][0:4] + w[k % 2, k // 2][4:8] for k in range(16)]
        imag = [w[k % 2, k // 2][0:4] - u[k % 2, k // 2][4:8] for k in range(16)]
        return mm(ones, jnp.concatenate(real + imag, axis=0), NT, HIGHEST)[0:1, :]

    vecs[0] = m_re
    vecs[1] = m_im
    base_re = kin * m_re + nonl[0]
    base_im = kin * m_im + nonl[1]
    swap.wait_recv()
    s_row = correlate(0)

    every = pltpu.make_async_remote_copy(
        tiles.at[pl.ds(1, NF - 1)], ret.at[pl.ds(0, NF - 1)], sb, rb, device_id={"fft": fft_at(0, 1)}, device_id_type=MESH
    )
    every.wait_recv()
    came = jnp.concatenate([ret[d] for d in range(NF)], axis=0)
    came = jnp.concatenate([came] + [pltpu.roll(came, 128 - 32 * q, 1) for q in range(1, 4)], axis=0)
    loc = mm_left(tback, jnp.concatenate([came * cosp, came * sinp], axis=0)).T
    loc_re = jnp.concatenate([loc[0:16, :GZ], loc[16:32, :GZ]], axis=1)
    loc_im = jnp.concatenate([loc[0:16, GZ:], loc[16:32, GZ:]], axis=1)
    a_re = jnp.where(mask, base_re + loc_re, 0.0)
    a_im = jnp.where(mask, base_im + loc_im, 0.0)
    vecs[2] = a_re
    vecs[3] = a_im
    store = pltpu.make_async_copy(vecs.at[pl.ds(2, 2)], out, keep)
    store.start()
    h_row = correlate(2)
    red[me] = jnp.concatenate([h_row, s_row], axis=0)
    for dz, dx in OFFSETS:
        pltpu.make_async_remote_copy(
            red.at[me], red.at[me], sr, rr, device_id={"fft": fft_at(dz, dx)}, device_id_type=MESH
        ).start()

    whole.wait_send()
    every.wait_send()
    for c in near:
        c.wait_send()
    for c in far:
        c.wait_send()
    swap.wait_send()
    last = pltpu.make_async_remote_copy(
        red.at[pl.ds(0, NF - 1)], red.at[pl.ds(0, NF - 1)], sr, rr, device_id={"fft": fft_at(0, 1)}, device_id_type=MESH
    )
    last.wait_recv()
    out_sums[...] = jnp.sum(red[...], axis=0)
    last.wait_send()
    store.wait()


def finish(applied, sums, out, out_h, out_s):
    out[...] = applied[...]
    for c in range(2):
        out_h[c] = sums[0:1, 64 * c : 64 * (c + 1)]
        out_s[c] = sums[1:2, 64 * c : 64 * (c + 1)]


def shards(orbitals, stick_columns, stick_depths, potential, projectors, atom_projectors, couplings, slab_orbitals):
    args = (
        orbitals.reshape(2, 16, 128),
        stick_columns.reshape(1, STK),
        stick_depths,
        potential,
        projectors,
        atom_projectors,
        couplings,
        slab_orbitals,
    ) + tuple(jnp.asarray(t) for t in tables())
    vmem = pl.BlockSpec(memory_space=pltpu.VMEM)
    hbm = pl.BlockSpec(memory_space=pltpu.HBM)
    dma = pltpu.SemaphoreType.DMA
    applied, sums = pl.pallas_call(
        kernel,
        out_shape=(jax.ShapeDtypeStruct((2, 16, 128), F32), jax.ShapeDtypeStruct((2, 128), F32)),
        in_specs=[hbm] * len(args),
        out_specs=(hbm, vmem),
        scratch_shapes=[pltpu.VMEM(a.shape, a.dtype) for a in args]
        + [
            pltpu.VMEM((NF, 2, 128), F32),
            pltpu.VMEM((NF, 2, 128), F32),
            pltpu.VMEM((NF, 2, 128), F32),
            pltpu.VMEM((NF, 2, 128), F32),
            pltpu.VMEM((2, 8, 8, 2048), F32),
            pltpu.VMEM((NF, 2, 128), F32),
            pltpu.VMEM((2, 16, 128), F32),
            pltpu.VMEM((4, 16, 128), F32),
            pltpu.VMEM((2, 8 * U, 128), F32),
            dma((len(args),)),
        ]
        + [dma] * 5
        + [dma((6,))] * 4
        + [dma] * 4,
        compiler_params=pltpu.CompilerParams(
            collective_id=0, has_side_effects=True, vmem_limit_bytes=64 * 1024 * 1024
        ),
        name="davidson",
    )(*args)
    applied, proj_h, proj_s = pl.pallas_call(
        finish,
        out_shape=(
            jax.ShapeDtypeStruct((2, 16, 128), F32),
            jax.ShapeDtypeStruct((2, 1, 64), F32),
            jax.ShapeDtypeStruct((2, 1, 64), F32),
        ),
        in_specs=[vmem, vmem],
        out_specs=(vmem, vmem, vmem),
        compiler_params=pltpu.CompilerParams(vmem_limit_bytes=64 * 1024 * 1024),
        name="finish",
    )(applied, sums)
    return applied.reshape(2, 1, 2048), proj_h, proj_s


def solution(mesh):
    in_specs = (
        P(None, "band", "fft"),
        P("fft"),
        P("fft", None),
        P("fft", None),
        P(None, None, "fft"),
        P(),
        P(),
        P(None, "band", "fft"),
    )
    out_specs = (P(None, "band", "fft"), P(None, "band", None), P(None, "band", None))
    return jax.shard_map(shards, mesh=mesh, in_specs=in_specs, out_specs=out_specs, check_vma=False)
```

```python
import functools
import math

import jax
import jax.numpy as jnp
import ml_dtypes
import numpy as np
from jax import lax
from jax.experimental import pallas as pl
from jax.experimental.pallas import tpu as pltpu
from jax.sharding import PartitionSpec as P

NX = 180
NY = 180
NZ = 96
GZ = 64
RADIUS = 45
NXY = NX * NY
NF = 32
STK = 32
KA = 48
KB = 64
U = 96
V = 256
PLANES = 3

MESH = pl.DeviceIdType.MESH
HIGHEST = lax.Precision.HIGHEST
F32 = jnp.float32
BF16 = jnp.bfloat16
NN = (((1,), (0,)), ((), ()))
NT = (((1,), (1,)), ((), ()))


def mm(a, b, dims=NN, precision=None):
    return lax.dot_general(a, b, dims, precision=precision, preferred_element_type=F32)


def split(x):
    hi = x.astype(BF16)
    return hi, (x - hi.astype(F32)).astype(BF16)


def mm_right(a, table, dims=NN):
    hi, lo = split(a)
    return mm(hi, table[0], dims) + (mm(lo, table[0], dims) + mm(hi, table[1], dims))


def mm_left(table, b, dims=NN):
    hi, lo = split(b)
    return mm(table[0], hi, dims) + (mm(table[0], lo, dims) + mm(table[1], hi, dims))


def far_first():
    hops = lambda o: min(o[0], 8 - o[0]) + min(o[1], 4 - o[1])
    every = [(dz, dx) for dz in range(8) for dx in range(4)]
    return sorted((o for o in every if o != (0, 0)), key=lambda o: (-hops(o), o))


OFFSETS = far_first()


@functools.lru_cache(maxsize=None)
def tables():
    tau = 2.0 * math.pi
    j = np.arange(GZ)
    depth = np.arange(NZ + 1)
    t1 = np.zeros((4, NF, 2, 2, GZ))
    t2 = np.zeros((4, NF, 2, 2, GZ))
    tb = np.zeros((2, GZ, 2, 4, NF, 2))
    turn = np.zeros((2, 4, NF, 2, 128))
    for d in range(NF):
        for p in range(2 * PLANES):
            h, q = p // 4, p % 4
            z = PLANES * d + p // 2
            th = tau * (j * z % NZ) / NZ
            c, s = np.cos(th), np.sin(th)
            if p % 2 == 0:
                t1[q, d, h] = c, -s
                t2[q, d, h] = -s, -c
                tb[0, :, 0, q, d, h], tb[0, :, 1, q, d, h] = c, -s
                tb[1, :, 0, q, d, h], tb[1, :, 1, q, d, h] = -s, -c
            else:
                t1[q, d, h] = s, c
                t2[q, d, h] = c, -s
                tb[0, :, 0, q, d, h], tb[0, :, 1, q, d, h] = s, c
                tb[1, :, 0, q, d, h], tb[1, :, 1, q, d, h] = c, -s
            ph = tau * (depth * z % NZ) / NZ
            turn[0, q, d, h, : NZ + 1] = np.cos(ph)
            turn[1, q, d, h, : NZ + 1] = np.sin(ph)
    n = RADIUS + 1
    k = np.arange(n)
    ang = tau * ((k[:, None] * np.arange(NY)[None, :]) % NY) / NY
    wiy = np.zeros((2, KB, V))
    wiy[0, :n, :NY], wiy[1, :n, :NY] = np.cos(ang) / NY, np.sin(ang) / NY
    wfy = np.zeros((V, 2, KB))
    wfy[:NY, 0, :n], wfy[:NY, 1, :n] = np.cos(ang).T, np.sin(ang).T
    g = np.arange(NX // 2 + 1)
    ang = tau * ((k[:, None] * g[None, :]) % NX) / NX
    c, s = np.cos(ang), np.sin(ang)
    wix = np.zeros((2, U, KA))
    wix[0, : len(g), :n], wix[1, : len(g), :n] = c.T / NX, s.T / NX
    wfx = np.zeros((2, KA, 2, U))
    wfx[0, :n, 0, : len(g)], wfx[0, :n, 1, : len(g)] = c, c
    wfx[1, :n, 0, : len(g)], wfx[1, :n, 1, : len(g)] = s, -s
    back = np.transpose(tb.reshape(2, GZ, 2, 256), (2, 1, 0, 3)).reshape(2 * GZ, 512)
    tz = np.concatenate([t1.reshape(256, 128), t2.reshape(256, 128)], axis=0) / NZ

    def parts(x):
        x = np.asarray(x, np.float32)
        hi = x.astype(ml_dtypes.bfloat16)
        lo = (x - hi.astype(np.float32)).astype(ml_dtypes.bfloat16)
        return np.stack([hi, lo])

    yh, yl = parts(wiy.reshape(2 * KB, V))
    xh, xl = parts(wix)
    fh, fl = parts(wfy.reshape(V, 2 * KB))
    gh, gl = parts(wfx.reshape(2 * KA, 2 * U))
    return (
        parts(tz),
        parts(turn.reshape(512, 128)),
        np.concatenate([yh, yh, yl], axis=0),
        np.concatenate([xh, xh, xl], axis=2),
        np.concatenate([fh, fl], axis=1),
        np.concatenate([gh, gl], axis=0),
        parts(back),
    )


def kernel(
    orb_h, cols_h, deps_h, pot_h, proj_h, atoms_h, coup_h, slab_h, tz_h, turn_h, wiy_h, wix_h, wfy_h, wfx_h, tback_h,
    out, out_sums,
    orb, cols, deps, pot, proj, atoms, coup, slab, tz, turn, wiy, wix, wfy, wfx, tback,
    mine, got, tiles, ret, pool, red, nonl, vecs, field_pot,
    loads, sa, ra, sb, rb, near_s, near_r, far_s, far_r, sf, rf, sr, rr,
):
    me = lax.axis_index("fft")
    band = lax.axis_index("band")
    my_z, my_x = me // 4, lax.rem(me, 4)
    core = lax.rem(band, 2)
    row = band // 2
    twin = band + 1 - 2 * core

    def fft_at(dz, dx):
        return lax.rem(my_z + dz, 8) * 4 + lax.rem(my_x + dx, 4)

    def band_at(dy):
        return lax.rem(band + 2 * dy, 16)

    barrier = pltpu.get_barrier_semaphore()
    for dz, dx in OFFSETS:
        pl.semaphore_signal(barrier, inc=1, device_id={"fft": fft_at(dz, dx)}, device_id_type=MESH)
    for dy in (2, 6, 1, 7):
        pl.semaphore_signal(barrier, inc=1, device_id={"band": band_at(dy)}, device_id_type=MESH)
    pl.semaphore_signal(barrier, inc=1, device_id={"band": twin}, device_id_type=MESH)

    pairs = (
        (orb_h, orb), (deps_h, deps), (cols_h, cols), (tz_h, tz), (turn_h, turn), (proj_h, proj), (slab_h, slab),
        (pot_h, pot), (atoms_h, atoms), (coup_h, coup), (wiy_h, wiy), (wix_h, wix), (wfy_h, wfy), (wfx_h, wfx),
        (tback_h, tback),
    )
    copies = [pltpu.make_async_copy(a, b, loads.at[i]) for i, (a, b) in enumerate(pairs)]
    for c in copies:
        c.start()
    for c in copies[:5]:
        c.wait()

    dep_even = deps[pl.ds(0, 16, stride=2), :]
    dep_odd = deps[pl.ds(1, 16, stride=2), :]
    dep16 = jnp.concatenate([dep_even, dep_odd], axis=1)
    mask = dep16 < NZ
    m_re = jnp.where(mask, orb[0], 0.0)
    m_im = jnp.where(mask, orb[1], 0.0)
    x2 = jnp.concatenate(
        [
            jnp.concatenate([m_re[:, :GZ], m_im[:, :GZ]], axis=1),
            jnp.concatenate([m_re[:, GZ:], m_im[:, GZ:]], axis=1),
        ],
        axis=0,
    )
    x2 = jnp.concatenate([x2] * 4, axis=0)
    d12 = mm_left(tz, x2, NT)

    dep32 = jnp.concatenate([dep_even, dep_odd] * 4, axis=0).astype(F32)
    first = (lax.broadcasted_iota(jnp.int32, (8, GZ), 1) == 0).astype(F32)
    dep0 = mm(first, dep32, NT)
    hot = (lax.broadcasted_iota(jnp.int32, (128, 128), 0).astype(F32) == dep0[0:1, :]).astype(F32).astype(BF16)
    phase = mm(turn[0], hot) + mm(turn[1], hot)
    cosp, sinp = phase[:256], phase[256:]

    colf = cols[...].astype(F32)
    qx = jnp.floor((colf + 0.5) * (1.0 / NY))
    qy = colf - NY * qx
    live = cols[...] < NXY
    far_x, far_y = qx >= 90.0, qy >= 90.0
    kx = jnp.where(live, jnp.where(far_x, NX - qx, qx), 63.0)
    ky = jnp.where(live, jnp.where(far_y, NY - qy, qy), 0.0)
    col = ky + jnp.where(far_x, 2.0 * KB, 0.0) + jnp.where(far_y, 1.0 * KB, 0.0)
    si = lax.broadcasted_iota(jnp.int32, (STK, 128), 0)
    so = lax.rem(lax.broadcasted_iota(jnp.int32, (STK, 128), 1), 32)
    perm = (si == 2 * lax.rem(so, 16) + so // 16).astype(F32)
    kxy = mm(jnp.concatenate([kx, col, jnp.zeros((6, STK), F32)], axis=0), perm)
    code = kxy[0:1, :] * 256.0 + kxy[1:2, :]

    copies[5].wait()
    acc_re = jnp.zeros((16, 128), F32)
    acc_im = jnp.zeros((16, 128), F32)
    for r in range(16):
        lanes = slice(128 * r, 128 * (r + 1))
        p_re, p_im = proj[0, :, lanes], proj[1, :, lanes]
        a, b = m_re[r : r + 1, :], m_im[r : r + 1, :]
        acc_re += a * p_re + b * p_im
        acc_im += b * p_re - a * p_im
    ones = jnp.ones((8, 128), F32)
    part = mm(ones, jnp.concatenate([acc_re, acc_im] * 4, axis=0), NT, HIGHEST)

    field = cosp * d12[:256] + sinp * d12[256:]
    group = lax.broadcasted_iota(jnp.int32, (64, 128), 1) // 32
    odd = lax.rem(lax.broadcasted_iota(jnp.int32, (64, 128), 0), 2) == 1
    message = jnp.where(
        group == 0,
        field[0:64],
        jnp.where(
            group == 1,
            field[64:128],
            jnp.where(
                group == 2,
                jnp.where(odd, jnp.broadcast_to(code, (64, 128)), field[128:192]),
                jnp.where(odd, jnp.broadcast_to(part[0:1, :], (64, 128)), field[192:256]),
            ),
        ),
    )
    for d in range(NF):
        mine[d] = message[2 * d : 2 * d + 2]
    got[0] = mine[me]

    copies[6].wait()
    pool[core, row] = jnp.concatenate([slab[0], slab[1]], axis=0)

    pl.semaphore_wait(barrier, NF - 1 + 4 + 1)

    for dz, dx in OFFSETS:
        to = fft_at(dz, dx)
        pltpu.make_async_remote_copy(
            mine.at[to], got.at[4 * dz + dx], sa, ra, device_id={"fft": to}, device_id_type=MESH
        ).start()

    def to_band(src, dst, send, recv, dy):
        return pltpu.make_async_remote_copy(
            src, dst, send, recv, device_id={"band": band_at(dy)}, device_id_type=MESH
        )

    own = pool.at[core, row]
    first_half, second_half = pl.ds(0, 1024), pl.ds(1024, 1024)
    near = [
        to_band(src, src, near_s.at[i], near_r.at[i], dy)
        for i, (src, dy) in enumerate(
            (
                (own.at[:, first_half], 2),
                (own.at[:, second_half], 6),
                (own.at[:, second_half], 2),
                (own.at[:, first_half], 6),
                (own, 1),
                (own, 7),
            )
        )
    ]
    for c in near:
        c.start()

    sr_i = lax.broadcasted_iota(jnp.int32, (16, STK), 1) // 2
    rr_i = lax.broadcasted_iota(jnp.int32, (16, STK), 0)
    s_i = lax.broadcasted_iota(jnp.int32, (STK, 128), 0)
    l_i = lax.broadcasted_iota(jnp.int32, (STK, 128), 1)
    half = (lax.rem(s_i, 2) == l_i // GZ).astype(F32)
    kx16 = mm(jnp.where(sr_i == rr_i, jnp.broadcast_to(kx, (16, STK)), 0.0), half)
    ky16 = mm(jnp.where(sr_i == rr_i, jnp.broadcast_to(ky, (16, STK)), 0.0), half)
    fz = jnp.where(dep16 < NZ // 2, dep16, dep16 - NZ).astype(F32)
    kin = (0.5 / (RADIUS * RADIUS)) * (kx16 * kx16 + ky16 * ky16 + fz * fz)

    for c in copies[7:]:
        c.wait()

    dfull = jnp.zeros((16, 16), F32)
    p_i = lax.broadcasted_iota(jnp.int32, (16, 8), 0)
    for a in range(2):
        owner = (p_i == jnp.broadcast_to(atoms[a : a + 1, :], (16, 8))).astype(F32)
        dfull += mm(mm(owner, coup[a], NN, HIGHEST), owner, NT, HIGHEST)

    field_pot[...] = jnp.zeros_like(field_pot)
    for x in range(NX):
        r = 4 * (x if x <= NX // 2 else U + NX - x)
        field_pot[0, r : r + PLANES, :] = pot[:, NY * x : NY * x + 128]
        field_pot[1, r : r + PLANES, 0 : NY - 128] = pot[:, NY * x + 128 : NY * x + NY]

    ahead = pool.at[core, lax.rem(row + 6, 8)]
    behind = pool.at[core, lax.rem(row + 2, 8)]
    far = [
        to_band(src, src, far_s.at[i], far_r.at[i], dy)
        for i, (src, dy) in enumerate(
            (
                (ahead.at[:, first_half], 2),
                (ahead.at[:, first_half], 1),
                (behind.at[:, second_half], 6),
                (behind.at[:, second_half], 7),
                (ahead.at[:, second_half], 1),
                (behind.at[:, first_half], 7),
            )
        )
    ]
    whole = pltpu.make_async_remote_copy(
        got.at[pl.ds(1, NF - 1)], got.at[pl.ds(1, NF - 1)], sa, ra, device_id={"fft": fft_at(0, 1)}, device_id_type=MESH
    )
    whole.wait_recv()

    lane = lax.broadcasted_iota(jnp.int32, (8, 128), 1) // 32
    parts = [[None] * 4 for _ in range(2)]
    for h in range(2):
        for b in range(4):
            rows = jnp.concatenate([got[4 * a + b, h : h + 1, :] for a in range(8)], axis=0)
            for q in range(4):
                shift = 32 * ((b - q) % 4)
                turned = pltpu.roll(rows, shift, 1) if shift else rows
                parts[h][q] = turned if b == 0 else jnp.where(lane == b, turned, parts[h][q])
    fields = [parts[p // 4][p % 4] for p in range(6)]
    code = parts[1][2]
    kx_at = jnp.floor(code * (1.0 / 256.0))
    col_at = code - 256.0 * kx_at

    ix = lax.broadcasted_iota(jnp.int32, (KA, 128), 0).astype(F32)
    iy = lax.broadcasted_iota(jnp.int32, (4 * KB, 128), 0).astype(F32)
    his = [f.astype(BF16).astype(F32) for f in fields]
    los = [f - h for f, h in zip(fields, his)]
    on = [ix == kx_at[a : a + 1, :] for a in range(8)]
    hot_y = [(iy == col_at[a : a + 1, :]).astype(F32).astype(BF16) for a in range(8)]
    wide = [jnp.concatenate(hot_y[a : a + 2], axis=1) for a in range(0, 8, 2)]
    grid = jnp.zeros((6 * KA, 4 * KB), F32)
    for a in range(0, 8, 2):
        for values in (his, los):
            placed = jnp.concatenate(
                [
                    jnp.concatenate(
                        [jnp.where(on[i], values[p][i : i + 1, :], 0.0).astype(BF16) for i in (a, a + 1)], axis=1
                    )
                    for p in range(6)
                ],
                axis=0,
            )
            grid += mm(placed, wide[a // 2], NT)

    low = lax.broadcasted_iota(jnp.int32, (KA, 2 * KB), 1) < KB
    rows = []
    for z in range(PLANES):
        real, imag = grid[2 * z * KA : (2 * z + 1) * KA], grid[(2 * z + 1) * KA : (2 * z + 2) * KA]
        pair = []
        for s in range(2):
            re, im = real[:, 128 * s : 128 * (s + 1)], imag[:, 128 * s : 128 * (s + 1)]
            re_t, im_t = pltpu.roll(re, KB, 1), pltpu.roll(im, KB, 1)
            pair.append((jnp.where(low, re + re_t, im - im_t), jnp.where(low, im + im_t, re_t - re)))
        rows += [pair[0][0], pair[1][0], pair[0][1], pair[1][1]]
    hi, lo = split(jnp.concatenate(rows, axis=0))
    inv_y = mm(jnp.concatenate([hi, lo], axis=1), wiy[0:256, :]) + mm(hi, wiy[256:384, :])

    planes = []
    for z in range(PLANES):
        part4 = [inv_y[(4 * z + i) * KA : (4 * z + i + 1) * KA] for i in range(4)]
        even = jnp.concatenate([part4[0] + part4[1], part4[2] + part4[3]], axis=1)
        odd = jnp.concatenate([part4[2] - part4[3], part4[0] - part4[1]], axis=1)
        made = []
        for t, values in enumerate((even, odd)):
            hi, lo = split(values)
            made.append(mm(wix[t], jnp.concatenate([hi, lo, hi], axis=0)))
        value = [
            jnp.concatenate(
                [
                    jnp.concatenate([field_pot[i, pl.ds(32 * x + z, 8, stride=4), :] for i in range(2)], axis=1)
                    for x in range(f * U // 8, (f + 1) * U // 8)
                ],
                axis=0,
            )
            for f in range(2)
        ]
        e_re, e_im, o_im, o_re = made[0][:, :V], made[0][:, V:], made[1][:, :V], made[1][:, V:]
        planes += [
            (e_re - o_im) * value[0],
            (e_re + o_im) * value[1],
            (e_im + o_re) * value[0],
            (e_im - o_re) * value[1],
        ]
    hi, lo = split(jnp.concatenate(planes, axis=0))
    near[0].wait_recv()
    far[0].start()
    far[1].start()
    near[1].wait_recv()
    far[2].start()
    far[3].start()
    near[2].wait_recv()
    far[4].start()
    near[3].wait_recv()
    far[5].start()

    fwd_y = mm(hi, wfy[...]) + mm(lo, wfy[...])
    fwd_y = fwd_y[:, :128] + fwd_y[:, 128:]
    stack = []
    for z in range(PLANES):
        right = jnp.concatenate([fwd_y[4 * z * U : (4 * z + 2) * U], fwd_y[(4 * z + 2) * U : (4 * z + 4) * U]], axis=1)
        hi, lo = split(right)
        all_hi = mm(wfx[...], hi)
        sums = all_hi[: 2 * KA] + (all_hi[2 * KA :] + mm(wfx[0 : 2 * KA, :], lo))
        c_re, c_im, s_re, s_im = sums[:KA, :128], sums[:KA, 128:], sums[KA:, :128], sums[KA:, 128:]
        real, imag = [], []
        for p, q in ((c_re + s_im, c_im - s_re), (c_re - s_im, c_im + s_re)):
            m, n = jnp.where(low, p, q), jnp.where(low, q, -p)
            m_t, n_t = pltpu.roll(m, KB, 1), pltpu.roll(n, KB, 1)
            real.append(jnp.where(low, m + m_t, m_t - m))
            imag.append(jnp.where(low, n + n_t, n_t - n))
        stack += [jnp.concatenate(real, axis=1), jnp.concatenate(imag, axis=1)]
    hi, lo = split(jnp.concatenate(stack, axis=0))
    picked = [[] for _ in range(6)]
    for a in range(0, 8, 2):
        spread = mm(hi, wide[a // 2]) + mm(lo, wide[a // 2])
        for i in range(2):
            for p in range(6):
                block = spread[p * KA : (p + 1) * KA, 128 * i : 128 * (i + 1)]
                picked[p].append(jnp.sum(jnp.where(on[a + i], block, 0.0), axis=0, keepdims=True))
    picked = [jnp.concatenate(rows, axis=0) for rows in picked] + [jnp.zeros((8, 128), F32)] * 2
    for h in range(2):
        for b in range(4):
            rows = None
            for q in range(4):
                shift = 32 * ((q - b) % 4)
                turned = pltpu.roll(picked[4 * h + q], shift, 1) if shift else picked[4 * h + q]
                rows = turned if q == 0 else jnp.where(lane == q, turned, rows)
            for a in range(8):
                tiles[4 * a + b, h : h + 1, :] = rows[a : a + 1, :]
    ret[me] = tiles[0]

    for dz, dx in OFFSETS:
        pltpu.make_async_remote_copy(
            tiles.at[4 * dz + dx], ret.at[me], sb, rb, device_id={"fft": fft_at(8 - dz, 4 - dx)}, device_id_type=MESH
        ).start()

    total = jnp.sum(parts[1][3], axis=0, keepdims=True)
    total = total + pltpu.roll(total, 64, 1)
    total = total + pltpu.roll(total, 32, 1)
    c_re = jnp.sum(dfull * total[:, 0:16], axis=1, keepdims=True)
    c_im = jnp.sum(dfull * total[:, 16:32], axis=1, keepdims=True)
    for r in range(16):
        lanes = slice(128 * r, 128 * (r + 1))
        p_re, p_im = proj[0, :, lanes], proj[1, :, lanes]
        nonl[0, r : r + 1, :] = jnp.sum(c_re * p_re - c_im * p_im, axis=0, keepdims=True)
        nonl[1, r : r + 1, :] = jnp.sum(c_re * p_im + c_im * p_re, axis=0, keepdims=True)

    def pass_on(k):
        block = pool.at[core, lax.rem(row + k, 8)]
        pltpu.make_async_remote_copy(block, block, sf, rf, device_id={"band": twin}, device_id_type=MESH).start()

    near[4].wait_recv()
    near[5].wait_recv()
    for k in (0, 1, 2, 6, 7):
        pass_on(k)
    for c in far:
        c.wait_recv()
    for k in (3, 4, 5):
        pass_on(k)
    swap = pltpu.make_async_remote_copy(
        pool.at[core], pool.at[core], sf, rf, device_id={"band": twin}, device_id_type=MESH
    )

    def correlate(at):
        def step(r, carry):
            u, w = carry
            block = pool[:, :, :, pl.ds(pl.multiple_of(128 * r, 128), 128)]
            u = u + block * vecs[at, pl.ds(r, 1), :]
            w = w + block * vecs[at + 1, pl.ds(r, 1), :]
            return u, w

        zero = jnp.zeros((2, 8, 8, 128), F32)
        u, w = lax.fori_loop(0, 16, step, (zero, zero))
        real = [u[k % 2, k // 2][0:4] + w[k % 2, k // 2][4:8] for k in range(16)]
        imag = [w[k % 2, k // 2][0:4] - u[k % 2, k // 2][4:8] for k in range(16)]
        return mm(ones, jnp.concatenate(real + imag, axis=0), NT, HIGHEST)[0:1, :]

    vecs[0] = m_re
    vecs[1] = m_im
    base_re = kin * m_re + nonl[0]
    base_im = kin * m_im + nonl[1]

    every = pltpu.make_async_remote_copy(
        tiles.at[pl.ds(1, NF - 1)], ret.at[pl.ds(0, NF - 1)], sb, rb, device_id={"fft": fft_at(0, 1)}, device_id_type=MESH
    )
    every.wait_recv()
    came = jnp.concatenate([ret[d] for d in range(NF)], axis=0)
    came = jnp.concatenate([came] + [pltpu.roll(came, 128 - 32 * q, 1) for q in range(1, 4)], axis=0)
    loc = mm_left(tback, jnp.concatenate([came * cosp, came * sinp], axis=0)).T
    loc_re = jnp.concatenate([loc[0:16, :GZ], loc[16:32, :GZ]], axis=1)
    loc_im = jnp.concatenate([loc[0:16, GZ:], loc[16:32, GZ:]], axis=1)
    a_re = jnp.where(mask, base_re + loc_re, 0.0)
    a_im = jnp.where(mask, base_im + loc_im, 0.0)
    vecs[2] = a_re
    vecs[3] = a_im
    out[0] = a_re
    out[1] = a_im
    swap.wait_recv()
    s_row = correlate(0)
    h_row = correlate(2)
    red[me] = jnp.concatenate([h_row, s_row], axis=0)
    for dz, dx in OFFSETS:
        pltpu.make_async_remote_copy(
            red.at[me], red.at[me], sr, rr, device_id={"fft": fft_at(dz, dx)}, device_id_type=MESH
        ).start()

    whole.wait_send()
    every.wait_send()
    for c in near:
        c.wait_send()
    for c in far:
        c.wait_send()
    swap.wait_send()
    last = pltpu.make_async_remote_copy(
        red.at[pl.ds(0, NF - 1)], red.at[pl.ds(0, NF - 1)], sr, rr, device_id={"fft": fft_at(0, 1)}, device_id_type=MESH
    )
    last.wait_recv()
    out_sums[...] = jnp.sum(red[...], axis=0)
    last.wait_send()


def finish(applied, sums, out, out_h, out_s):
    out[...] = applied[...]
    for c in range(2):
        out_h[c] = sums[0:1, 64 * c : 64 * (c + 1)]
        out_s[c] = sums[1:2, 64 * c : 64 * (c + 1)]


def shards(orbitals, stick_columns, stick_depths, potential, projectors, atom_projectors, couplings, slab_orbitals):
    args = (
        orbitals.reshape(2, 16, 128),
        stick_columns.reshape(1, STK),
        stick_depths,
        potential,
        projectors,
        atom_projectors,
        couplings,
        slab_orbitals,
    ) + tuple(jnp.asarray(t) for t in tables())
    vmem = pl.BlockSpec(memory_space=pltpu.VMEM)
    hbm = pl.BlockSpec(memory_space=pltpu.HBM)
    dma = pltpu.SemaphoreType.DMA
    applied, sums = pl.pallas_call(
        kernel,
        out_shape=(pltpu.VMEM((2, 16, 128), F32), pltpu.VMEM((2, 128), F32)),
        in_specs=[hbm] * len(args),
        out_specs=(vmem, vmem),
        scratch_shapes=[pltpu.VMEM(a.shape, a.dtype) for a in args]
        + [
            pltpu.VMEM((NF, 2, 128), F32),
            pltpu.VMEM((NF, 2, 128), F32),
            pltpu.VMEM((NF, 2, 128), F32),
            pltpu.VMEM((NF, 2, 128), F32),
            pltpu.VMEM((2, 8, 8, 2048), F32),
            pltpu.VMEM((NF, 2, 128), F32),
            pltpu.VMEM((2, 16, 128), F32),
            pltpu.VMEM((4, 16, 128), F32),
            pltpu.VMEM((2, 8 * U, 128), F32),
            dma((len(args),)),
        ]
        + [dma] * 4
        + [dma((6,))] * 4
        + [dma] * 4,
        compiler_params=pltpu.CompilerParams(
            collective_id=0, has_side_effects=True, vmem_limit_bytes=65024 * 1024
        ),
        name="davidson",
    )(*args)
    applied, proj_h, proj_s = pl.pallas_call(
        finish,
        out_shape=(
            jax.ShapeDtypeStruct((2, 16, 128), F32),
            jax.ShapeDtypeStruct((2, 1, 64), F32),
            jax.ShapeDtypeStruct((2, 1, 64), F32),
        ),
        in_specs=[vmem, vmem],
        out_specs=(vmem, vmem, vmem),
        compiler_params=pltpu.CompilerParams(vmem_limit_bytes=1024 * 1024),
        name="finish",
    )(applied, sums)
    return applied.reshape(2, 1, 2048), proj_h, proj_s


def solution(mesh):
    in_specs = (
        P(None, "band", "fft"),
        P("fft"),
        P("fft", None),
        P("fft", None),
        P(None, None, "fft"),
        P(),
        P(),
        P(None, "band", "fft"),
    )
    out_specs = (P(None, "band", "fft"), P(None, "band", None), P(None, "band", None))
    return jax.shard_map(shards, mesh=mesh, in_specs=in_specs, out_specs=out_specs, check_vma=False)
```

```python
import functools
import math

import jax
import jax.numpy as jnp
import ml_dtypes
import numpy as np
from jax import lax
from jax.experimental import pallas as pl
from jax.experimental.pallas import tpu as pltpu
from jax.sharding import PartitionSpec as P

NX = 180
NY = 180
NZ = 96
GZ = 64
RADIUS = 45
NXY = NX * NY
NF = 32
STK = 32
KA = 48
KB = 64
U = 96
V = 256
PLANES = 3

MESH = pl.DeviceIdType.MESH
HIGHEST = lax.Precision.HIGHEST
F32 = jnp.float32
BF16 = jnp.bfloat16
NN = (((1,), (0,)), ((), ()))
NT = (((1,), (1,)), ((), ()))


def mm(a, b, dims=NN, precision=None):
    return lax.dot_general(a, b, dims, precision=precision, preferred_element_type=F32)


def split(x):
    hi = x.astype(BF16)
    return hi, (x - hi.astype(F32)).astype(BF16)


def mm_right(a, table, dims=NN):
    hi, lo = split(a)
    return mm(hi, table[0], dims) + (mm(lo, table[0], dims) + mm(hi, table[1], dims))


def mm_left(table, b, dims=NN):
    hi, lo = split(b)
    return mm(table[0], hi, dims) + (mm(table[0], lo, dims) + mm(table[1], hi, dims))


def far_first():
    hops = lambda o: min(o[0], 8 - o[0]) + min(o[1], 4 - o[1])
    every = [(dz, dx) for dz in range(8) for dx in range(4)]
    return sorted((o for o in every if o != (0, 0)), key=lambda o: (-hops(o), o))


OFFSETS = far_first()


@functools.lru_cache(maxsize=None)
def tables():
    tau = 2.0 * math.pi
    j = np.arange(GZ)
    depth = np.arange(NZ + 1)
    t1 = np.zeros((4, NF, 2, 2, GZ))
    t2 = np.zeros((4, NF, 2, 2, GZ))
    tb = np.zeros((2, GZ, 2, 4, NF, 2))
    turn = np.zeros((2, 4, NF, 2, 128))
    for d in range(NF):
        for p in range(2 * PLANES):
            h, q = p // 4, p % 4
            z = PLANES * d + p // 2
            th = tau * (j * z % NZ) / NZ
            c, s = np.cos(th), np.sin(th)
            if p % 2 == 0:
                t1[q, d, h] = c, -s
                t2[q, d, h] = -s, -c
                tb[0, :, 0, q, d, h], tb[0, :, 1, q, d, h] = c, -s
                tb[1, :, 0, q, d, h], tb[1, :, 1, q, d, h] = -s, -c
            else:
                t1[q, d, h] = s, c
                t2[q, d, h] = c, -s
                tb[0, :, 0, q, d, h], tb[0, :, 1, q, d, h] = s, c
                tb[1, :, 0, q, d, h], tb[1, :, 1, q, d, h] = c, -s
            ph = tau * (depth * z % NZ) / NZ
            turn[0, q, d, h, : NZ + 1] = np.cos(ph)
            turn[1, q, d, h, : NZ + 1] = np.sin(ph)
    n = RADIUS + 1
    k = np.arange(n)
    ang = tau * ((k[:, None] * np.arange(NY)[None, :]) % NY) / NY
    wiy = np.zeros((2, KB, V))
    wiy[0, :n, :NY], wiy[1, :n, :NY] = np.cos(ang) / NY, np.sin(ang) / NY
    wfy = np.zeros((V, 2, KB))
    wfy[:NY, 0, :n], wfy[:NY, 1, :n] = np.cos(ang).T, np.sin(ang).T
    g = np.arange(NX // 2 + 1)
    ang = tau * ((k[:, None] * g[None, :]) % NX) / NX
    c, s = np.cos(ang), np.sin(ang)
    wix = np.zeros((2, U, KA))
    wix[0, : len(g), :n], wix[1, : len(g), :n] = c.T / NX, s.T / NX
    wfx = np.zeros((2, KA, 2, U))
    wfx[0, :n, 0, : len(g)], wfx[0, :n, 1, : len(g)] = c, c
    wfx[1, :n, 0, : len(g)], wfx[1, :n, 1, : len(g)] = s, -s
    back = np.transpose(tb.reshape(2, GZ, 2, 256), (0, 3, 2, 1)).reshape(512, 2 * GZ)
    tz = np.concatenate([t1.reshape(256, 128), t2.reshape(256, 128)], axis=0) / NZ

    def parts(x):
        x = np.asarray(x, np.float32)
        hi = x.astype(ml_dtypes.bfloat16)
        lo = (x - hi.astype(np.float32)).astype(ml_dtypes.bfloat16)
        return np.stack([hi, lo])

    yh, yl = parts(wiy.reshape(2 * KB, V))
    xh, xl = parts(wix)
    fh, fl = parts(wfy.reshape(V, 2 * KB))
    gh, gl = parts(wfx.reshape(2 * KA, 2 * U))
    return (
        parts(tz),
        parts(turn.reshape(512, 128)),
        np.concatenate([yh, yh, yl], axis=0),
        np.concatenate([xh, xh, xl], axis=2),
        np.concatenate([fh, fl], axis=1),
        np.concatenate([gh, gl], axis=0),
        np.concatenate(list(parts(back)), axis=1),
    )


def kernel(
    orb_h, cols_h, deps_h, pot_h, proj_h, atoms_h, coup_h, slab_h, tz_h, turn_h, wiy_h, wix_h, wfy_h, wfx_h, tback_h,
    out, out_sums,
    orb, cols, deps, pot, proj, atoms, coup, slab, tz, turn, wiy, wix, wfy, wfx, tback,
    mine, got, tiles, ret, pool, red, nonl, vecs, field_pot, angles, work,
    loads, sa, ra, sb, rb, near_s, near_r, far_s, far_r, sf, rf, sr, rr,
):
    me = lax.axis_index("fft")
    band = lax.axis_index("band")
    my_z, my_x = me // 4, lax.rem(me, 4)
    core = lax.rem(band, 2)
    row = band // 2
    twin = band + 1 - 2 * core

    def fft_at(dz, dx):
        return lax.rem(my_z + dz, 8) * 4 + lax.rem(my_x + dx, 4)

    def band_at(dy):
        return lax.rem(band + 2 * dy, 16)

    barrier = pltpu.get_barrier_semaphore()
    for dz, dx in OFFSETS:
        pl.semaphore_signal(barrier, inc=1, device_id={"fft": fft_at(dz, dx)}, device_id_type=MESH)
    for dy in (2, 6, 1, 7):
        pl.semaphore_signal(barrier, inc=1, device_id={"band": band_at(dy)}, device_id_type=MESH)
    pl.semaphore_signal(barrier, inc=1, device_id={"band": twin}, device_id_type=MESH)

    pairs = (
        (orb_h, orb), (deps_h, deps), (cols_h, cols), (tz_h, tz), (turn_h, turn), (proj_h, proj), (slab_h, slab),
        (pot_h, pot), (atoms_h, atoms), (coup_h, coup), (wiy_h, wiy), (wix_h, wix), (wfy_h, wfy), (wfx_h, wfx),
        (tback_h, tback),
    )
    copies = [pltpu.make_async_copy(a, b, loads.at[i]) for i, (a, b) in enumerate(pairs)]
    for c in copies:
        c.start()
    for c in copies[:5]:
        c.wait()

    dep_even = deps[pl.ds(0, 16, stride=2), :]
    dep_odd = deps[pl.ds(1, 16, stride=2), :]
    dep16 = jnp.concatenate([dep_even, dep_odd], axis=1)
    mask = dep16 < NZ
    m_re = jnp.where(mask, orb[0], 0.0)
    m_im = jnp.where(mask, orb[1], 0.0)
    x2 = jnp.concatenate(
        [
            jnp.concatenate([m_re[:, :GZ], m_im[:, :GZ]], axis=1),
            jnp.concatenate([m_re[:, GZ:], m_im[:, GZ:]], axis=1),
        ],
        axis=0,
    )
    x2 = jnp.concatenate([x2] * 4, axis=0)
    d12 = mm_left(tz, x2, NT)

    dep32 = jnp.concatenate([dep_even, dep_odd] * 4, axis=0).astype(F32)
    first = (lax.broadcasted_iota(jnp.int32, (8, GZ), 1) == 0).astype(F32)
    dep0 = mm(first, dep32, NT)
    hot = (lax.broadcasted_iota(jnp.int32, (128, 128), 0).astype(F32) == dep0[0:1, :]).astype(F32).astype(BF16)
    phase = mm(turn[0], hot) + mm(turn[1], hot)
    cosp, sinp = phase[:256], phase[256:]

    colf = cols[...].astype(F32)
    qx = jnp.floor((colf + 0.5) * (1.0 / NY))
    qy = colf - NY * qx
    live = cols[...] < NXY
    far_x, far_y = qx >= 90.0, qy >= 90.0
    kx = jnp.where(live, jnp.where(far_x, NX - qx, qx), 63.0)
    ky = jnp.where(live, jnp.where(far_y, NY - qy, qy), 0.0)
    col = ky + jnp.where(far_x, 2.0 * KB, 0.0) + jnp.where(far_y, 1.0 * KB, 0.0)
    si = lax.broadcasted_iota(jnp.int32, (STK, 128), 0)
    so = lax.rem(lax.broadcasted_iota(jnp.int32, (STK, 128), 1), 32)
    perm = (si == 2 * lax.rem(so, 16) + so // 16).astype(F32)
    kxy = mm(jnp.concatenate([kx, col, jnp.zeros((6, STK), F32)], axis=0), perm)
    code = kxy[0:1, :] * 256.0 + kxy[1:2, :]

    copies[5].wait()
    acc_re = jnp.zeros((16, 128), F32)
    acc_im = jnp.zeros((16, 128), F32)
    for r in range(16):
        lanes = slice(128 * r, 128 * (r + 1))
        p_re, p_im = proj[0, :, lanes], proj[1, :, lanes]
        a, b = m_re[r : r + 1, :], m_im[r : r + 1, :]
        acc_re += a * p_re + b * p_im
        acc_im += b * p_re - a * p_im
    ones = jnp.ones((8, 128), F32)
    part = mm(ones, jnp.concatenate([acc_re, acc_im] * 4, axis=0), NT, HIGHEST)

    field = cosp * d12[:256] + sinp * d12[256:]
    group = lax.broadcasted_iota(jnp.int32, (64, 128), 1) // 32
    odd = lax.rem(lax.broadcasted_iota(jnp.int32, (64, 128), 0), 2) == 1
    message = jnp.where(
        group == 0,
        field[0:64],
        jnp.where(
            group == 1,
            field[64:128],
            jnp.where(
                group == 2,
                jnp.where(odd, jnp.broadcast_to(code, (64, 128)), field[128:192]),
                jnp.where(odd, jnp.broadcast_to(part[0:1, :], (64, 128)), field[192:256]),
            ),
        ),
    )
    for d in range(NF):
        mine[d] = message[2 * d : 2 * d + 2]
    got[0] = mine[me]

    copies[6].wait()
    pool[core, row] = jnp.concatenate([slab[0], slab[1]], axis=0)

    pl.semaphore_wait(barrier, NF - 1 + 4 + 1)

    for dz, dx in OFFSETS:
        to = fft_at(dz, dx)
        pltpu.make_async_remote_copy(
            mine.at[to], got.at[4 * dz + dx], sa, ra, device_id={"fft": to}, device_id_type=MESH
        ).start()

    def to_band(src, dst, send, recv, dy):
        return pltpu.make_async_remote_copy(
            src, dst, send, recv, device_id={"band": band_at(dy)}, device_id_type=MESH
        )

    own = pool.at[core, row]
    first_half, second_half = pl.ds(0, 1024), pl.ds(1024, 1024)
    near = [
        to_band(src, src, near_s.at[i], near_r.at[i], dy)
        for i, (src, dy) in enumerate(
            (
                (own.at[:, first_half], 2),
                (own.at[:, second_half], 6),
                (own.at[:, second_half], 2),
                (own.at[:, first_half], 6),
                (own, 1),
                (own, 7),
            )
        )
    ]
    for c in near:
        c.start()

    angles[0] = cosp.T[:STK]
    angles[1] = sinp.T[:STK]

    sr_i = lax.broadcasted_iota(jnp.int32, (16, STK), 1) // 2
    rr_i = lax.broadcasted_iota(jnp.int32, (16, STK), 0)
    s_i = lax.broadcasted_iota(jnp.int32, (STK, 128), 0)
    l_i = lax.broadcasted_iota(jnp.int32, (STK, 128), 1)
    half = (lax.rem(s_i, 2) == l_i // GZ).astype(F32)
    kx16 = mm(jnp.where(sr_i == rr_i, jnp.broadcast_to(kx, (16, STK)), 0.0), half)
    ky16 = mm(jnp.where(sr_i == rr_i, jnp.broadcast_to(ky, (16, STK)), 0.0), half)
    fz = jnp.where(dep16 < NZ // 2, dep16, dep16 - NZ).astype(F32)
    kin = (0.5 / (RADIUS * RADIUS)) * (kx16 * kx16 + ky16 * ky16 + fz * fz)

    for c in copies[7:]:
        c.wait()

    dfull = jnp.zeros((16, 16), F32)
    p_i = lax.broadcasted_iota(jnp.int32, (16, 8), 0)
    for a in range(2):
        owner = (p_i == jnp.broadcast_to(atoms[a : a + 1, :], (16, 8))).astype(F32)
        dfull += mm(mm(owner, coup[a], NN, HIGHEST), owner, NT, HIGHEST)

    field_pot[...] = jnp.zeros_like(field_pot)
    for x in range(NX):
        r = 4 * (x if x <= NX // 2 else U + NX - x)
        field_pot[0, r : r + PLANES, :] = pot[:, NY * x : NY * x + 128]
        field_pot[1, r : r + PLANES, 0 : NY - 128] = pot[:, NY * x + 128 : NY * x + NY]

    ahead = pool.at[core, lax.rem(row + 6, 8)]
    behind = pool.at[core, lax.rem(row + 2, 8)]
    far = [
        to_band(src, src, far_s.at[i], far_r.at[i], dy)
        for i, (src, dy) in enumerate(
            (
                (ahead.at[:, first_half], 2),
                (ahead.at[:, first_half], 1),
                (behind.at[:, second_half], 6),
                (behind.at[:, second_half], 7),
                (ahead.at[:, second_half], 1),
                (behind.at[:, first_half], 7),
            )
        )
    ]
    whole = pltpu.make_async_remote_copy(
        got.at[pl.ds(1, NF - 1)], got.at[pl.ds(1, NF - 1)], sa, ra, device_id={"fft": fft_at(0, 1)}, device_id_type=MESH
    )
    whole.wait_recv()

    lane = lax.broadcasted_iota(jnp.int32, (8, 128), 1) // 32
    parts = [[None] * 4 for _ in range(2)]
    for h in range(2):
        for b in range(4):
            rows = jnp.concatenate([got[4 * a + b, h : h + 1, :] for a in range(8)], axis=0)
            for q in range(4):
                shift = 32 * ((b - q) % 4)
                turned = pltpu.roll(rows, shift, 1) if shift else rows
                parts[h][q] = turned if b == 0 else jnp.where(lane == b, turned, parts[h][q])
    fields = [parts[p // 4][p % 4] for p in range(6)]
    code = parts[1][2]
    kx_at = jnp.floor(code * (1.0 / 256.0))
    col_at = code - 256.0 * kx_at

    ix = lax.broadcasted_iota(jnp.int32, (KA, 128), 0).astype(F32)
    iy = lax.broadcasted_iota(jnp.int32, (4 * KB, 128), 0).astype(F32)
    his = [f.astype(BF16).astype(F32) for f in fields]
    los = [f - h for f, h in zip(fields, his)]
    on = [ix == kx_at[a : a + 1, :] for a in range(8)]
    hot_y = [(iy == col_at[a : a + 1, :]).astype(F32).astype(BF16) for a in range(8)]
    wide = [jnp.concatenate(hot_y[a : a + 2], axis=1) for a in range(0, 8, 2)]
    grid = jnp.zeros((6 * KA, 4 * KB), F32)
    for a in range(0, 8, 2):
        for values in (his, los):
            placed = jnp.concatenate(
                [
                    jnp.concatenate(
                        [jnp.where(on[i], values[p][i : i + 1, :], 0.0).astype(BF16) for i in (a, a + 1)], axis=1
                    )
                    for p in range(6)
                ],
                axis=0,
            )
            grid += mm(placed, wide[a // 2], NT)

    low = lax.broadcasted_iota(jnp.int32, (KA, 2 * KB), 1) < KB
    rows = []
    for z in range(PLANES):
        real, imag = grid[2 * z * KA : (2 * z + 1) * KA], grid[(2 * z + 1) * KA : (2 * z + 2) * KA]
        pair = []
        for s in range(2):
            re, im = real[:, 128 * s : 128 * (s + 1)], imag[:, 128 * s : 128 * (s + 1)]
            re_t, im_t = pltpu.roll(re, KB, 1), pltpu.roll(im, KB, 1)
            pair.append((jnp.where(low, re + re_t, im - im_t), jnp.where(low, im + im_t, re_t - re)))
        rows += [pair[0][0], pair[1][0], pair[0][1], pair[1][1]]
    hi, lo = split(jnp.concatenate(rows, axis=0))
    inv_y = mm(jnp.concatenate([hi, lo], axis=1), wiy[0:256, :]) + mm(hi, wiy[256:384, :])

    planes = []
    for z in range(PLANES):
        part4 = [inv_y[(4 * z + i) * KA : (4 * z + i + 1) * KA] for i in range(4)]
        even = jnp.concatenate([part4[0] + part4[1], part4[2] + part4[3]], axis=1)
        odd = jnp.concatenate([part4[2] - part4[3], part4[0] - part4[1]], axis=1)
        made = []
        for t, values in enumerate((even, odd)):
            hi, lo = split(values)
            made.append(mm(wix[t], jnp.concatenate([hi, lo, hi], axis=0)))
        value = [
            jnp.concatenate(
                [
                    jnp.concatenate([field_pot[i, pl.ds(32 * x + z, 8, stride=4), :] for i in range(2)], axis=1)
                    for x in range(f * U // 8, (f + 1) * U // 8)
                ],
                axis=0,
            )
            for f in range(2)
        ]
        e_re, e_im, o_im, o_re = made[0][:, :V], made[0][:, V:], made[1][:, :V], made[1][:, V:]
        planes += [
            (e_re - o_im) * value[0],
            (e_re + o_im) * value[1],
            (e_im + o_re) * value[0],
            (e_im - o_re) * value[1],
        ]
    hi, lo = split(jnp.concatenate(planes, axis=0))
    near[0].wait_recv()
    far[0].start()
    far[1].start()
    near[1].wait_recv()
    far[2].start()
    far[3].start()
    near[2].wait_recv()
    far[4].start()
    near[3].wait_recv()
    far[5].start()

    fwd_y = mm(hi, wfy[...])
    fwd_y = fwd_y[:, :128] + (fwd_y[:, 128:] + mm(lo, wfy[:, 0:128]))
    stack = []
    for z in range(PLANES):
        right = jnp.concatenate([fwd_y[4 * z * U : (4 * z + 2) * U], fwd_y[(4 * z + 2) * U : (4 * z + 4) * U]], axis=1)
        hi, lo = split(right)
        all_hi = mm(wfx[...], hi)
        sums = all_hi[: 2 * KA] + (all_hi[2 * KA :] + mm(wfx[0 : 2 * KA, :], lo))
        c_re, c_im, s_re, s_im = sums[:KA, :128], sums[:KA, 128:], sums[KA:, :128], sums[KA:, 128:]
        real, imag = [], []
        for p, q in ((c_re + s_im, c_im - s_re), (c_re - s_im, c_im + s_re)):
            m, n = jnp.where(low, p, q), jnp.where(low, q, -p)
            m_t, n_t = pltpu.roll(m, KB, 1), pltpu.roll(n, KB, 1)
            real.append(jnp.where(low, m + m_t, m_t - m))
            imag.append(jnp.where(low, n + n_t, n_t - n))
        stack += [jnp.concatenate(real, axis=1), jnp.concatenate(imag, axis=1)]
    hi, lo = split(jnp.concatenate(stack, axis=0))
    picked = [[] for _ in range(6)]
    for a in range(0, 8, 2):
        spread = mm(hi, wide[a // 2]) + mm(lo, wide[a // 2])
        for i in range(2):
            for p in range(6):
                block = spread[p * KA : (p + 1) * KA, 128 * i : 128 * (i + 1)]
                picked[p].append(jnp.sum(jnp.where(on[a + i], block, 0.0), axis=0, keepdims=True))
    picked = [jnp.concatenate(rows, axis=0) for rows in picked] + [jnp.zeros((8, 128), F32)] * 2
    for h in range(2):
        for b in range(4):
            rows = None
            for q in range(4):
                shift = 32 * ((q - b) % 4)
                turned = pltpu.roll(picked[4 * h + q], shift, 1) if shift else picked[4 * h + q]
                rows = turned if q == 0 else jnp.where(lane == q, turned, rows)
            for a in range(8):
                tiles[4 * a + b, h : h + 1, :] = rows[a : a + 1, :]
    ret[me] = tiles[0]

    for dz, dx in OFFSETS:
        pltpu.make_async_remote_copy(
            tiles.at[4 * dz + dx], ret.at[me], sb, rb, device_id={"fft": fft_at(8 - dz, 4 - dx)}, device_id_type=MESH
        ).start()

    total = jnp.sum(parts[1][3], axis=0, keepdims=True)
    total = total + pltpu.roll(total, 64, 1)
    total = total + pltpu.roll(total, 32, 1)
    c_re = jnp.sum(dfull * total[:, 0:16], axis=1, keepdims=True)
    c_im = jnp.sum(dfull * total[:, 16:32], axis=1, keepdims=True)
    for r in range(16):
        lanes = slice(128 * r, 128 * (r + 1))
        p_re, p_im = proj[0, :, lanes], proj[1, :, lanes]
        nonl[0, r : r + 1, :] = jnp.sum(c_re * p_re - c_im * p_im, axis=0, keepdims=True)
        nonl[1, r : r + 1, :] = jnp.sum(c_re * p_im + c_im * p_re, axis=0, keepdims=True)

    def pass_on(k):
        block = pool.at[core, lax.rem(row + k, 8)]
        pltpu.make_async_remote_copy(block, block, sf, rf, device_id={"band": twin}, device_id_type=MESH).start()

    near[4].wait_recv()
    near[5].wait_recv()
    for k in (0, 1, 2, 6, 7):
        pass_on(k)
    for c in far:
        c.wait_recv()
    for k in (3, 4, 5):
        pass_on(k)
    swap = pltpu.make_async_remote_copy(
        pool.at[core], pool.at[core], sf, rf, device_id={"band": twin}, device_id_type=MESH
    )

    def correlate(at, half):
        def step(r4, carry):
            u, w = carry
            for r in range(4):
                block = pool[half, :, :, pl.ds(pl.multiple_of(512 * r4 + 128 * r, 128), 128)]
                u = u + block * vecs[at, pl.ds(4 * r4 + r, 1), :]
                w = w + block * vecs[at + 1, pl.ds(4 * r4 + r, 1), :]
            return u, w

        zero = jnp.zeros((8, 8, 128), F32)
        u, w = lax.fori_loop(0, 4, step, (zero, zero))
        for y in range(8):
            work[at // 2, half, y, 0:4, :] = u[y, 0:4] + w[y, 4:8]
            work[at // 2, half, y, 4:8, :] = w[y, 0:4] - u[y, 4:8]

    vecs[0] = m_re
    vecs[1] = m_im
    base_re = kin * m_re + nonl[0]
    base_im = kin * m_im + nonl[1]
    correlate(0, core)

    every = pltpu.make_async_remote_copy(
        tiles.at[pl.ds(1, NF - 1)], ret.at[pl.ds(0, NF - 1)], sb, rb, device_id={"fft": fft_at(0, 1)}, device_id_type=MESH
    )
    every.wait_recv()
    came = jnp.concatenate([ret[d] for d in range(NF)], axis=0).T
    came = jnp.concatenate([came[STK * q : STK * (q + 1)] for q in range(4)], axis=1)
    hi, lo = split(jnp.concatenate([came * angles[0], came * angles[1]], axis=1))
    loc = mm(jnp.concatenate([hi, lo], axis=0), tback[...])
    loc = loc[:STK, :128] + (loc[:STK, 128:] + loc[STK:, :128])
    loc_re = jnp.concatenate([loc[0:16, :GZ], loc[16:32, :GZ]], axis=1)
    loc_im = jnp.concatenate([loc[0:16, GZ:], loc[16:32, GZ:]], axis=1)
    a_re = jnp.where(mask, base_re + loc_re, 0.0)
    a_im = jnp.where(mask, base_im + loc_im, 0.0)
    vecs[2] = a_re
    vecs[3] = a_im
    out[0] = a_re
    out[1] = a_im
    correlate(2, core)
    swap.wait_recv()
    correlate(0, 1 - core)
    correlate(2, 1 - core)
    order = [(c, k) for c in range(2) for k in range(16)]
    full = jnp.concatenate(
        [work[t, k % 2, k // 2, 4 * c : 4 * c + 4, :] for t in (1, 0) for c, k in order], axis=0
    )
    hi = full.astype(BF16)
    rest = full - hi.astype(F32)
    mid, lo = split(rest)
    one = jnp.ones((8, 128), BF16)
    sums = mm(one, hi, NT) + (mm(one, mid, NT) + mm(one, lo, NT))
    red[me] = jnp.concatenate([sums[0:1, :128], sums[0:1, 128:]], axis=0)
    for dz, dx in OFFSETS:
        pltpu.make_async_remote_copy(
            red.at[me], red.at[me], sr, rr, device_id={"fft": fft_at(dz, dx)}, device_id_type=MESH
        ).start()

    whole.wait_send()
    every.wait_send()
    for c in near:
        c.wait_send()
    for c in far:
        c.wait_send()
    swap.wait_send()
    last = pltpu.make_async_remote_copy(
        red.at[pl.ds(0, NF - 1)], red.at[pl.ds(0, NF - 1)], sr, rr, device_id={"fft": fft_at(0, 1)}, device_id_type=MESH
    )
    last.wait_recv()
    out_sums[...] = jnp.sum(red[...], axis=0)
    last.wait_send()


def finish(applied, sums, out, out_h, out_s):
    out[...] = applied[...]
    for c in range(2):
        out_h[c] = sums[0:1, 64 * c : 64 * (c + 1)]
        out_s[c] = sums[1:2, 64 * c : 64 * (c + 1)]


def shards(orbitals, stick_columns, stick_depths, potential, projectors, atom_projectors, couplings, slab_orbitals):
    args = (
        orbitals.reshape(2, 16, 128),
        stick_columns.reshape(1, STK),
        stick_depths,
        potential,
        projectors,
        atom_projectors,
        couplings,
        slab_orbitals,
    ) + tuple(jnp.asarray(t) for t in tables())
    vmem = pl.BlockSpec(memory_space=pltpu.VMEM)
    hbm = pl.BlockSpec(memory_space=pltpu.HBM)
    dma = pltpu.SemaphoreType.DMA
    applied, sums = pl.pallas_call(
        kernel,
        out_shape=(pltpu.VMEM((2, 16, 128), F32), pltpu.VMEM((2, 128), F32)),
        in_specs=[hbm] * len(args),
        out_specs=(vmem, vmem),
        scratch_shapes=[pltpu.VMEM(a.shape, a.dtype) for a in args]
        + [
            pltpu.VMEM((NF, 2, 128), F32),
            pltpu.VMEM((NF, 2, 128), F32),
            pltpu.VMEM((NF, 2, 128), F32),
            pltpu.VMEM((NF, 2, 128), F32),
            pltpu.VMEM((2, 8, 8, 2048), F32),
            pltpu.VMEM((NF, 2, 128), F32),
            pltpu.VMEM((2, 16, 128), F32),
            pltpu.VMEM((4, 16, 128), F32),
            pltpu.VMEM((2, 8 * U, 128), F32),
            pltpu.VMEM((2, STK, 256), F32),
            pltpu.VMEM((2, 2, 8, 8, 128), F32),
            dma((len(args),)),
        ]
        + [dma] * 4
        + [dma((6,))] * 4
        + [dma] * 4,
        compiler_params=pltpu.CompilerParams(
            collective_id=0, has_side_effects=True, vmem_limit_bytes=65024 * 1024
        ),
        name="davidson",
    )(*args)
    applied, proj_h, proj_s = pl.pallas_call(
        finish,
        out_shape=(
            jax.ShapeDtypeStruct((2, 16, 128), F32),
            jax.ShapeDtypeStruct((2, 1, 64), F32),
            jax.ShapeDtypeStruct((2, 1, 64), F32),
        ),
        in_specs=[vmem, vmem],
        out_specs=(vmem, vmem, vmem),
        compiler_params=pltpu.CompilerParams(vmem_limit_bytes=1024 * 1024),
        name="finish",
    )(applied, sums)
    return applied.reshape(2, 1, 2048), proj_h, proj_s


def solution(mesh):
    in_specs = (
        P(None, "band", "fft"),
        P("fft"),
        P("fft", None),
        P("fft", None),
        P(None, None, "fft"),
        P(),
        P(),
        P(None, "band", "fft"),
    )
    out_specs = (P(None, "band", "fft"), P(None, "band", None), P(None, "band", None))
    return jax.shard_map(shards, mesh=mesh, in_specs=in_specs, out_specs=out_specs, check_vma=False)
```

```python
import functools
import math

import jax
import jax.numpy as jnp
import ml_dtypes
import numpy as np
from jax import lax
from jax.experimental import pallas as pl
from jax.experimental.pallas import tpu as pltpu
from jax.sharding import PartitionSpec as P

NX = 180
NY = 180
NZ = 96
GZ = 64
RADIUS = 45
NXY = NX * NY
NF = 32
STK = 32
KA = 48
KB = 64
U = 96
V = 256
PLANES = 3

MESH = pl.DeviceIdType.MESH
HIGHEST = lax.Precision.HIGHEST
F32 = jnp.float32
BF16 = jnp.bfloat16
NN = (((1,), (0,)), ((), ()))
NT = (((1,), (1,)), ((), ()))


def mm(a, b, dims=NN, precision=None):
    return lax.dot_general(a, b, dims, precision=precision, preferred_element_type=F32)


def split(x):
    hi = x.astype(BF16)
    return hi, (x - hi.astype(F32)).astype(BF16)


def mm_right(a, table, dims=NN):
    hi, lo = split(a)
    return mm(hi, table[0], dims) + (mm(lo, table[0], dims) + mm(hi, table[1], dims))


def mm_left(table, b, dims=NN):
    hi, lo = split(b)
    return mm(table[0], hi, dims) + (mm(table[0], lo, dims) + mm(table[1], hi, dims))


def far_first():
    hops = lambda o: min(o[0], 8 - o[0]) + min(o[1], 4 - o[1])
    every = [(dz, dx) for dz in range(8) for dx in range(4)]
    return sorted((o for o in every if o != (0, 0)), key=lambda o: (-hops(o), o))


OFFSETS = far_first()


@functools.lru_cache(maxsize=None)
def tables():
    tau = 2.0 * math.pi
    j = np.arange(GZ)
    depth = np.arange(NZ + 1)
    t1 = np.zeros((4, NF, 2, 2, GZ))
    t2 = np.zeros((4, NF, 2, 2, GZ))
    tb = np.zeros((2, GZ, 2, 4, NF, 2))
    turn = np.zeros((2, 4, NF, 2, 128))
    for d in range(NF):
        for p in range(2 * PLANES):
            h, q = p // 4, p % 4
            z = PLANES * d + p // 2
            th = tau * (j * z % NZ) / NZ
            c, s = np.cos(th), np.sin(th)
            if p % 2 == 0:
                t1[q, d, h] = c, -s
                t2[q, d, h] = -s, -c
                tb[0, :, 0, q, d, h], tb[0, :, 1, q, d, h] = c, -s
                tb[1, :, 0, q, d, h], tb[1, :, 1, q, d, h] = -s, -c
            else:
                t1[q, d, h] = s, c
                t2[q, d, h] = c, -s
                tb[0, :, 0, q, d, h], tb[0, :, 1, q, d, h] = s, c
                tb[1, :, 0, q, d, h], tb[1, :, 1, q, d, h] = c, -s
            ph = tau * (depth * z % NZ) / NZ
            turn[0, q, d, h, : NZ + 1] = np.cos(ph)
            turn[1, q, d, h, : NZ + 1] = np.sin(ph)
    n = RADIUS + 1
    k = np.arange(n)
    ang = tau * ((k[:, None] * np.arange(NY)[None, :]) % NY) / NY
    wiy = np.zeros((2, KB, V))
    wiy[0, :n, :NY], wiy[1, :n, :NY] = np.cos(ang) / NY, np.sin(ang) / NY
    wfy = np.zeros((V, 2, KB))
    wfy[:NY, 0, :n], wfy[:NY, 1, :n] = np.cos(ang).T, np.sin(ang).T
    g = np.arange(NX // 2 + 1)
    ang = tau * ((k[:, None] * g[None, :]) % NX) / NX
    c, s = np.cos(ang), np.sin(ang)
    wix = np.zeros((2, U, KA))
    wix[0, : len(g), :n], wix[1, : len(g), :n] = c.T / NX, s.T / NX
    wfx = np.zeros((2, KA, 2, U))
    wfx[0, :n, 0, : len(g)], wfx[0, :n, 1, : len(g)] = c, c
    wfx[1, :n, 0, : len(g)], wfx[1, :n, 1, : len(g)] = s, -s
    back = np.transpose(tb.reshape(2, GZ, 2, 256), (0, 3, 2, 1)).reshape(512, 2 * GZ)
    tz = np.concatenate([t1.reshape(256, 128), t2.reshape(256, 128)], axis=0) / NZ

    def parts(x):
        x = np.asarray(x, np.float32)
        hi = x.astype(ml_dtypes.bfloat16)
        lo = (x - hi.astype(np.float32)).astype(ml_dtypes.bfloat16)
        return np.stack([hi, lo])

    yh, yl = parts(wiy.reshape(2 * KB, V))
    xh, xl = parts(wix)
    fh, fl = parts(wfy.reshape(V, 2 * KB))
    gh, gl = parts(wfx.reshape(2 * KA, 2 * U))
    return (
        parts(tz),
        parts(turn.reshape(512, 128)),
        np.concatenate([yh, yh, yl], axis=0),
        np.concatenate([xh, xh, xl], axis=2),
        np.concatenate([fh, fl], axis=1),
        np.concatenate([gh, gl], axis=0),
        np.concatenate(list(parts(back)), axis=1),
    )


def kernel(
    orb_h, cols_h, deps_h, pot_h, proj_h, atoms_h, coup_h, slab_h, tz_h, turn_h, wiy_h, wix_h, wfy_h, wfx_h, tback_h,
    out, out_sums,
    orb, cols, deps, pot, proj, atoms, coup, slab, tz, turn, wiy, wix, wfy, wfx, tback,
    mine, got, tiles, ret, pool, red, nonl, vecs, field_pot, angles, work,
    loads, sa, ra, sb, rb, near_s, near_r, far_s, far_r, sf, rf, sr, rr,
):
    me = lax.axis_index("fft")
    band = lax.axis_index("band")
    my_z, my_x = me // 4, lax.rem(me, 4)
    core = lax.rem(band, 2)
    row = band // 2
    twin = band + 1 - 2 * core

    def fft_at(dz, dx):
        return lax.rem(my_z + dz, 8) * 4 + lax.rem(my_x + dx, 4)

    def band_at(dy):
        return lax.rem(band + 2 * dy, 16)

    barrier = pltpu.get_barrier_semaphore()
    for dz, dx in OFFSETS:
        pl.semaphore_signal(barrier, inc=1, device_id={"fft": fft_at(dz, dx)}, device_id_type=MESH)
    for dy in (2, 6, 1, 7):
        pl.semaphore_signal(barrier, inc=1, device_id={"band": band_at(dy)}, device_id_type=MESH)
    pl.semaphore_signal(barrier, inc=1, device_id={"band": twin}, device_id_type=MESH)

    pairs = (
        (orb_h, orb), (deps_h, deps), (cols_h, cols), (tz_h, tz), (turn_h, turn), (proj_h, proj), (slab_h, slab),
        (pot_h, pot), (atoms_h, atoms), (coup_h, coup), (wiy_h, wiy), (wix_h, wix), (wfy_h, wfy), (wfx_h, wfx),
        (tback_h, tback),
    )
    copies = [pltpu.make_async_copy(a, b, loads.at[i]) for i, (a, b) in enumerate(pairs)]
    for c in copies:
        c.start()
    for c in copies[:5]:
        c.wait()

    dep_even = deps[pl.ds(0, 16, stride=2), :]
    dep_odd = deps[pl.ds(1, 16, stride=2), :]
    dep16 = jnp.concatenate([dep_even, dep_odd], axis=1)
    mask = dep16 < NZ
    m_re = jnp.where(mask, orb[0], 0.0)
    m_im = jnp.where(mask, orb[1], 0.0)
    x2 = jnp.concatenate(
        [
            jnp.concatenate([m_re[:, :GZ], m_im[:, :GZ]], axis=1),
            jnp.concatenate([m_re[:, GZ:], m_im[:, GZ:]], axis=1),
        ],
        axis=0,
    )
    x2 = jnp.concatenate([x2] * 4, axis=0)
    d12 = mm_left(tz, x2, NT)

    dep32 = jnp.concatenate([dep_even, dep_odd] * 4, axis=0).astype(F32)
    first = (lax.broadcasted_iota(jnp.int32, (8, GZ), 1) == 0).astype(F32)
    dep0 = mm(first, dep32, NT)
    hot = (lax.broadcasted_iota(jnp.int32, (128, 128), 0).astype(F32) == dep0[0:1, :]).astype(F32).astype(BF16)
    phase = mm(turn[0], hot) + mm(turn[1], hot)
    cosp, sinp = phase[:256], phase[256:]

    colf = cols[...].astype(F32)
    qx = jnp.floor((colf + 0.5) * (1.0 / NY))
    qy = colf - NY * qx
    live = cols[...] < NXY
    far_x, far_y = qx >= 90.0, qy >= 90.0
    kx = jnp.where(live, jnp.where(far_x, NX - qx, qx), 63.0)
    ky = jnp.where(live, jnp.where(far_y, NY - qy, qy), 0.0)
    col = ky + jnp.where(far_x, 2.0 * KB, 0.0) + jnp.where(far_y, 1.0 * KB, 0.0)
    si = lax.broadcasted_iota(jnp.int32, (STK, 128), 0)
    so = lax.rem(lax.broadcasted_iota(jnp.int32, (STK, 128), 1), 32)
    perm = (si == 2 * lax.rem(so, 16) + so // 16).astype(F32)
    kxy = mm(jnp.concatenate([kx, col, jnp.zeros((6, STK), F32)], axis=0), perm)
    code = kxy[0:1, :] * 256.0 + kxy[1:2, :]

    copies[5].wait()
    acc_re = jnp.zeros((16, 128), F32)
    acc_im = jnp.zeros((16, 128), F32)
    for r in range(16):
        lanes = slice(128 * r, 128 * (r + 1))
        p_re, p_im = proj[0, :, lanes], proj[1, :, lanes]
        a, b = m_re[r : r + 1, :], m_im[r : r + 1, :]
        acc_re += a * p_re + b * p_im
        acc_im += b * p_re - a * p_im
    ones = jnp.ones((8, 128), F32)
    part = mm(ones, jnp.concatenate([acc_re, acc_im] * 4, axis=0), NT, HIGHEST)

    field = cosp * d12[:256] + sinp * d12[256:]
    group = lax.broadcasted_iota(jnp.int32, (64, 128), 1) // 32
    odd = lax.rem(lax.broadcasted_iota(jnp.int32, (64, 128), 0), 2) == 1
    message = jnp.where(
        group == 0,
        field[0:64],
        jnp.where(
            group == 1,
            field[64:128],
            jnp.where(
                group == 2,
                jnp.where(odd, jnp.broadcast_to(code, (64, 128)), field[128:192]),
                jnp.where(odd, jnp.broadcast_to(part[0:1, :], (64, 128)), field[192:256]),
            ),
        ),
    )
    for d in range(NF):
        mine[d] = message[2 * d : 2 * d + 2]
    got[0] = mine[me]

    copies[6].wait()
    pool[core, row] = jnp.concatenate([slab[0], slab[1]], axis=0)

    pl.semaphore_wait(barrier, NF - 1 + 4 + 1)

    for dz, dx in OFFSETS:
        to = fft_at(dz, dx)
        pltpu.make_async_remote_copy(
            mine.at[to], got.at[4 * dz + dx], sa, ra.at[dz], device_id={"fft": to}, device_id_type=MESH
        ).start()

    def to_band(src, dst, send, recv, dy):
        return pltpu.make_async_remote_copy(
            src, dst, send, recv, device_id={"band": band_at(dy)}, device_id_type=MESH
        )

    own = pool.at[core, row]
    first_half, second_half = pl.ds(0, 1024), pl.ds(1024, 1024)
    near = [
        to_band(src, src, near_s.at[i], near_r.at[i], dy)
        for i, (src, dy) in enumerate(
            (
                (own.at[:, first_half], 2),
                (own.at[:, second_half], 6),
                (own.at[:, second_half], 2),
                (own.at[:, first_half], 6),
                (own, 1),
                (own, 7),
            )
        )
    ]
    for c in near:
        c.start()

    angles[0] = cosp.T[:STK]
    angles[1] = sinp.T[:STK]

    sr_i = lax.broadcasted_iota(jnp.int32, (16, STK), 1) // 2
    rr_i = lax.broadcasted_iota(jnp.int32, (16, STK), 0)
    s_i = lax.broadcasted_iota(jnp.int32, (STK, 128), 0)
    l_i = lax.broadcasted_iota(jnp.int32, (STK, 128), 1)
    half = (lax.rem(s_i, 2) == l_i // GZ).astype(F32)
    kx16 = mm(jnp.where(sr_i == rr_i, jnp.broadcast_to(kx, (16, STK)), 0.0), half)
    ky16 = mm(jnp.where(sr_i == rr_i, jnp.broadcast_to(ky, (16, STK)), 0.0), half)
    fz = jnp.where(dep16 < NZ // 2, dep16, dep16 - NZ).astype(F32)
    kin = (0.5 / (RADIUS * RADIUS)) * (kx16 * kx16 + ky16 * ky16 + fz * fz)

    for c in copies[7:]:
        c.wait()

    dfull = jnp.zeros((16, 16), F32)
    p_i = lax.broadcasted_iota(jnp.int32, (16, 8), 0)
    for a in range(2):
        owner = (p_i == jnp.broadcast_to(atoms[a : a + 1, :], (16, 8))).astype(F32)
        dfull += mm(mm(owner, coup[a], NN, HIGHEST), owner, NT, HIGHEST)

    field_pot[...] = jnp.zeros_like(field_pot)
    for x in range(NX):
        r = 4 * (x if x <= NX // 2 else U + NX - x)
        field_pot[0, r : r + PLANES, :] = pot[:, NY * x : NY * x + 128]
        field_pot[1, r : r + PLANES, 0 : NY - 128] = pot[:, NY * x + 128 : NY * x + NY]

    ahead = pool.at[core, lax.rem(row + 6, 8)]
    behind = pool.at[core, lax.rem(row + 2, 8)]
    far = [
        to_band(src, src, far_s.at[i], far_r.at[i], dy)
        for i, (src, dy) in enumerate(
            (
                (ahead.at[:, first_half], 2),
                (ahead.at[:, first_half], 1),
                (behind.at[:, second_half], 6),
                (behind.at[:, second_half], 7),
                (ahead.at[:, second_half], 1),
                (behind.at[:, first_half], 7),
            )
        )
    ]
    def arrival(dz):
        block = got.at[pl.ds(1, 3)] if dz == 0 else got.at[pl.ds(4 * dz, 4)]
        return pltpu.make_async_remote_copy(
            block, block, sa, ra.at[dz], device_id={"fft": fft_at(0, 1)}, device_id_type=MESH
        )

    halves = ((0, 1, 7, 2), (6, 3, 5, 4))
    lane = lax.broadcasted_iota(jnp.int32, (4, 128), 1) // 32
    ix = lax.broadcasted_iota(jnp.int32, (KA, 128), 0).astype(F32)
    iy = lax.broadcasted_iota(jnp.int32, (4 * KB, 128), 0).astype(F32)
    grid = jnp.zeros((12 * KA, 4 * KB), F32)
    total = jnp.zeros((1, 128), F32)
    on, wide = [], []
    for half_of in halves:
        for dz in half_of:
            arrival(dz).wait_recv()
        parts = [[None] * 4 for _ in range(2)]
        for h in range(2):
            for b in range(4):
                rows = jnp.concatenate([got[4 * a + b, h : h + 1, :] for a in half_of], axis=0)
                for q in range(4):
                    shift = 32 * ((b - q) % 4)
                    turned = pltpu.roll(rows, shift, 1) if shift else rows
                    parts[h][q] = turned if b == 0 else jnp.where(lane == b, turned, parts[h][q])
        fields = [parts[p // 4][p % 4] for p in range(6)]
        total += jnp.sum(parts[1][3], axis=0, keepdims=True)
        code = parts[1][2]
        kx_at = jnp.floor(code * (1.0 / 256.0))
        col_at = code - 256.0 * kx_at
        his = [f.astype(BF16).astype(F32) for f in fields]
        los = [f - h for f, h in zip(fields, his)]
        here = [ix == kx_at[a : a + 1, :] for a in range(4)]
        hot_y = [(iy == col_at[a : a + 1, :]).astype(F32).astype(BF16) for a in range(4)]
        placed = jnp.concatenate(
            [
                jnp.concatenate(
                    [jnp.where(here[a], values[p][a : a + 1, :], 0.0).astype(BF16) for a in range(4)], axis=1
                )
                for values in (his, los)
                for p in range(6)
            ],
            axis=0,
        )
        hot_half = jnp.concatenate(hot_y, axis=1)
        grid += mm(placed, hot_half, NT)
        on.append(here)
        wide.append(hot_half)
    grid = grid[: 6 * KA] + grid[6 * KA :]

    low = lax.broadcasted_iota(jnp.int32, (KA, 2 * KB), 1) < KB
    rows = []
    for z in range(PLANES):
        real, imag = grid[2 * z * KA : (2 * z + 1) * KA], grid[(2 * z + 1) * KA : (2 * z + 2) * KA]
        pair = []
        for s in range(2):
            re, im = real[:, 128 * s : 128 * (s + 1)], imag[:, 128 * s : 128 * (s + 1)]
            re_t, im_t = pltpu.roll(re, KB, 1), pltpu.roll(im, KB, 1)
            pair.append((jnp.where(low, re + re_t, im - im_t), jnp.where(low, im + im_t, re_t - re)))
        rows += [pair[0][0], pair[1][0], pair[0][1], pair[1][1]]
    hi, lo = split(jnp.concatenate(rows, axis=0))
    inv_y = mm(jnp.concatenate([hi, lo], axis=1), wiy[0:256, :]) + mm(hi, wiy[256:384, :])

    def pass_on(k):
        block = pool.at[core, lax.rem(row + k, 8)]
        pltpu.make_async_remote_copy(block, block, sf, rf, device_id={"band": twin}, device_id_type=MESH).start()

    near[0].wait_recv()
    far[0].start()
    far[1].start()
    near[1].wait_recv()
    far[2].start()
    far[3].start()
    near[2].wait_recv()
    far[4].start()
    near[3].wait_recv()
    far[5].start()
    for k in (0, 2, 6):
        pass_on(k)
    planes = []
    for z in range(PLANES):
        part4 = [inv_y[(4 * z + i) * KA : (4 * z + i + 1) * KA] for i in range(4)]
        even = jnp.concatenate([part4[0] + part4[1], part4[2] + part4[3]], axis=1)
        odd = jnp.concatenate([part4[2] - part4[3], part4[0] - part4[1]], axis=1)
        made = []
        for t, values in enumerate((even, odd)):
            hi, lo = split(values)
            made.append(mm(wix[t], jnp.concatenate([hi, lo, hi], axis=0)))
        value = [
            jnp.concatenate(
                [
                    jnp.concatenate([field_pot[i, pl.ds(32 * x + z, 8, stride=4), :] for i in range(2)], axis=1)
                    for x in range(f * U // 8, (f + 1) * U // 8)
                ],
                axis=0,
            )
            for f in range(2)
        ]
        e_re, e_im, o_im, o_re = made[0][:, :V], made[0][:, V:], made[1][:, :V], made[1][:, V:]
        planes += [
            (e_re - o_im) * value[0],
            (e_re + o_im) * value[1],
            (e_im + o_re) * value[0],
            (e_im - o_re) * value[1],
        ]
    hi, lo = split(jnp.concatenate(planes, axis=0))

    fwd_y = mm(hi, wfy[...])
    fwd_y = fwd_y[:, :128] + (fwd_y[:, 128:] + mm(lo, wfy[:, 0:128]))
    stack = []
    for z in range(PLANES):
        right = jnp.concatenate([fwd_y[4 * z * U : (4 * z + 2) * U], fwd_y[(4 * z + 2) * U : (4 * z + 4) * U]], axis=1)
        hi, lo = split(right)
        all_hi = mm(wfx[...], hi)
        sums = all_hi[: 2 * KA] + (all_hi[2 * KA :] + mm(wfx[0 : 2 * KA, :], lo))
        c_re, c_im, s_re, s_im = sums[:KA, :128], sums[:KA, 128:], sums[KA:, :128], sums[KA:, 128:]
        real, imag = [], []
        for p, q in ((c_re + s_im, c_im - s_re), (c_re - s_im, c_im + s_re)):
            m, n = jnp.where(low, p, q), jnp.where(low, q, -p)
            m_t, n_t = pltpu.roll(m, KB, 1), pltpu.roll(n, KB, 1)
            real.append(jnp.where(low, m + m_t, m_t - m))
            imag.append(jnp.where(low, n + n_t, n_t - n))
        stack += [jnp.concatenate(real, axis=1), jnp.concatenate(imag, axis=1)]
    hi, lo = split(jnp.concatenate(stack, axis=0))
    both_parts = jnp.concatenate([hi, lo], axis=0)
    for half_of, here, hot_half in ((halves[1], on[1], wide[1]), (halves[0], on[0], wide[0])):
        spread = mm(both_parts, hot_half)
        spread = spread[: 6 * KA] + spread[6 * KA :]
        picked = []
        for p in range(6):
            rows = []
            for a in range(4):
                block = spread[p * KA : (p + 1) * KA, 128 * a : 128 * (a + 1)]
                rows.append(jnp.sum(jnp.where(here[a], block, 0.0), axis=0, keepdims=True))
            picked.append(jnp.concatenate(rows, axis=0))
        picked += [jnp.zeros((4, 128), F32)] * 2
        for h in range(2):
            for b in range(4):
                rows = None
                for q in range(4):
                    shift = 32 * ((q - b) % 4)
                    turned = pltpu.roll(picked[4 * h + q], shift, 1) if shift else picked[4 * h + q]
                    rows = turned if q == 0 else jnp.where(lane == q, turned, rows)
                for a in range(4):
                    tiles[4 * half_of[a] + b, h : h + 1, :] = rows[a : a + 1, :]
        for dz, dx in OFFSETS:
            if dz in half_of:
                pltpu.make_async_remote_copy(
                    tiles.at[4 * dz + dx],
                    ret.at[me],
                    sb,
                    rb,
                    device_id={"fft": fft_at(8 - dz, 4 - dx)},
                    device_id_type=MESH,
                ).start()
    ret[me] = tiles[0]

    total = total + pltpu.roll(total, 64, 1)
    total = total + pltpu.roll(total, 32, 1)
    c_re = jnp.sum(dfull * total[:, 0:16], axis=1, keepdims=True)
    c_im = jnp.sum(dfull * total[:, 16:32], axis=1, keepdims=True)
    for r in range(16):
        lanes = slice(128 * r, 128 * (r + 1))
        p_re, p_im = proj[0, :, lanes], proj[1, :, lanes]
        nonl[0, r : r + 1, :] = jnp.sum(c_re * p_re - c_im * p_im, axis=0, keepdims=True)
        nonl[1, r : r + 1, :] = jnp.sum(c_re * p_im + c_im * p_re, axis=0, keepdims=True)

    near[4].wait_recv()
    near[5].wait_recv()
    for k in (1, 7):
        pass_on(k)
    far[1].wait_recv()
    far[4].wait_recv()
    pass_on(5)
    far[3].wait_recv()
    far[5].wait_recv()
    pass_on(3)
    far[0].wait_recv()
    far[2].wait_recv()
    pass_on(4)
    swap = pltpu.make_async_remote_copy(
        pool.at[core], pool.at[core], sf, rf, device_id={"band": twin}, device_id_type=MESH
    )

    def correlate(at, half):
        def step(r4, carry):
            u, w = carry
            for r in range(4):
                block = pool[half, :, :, pl.ds(pl.multiple_of(512 * r4 + 128 * r, 128), 128)]
                u = u + block * vecs[at, pl.ds(4 * r4 + r, 1), :]
                w = w + block * vecs[at + 1, pl.ds(4 * r4 + r, 1), :]
            return u, w

        zero = jnp.zeros((8, 8, 128), F32)
        u, w = lax.fori_loop(0, 4, step, (zero, zero))
        for y in range(8):
            work[at // 2, half, y, 0:4, :] = u[y, 0:4] + w[y, 4:8]
            work[at // 2, half, y, 4:8, :] = w[y, 0:4] - u[y, 4:8]

    vecs[0] = m_re
    vecs[1] = m_im
    base_re = kin * m_re + nonl[0]
    base_im = kin * m_im + nonl[1]
    correlate(0, core)

    every = pltpu.make_async_remote_copy(
        tiles.at[pl.ds(1, NF - 1)], ret.at[pl.ds(0, NF - 1)], sb, rb, device_id={"fft": fft_at(0, 1)}, device_id_type=MESH
    )
    every.wait_recv()
    came = jnp.concatenate([ret[d] for d in range(NF)], axis=0).T
    came = jnp.concatenate([came[STK * q : STK * (q + 1)] for q in range(4)], axis=1)
    hi, lo = split(jnp.concatenate([came * angles[0], came * angles[1]], axis=1))
    loc = mm(jnp.concatenate([hi, lo], axis=0), tback[...])
    loc = loc[:STK, :128] + (loc[:STK, 128:] + loc[STK:, :128])
    loc_re = jnp.concatenate([loc[0:16, :GZ], loc[16:32, :GZ]], axis=1)
    loc_im = jnp.concatenate([loc[0:16, GZ:], loc[16:32, GZ:]], axis=1)
    a_re = jnp.where(mask, base_re + loc_re, 0.0)
    a_im = jnp.where(mask, base_im + loc_im, 0.0)
    vecs[2] = a_re
    vecs[3] = a_im
    out[0] = a_re
    out[1] = a_im
    correlate(2, core)
    swap.wait_recv()
    correlate(0, 1 - core)
    correlate(2, 1 - core)
    order = [(c, k) for c in range(2) for k in range(16)]
    full = jnp.concatenate(
        [work[t, k % 2, k // 2, 4 * c : 4 * c + 4, :] for t in (1, 0) for c, k in order], axis=0
    )
    hi = full.astype(BF16)
    rest = full - hi.astype(F32)
    mid, lo = split(rest)
    one = jnp.ones((8, 128), BF16)
    sums = mm(one, hi, NT) + (mm(one, mid, NT) + mm(one, lo, NT))
    red[me] = jnp.concatenate([sums[0:1, :128], sums[0:1, 128:]], axis=0)
    for dz, dx in OFFSETS:
        pltpu.make_async_remote_copy(
            red.at[me], red.at[me], sr, rr, device_id={"fft": fft_at(dz, dx)}, device_id_type=MESH
        ).start()

    pltpu.make_async_remote_copy(
        got.at[pl.ds(1, NF - 1)], got.at[pl.ds(1, NF - 1)], sa, ra.at[0], device_id={"fft": fft_at(0, 1)}, device_id_type=MESH
    ).wait_send()
    every.wait_send()
    for c in near:
        c.wait_send()
    for c in far:
        c.wait_send()
    swap.wait_send()
    last = pltpu.make_async_remote_copy(
        red.at[pl.ds(0, NF - 1)], red.at[pl.ds(0, NF - 1)], sr, rr, device_id={"fft": fft_at(0, 1)}, device_id_type=MESH
    )
    last.wait_recv()
    out_sums[...] = jnp.sum(red[...], axis=0)
    last.wait_send()


def finish(applied, sums, out, out_h, out_s):
    out[...] = applied[...]
    for c in range(2):
        out_h[c] = sums[0:1, 64 * c : 64 * (c + 1)]
        out_s[c] = sums[1:2, 64 * c : 64 * (c + 1)]


def shards(orbitals, stick_columns, stick_depths, potential, projectors, atom_projectors, couplings, slab_orbitals):
    args = (
        orbitals.reshape(2, 16, 128),
        stick_columns.reshape(1, STK),
        stick_depths,
        potential,
        projectors,
        atom_projectors,
        couplings,
        slab_orbitals,
    ) + tuple(jnp.asarray(t) for t in tables())
    vmem = pl.BlockSpec(memory_space=pltpu.VMEM)
    hbm = pl.BlockSpec(memory_space=pltpu.HBM)
    dma = pltpu.SemaphoreType.DMA
    applied, sums = pl.pallas_call(
        kernel,
        out_shape=(pltpu.VMEM((2, 16, 128), F32), pltpu.VMEM((2, 128), F32)),
        in_specs=[hbm] * len(args),
        out_specs=(vmem, vmem),
        scratch_shapes=[pltpu.VMEM(a.shape, a.dtype) for a in args]
        + [
            pltpu.VMEM((NF, 2, 128), F32),
            pltpu.VMEM((NF, 2, 128), F32),
            pltpu.VMEM((NF, 2, 128), F32),
            pltpu.VMEM((NF, 2, 128), F32),
            pltpu.VMEM((2, 8, 8, 2048), F32),
            pltpu.VMEM((NF, 2, 128), F32),
            pltpu.VMEM((2, 16, 128), F32),
            pltpu.VMEM((4, 16, 128), F32),
            pltpu.VMEM((2, 8 * U, 128), F32),
            pltpu.VMEM((2, STK, 256), F32),
            pltpu.VMEM((2, 2, 8, 8, 128), F32),
            dma((len(args),)),
        ]
        + [dma, dma((8,)), dma, dma]
        + [dma((6,))] * 4
        + [dma] * 4,
        compiler_params=pltpu.CompilerParams(
            collective_id=0, has_side_effects=True, vmem_limit_bytes=65024 * 1024
        ),
        name="davidson",
    )(*args)
    applied, proj_h, proj_s = pl.pallas_call(
        finish,
        out_shape=(
            jax.ShapeDtypeStruct((2, 16, 128), F32),
            jax.ShapeDtypeStruct((2, 1, 64), F32),
            jax.ShapeDtypeStruct((2, 1, 64), F32),
        ),
        in_specs=[vmem, vmem],
        out_specs=(vmem, vmem, vmem),
        compiler_params=pltpu.CompilerParams(vmem_limit_bytes=1024 * 1024),
        name="finish",
    )(applied, sums)
    return applied.reshape(2, 1, 2048), proj_h, proj_s


def solution(mesh):
    in_specs = (
        P(None, "band", "fft"),
        P("fft"),
        P("fft", None),
        P("fft", None),
        P(None, None, "fft"),
        P(),
        P(),
        P(None, "band", "fft"),
    )
    out_specs = (P(None, "band", "fft"), P(None, "band", None), P(None, "band", None))
    return jax.shard_map(shards, mesh=mesh, in_specs=in_specs, out_specs=out_specs, check_vma=False)
```

```python
import functools
import math

import jax
import jax.numpy as jnp
import ml_dtypes
import numpy as np
from jax import lax
from jax.experimental import pallas as pl
from jax.experimental.pallas import tpu as pltpu
from jax.sharding import PartitionSpec as P

NX = 180
NY = 180
NZ = 96
GZ = 64
RADIUS = 45
NXY = NX * NY
NF = 32
STK = 32
KA = 48
KB = 64
U = 96
V = 256
PLANES = 3

MESH = pl.DeviceIdType.MESH
HIGHEST = lax.Precision.HIGHEST
F32 = jnp.float32
BF16 = jnp.bfloat16
NN = (((1,), (0,)), ((), ()))
NT = (((1,), (1,)), ((), ()))


def mm(a, b, dims=NN, precision=None):
    return lax.dot_general(a, b, dims, precision=precision, preferred_element_type=F32)


def split(x):
    hi = x.astype(BF16)
    return hi, (x - hi.astype(F32)).astype(BF16)


def mm_right(a, table, dims=NN):
    hi, lo = split(a)
    return mm(hi, table[0], dims) + (mm(lo, table[0], dims) + mm(hi, table[1], dims))


def mm_left(table, b, dims=NN):
    hi, lo = split(b)
    return mm(table[0], hi, dims) + (mm(table[0], lo, dims) + mm(table[1], hi, dims))


def far_first():
    hops = lambda o: min(o[0], 8 - o[0]) + min(o[1], 4 - o[1])
    every = [(dz, dx) for dz in range(8) for dx in range(4)]
    return sorted((o for o in every if o != (0, 0)), key=lambda o: (-hops(o), o))


OFFSETS = far_first()


@functools.lru_cache(maxsize=None)
def tables():
    tau = 2.0 * math.pi
    j = np.arange(GZ)
    depth = np.arange(NZ + 1)
    t1 = np.zeros((4, NF, 2, 2, GZ))
    t2 = np.zeros((4, NF, 2, 2, GZ))
    tb = np.zeros((2, GZ, 2, 4, NF, 2))
    turn = np.zeros((2, 4, NF, 2, 128))
    for d in range(NF):
        for p in range(2 * PLANES):
            h, q = p // 4, p % 4
            z = PLANES * d + p // 2
            th = tau * (j * z % NZ) / NZ
            c, s = np.cos(th), np.sin(th)
            if p % 2 == 0:
                t1[q, d, h] = c, -s
                t2[q, d, h] = -s, -c
                tb[0, :, 0, q, d, h], tb[0, :, 1, q, d, h] = c, -s
                tb[1, :, 0, q, d, h], tb[1, :, 1, q, d, h] = -s, -c
            else:
                t1[q, d, h] = s, c
                t2[q, d, h] = c, -s
                tb[0, :, 0, q, d, h], tb[0, :, 1, q, d, h] = s, c
                tb[1, :, 0, q, d, h], tb[1, :, 1, q, d, h] = c, -s
            ph = tau * (depth * z % NZ) / NZ
            turn[0, q, d, h, : NZ + 1] = np.cos(ph)
            turn[1, q, d, h, : NZ + 1] = np.sin(ph)
    n = RADIUS + 1
    k = np.arange(n)
    ang = tau * ((k[:, None] * np.arange(NY)[None, :]) % NY) / NY
    wiy = np.zeros((2, KB, V))
    wiy[0, :n, :NY], wiy[1, :n, :NY] = np.cos(ang) / NY, np.sin(ang) / NY
    wfy = np.zeros((V, 2, KB))
    wfy[:NY, 0, :n], wfy[:NY, 1, :n] = np.cos(ang).T, np.sin(ang).T
    g = np.arange(NX // 2 + 1)
    ang = tau * ((k[:, None] * g[None, :]) % NX) / NX
    c, s = np.cos(ang), np.sin(ang)
    wix = np.zeros((2, U, KA))
    wix[0, : len(g), :n], wix[1, : len(g), :n] = c.T / NX, s.T / NX
    wfx = np.zeros((2, KA, 2, U))
    wfx[0, :n, 0, : len(g)], wfx[0, :n, 1, : len(g)] = c, c
    wfx[1, :n, 0, : len(g)], wfx[1, :n, 1, : len(g)] = s, -s
    back = np.transpose(tb.reshape(2, GZ, 2, 256), (0, 3, 2, 1)).reshape(512, 2 * GZ)
    tz = np.concatenate([t1.reshape(256, 128), t2.reshape(256, 128)], axis=0) / NZ

    def parts(x):
        x = np.asarray(x, np.float32)
        hi = x.astype(ml_dtypes.bfloat16)
        lo = (x - hi.astype(np.float32)).astype(ml_dtypes.bfloat16)
        return np.stack([hi, lo])

    yh, yl = parts(wiy.reshape(2 * KB, V))
    xh, xl = parts(wix)
    fh, fl = parts(wfy.reshape(V, 2 * KB))
    gh, gl = parts(wfx.reshape(2 * KA, 2 * U))
    return (
        parts(tz),
        parts(turn.reshape(512, 128)),
        np.concatenate([yh, yh, yl], axis=0),
        np.concatenate([xh, xh, xl], axis=2),
        np.concatenate([fh, fl], axis=1),
        np.concatenate([gh, gl], axis=0),
        np.concatenate(list(parts(back)), axis=1),
    )


def kernel(
    orb_h, cols_h, deps_h, pot_h, proj_h, atoms_h, coup_h, slab_h, tz_h, turn_h, wiy_h, wix_h, wfy_h, wfx_h, tback_h,
    out, out_sums,
    orb, cols, deps, pot, proj, atoms, coup, slab, tz, turn, wiy, wix, wfy, wfx, tback,
    mine, got, tiles, ret, pool, red, nonl, vecs, field_pot, angles, work,
    loads, sa, ra, sb, rb, near_s, near_r, far_s, far_r, sf, rf, sr, rr,
):
    me = lax.axis_index("fft")
    band = lax.axis_index("band")
    my_z, my_x = me // 4, lax.rem(me, 4)
    core = lax.rem(band, 2)
    row = band // 2
    twin = band + 1 - 2 * core

    def fft_at(dz, dx):
        return lax.rem(my_z + dz, 8) * 4 + lax.rem(my_x + dx, 4)

    def band_at(dy):
        return lax.rem(band + 2 * dy, 16)

    barrier = pltpu.get_barrier_semaphore()
    for dz, dx in OFFSETS:
        pl.semaphore_signal(barrier, inc=1, device_id={"fft": fft_at(dz, dx)}, device_id_type=MESH)
    for dy in (2, 6, 1, 7):
        pl.semaphore_signal(barrier, inc=1, device_id={"band": band_at(dy)}, device_id_type=MESH)
    pl.semaphore_signal(barrier, inc=1, device_id={"band": twin}, device_id_type=MESH)

    pairs = (
        (orb_h, orb), (deps_h, deps), (cols_h, cols), (tz_h, tz), (turn_h, turn), (proj_h, proj), (slab_h, slab),
        (pot_h, pot), (atoms_h, atoms), (coup_h, coup), (wiy_h, wiy), (wix_h, wix), (wfy_h, wfy), (wfx_h, wfx),
        (tback_h, tback),
    )
    copies = [pltpu.make_async_copy(a, b, loads.at[i]) for i, (a, b) in enumerate(pairs)]
    for c in copies:
        c.start()
    for c in copies[:5]:
        c.wait()

    dep_even = deps[pl.ds(0, 16, stride=2), :]
    dep_odd = deps[pl.ds(1, 16, stride=2), :]
    dep16 = jnp.concatenate([dep_even, dep_odd], axis=1)
    mask = dep16 < NZ
    m_re = jnp.where(mask, orb[0], 0.0)
    m_im = jnp.where(mask, orb[1], 0.0)
    x2 = jnp.concatenate(
        [
            jnp.concatenate([m_re[:, :GZ], m_im[:, :GZ]], axis=1),
            jnp.concatenate([m_re[:, GZ:], m_im[:, GZ:]], axis=1),
        ],
        axis=0,
    )
    x2 = jnp.concatenate([x2] * 4, axis=0)
    d12 = mm_left(tz, x2, NT)

    dep32 = jnp.concatenate([dep_even, dep_odd] * 4, axis=0).astype(F32)
    first = (lax.broadcasted_iota(jnp.int32, (8, GZ), 1) == 0).astype(F32)
    dep0 = mm(first, dep32, NT)
    hot = (lax.broadcasted_iota(jnp.int32, (128, 128), 0).astype(F32) == dep0[0:1, :]).astype(F32).astype(BF16)
    phase = mm(turn[0], hot) + mm(turn[1], hot)
    cosp, sinp = phase[:256], phase[256:]

    colf = cols[...].astype(F32)
    qx = jnp.floor((colf + 0.5) * (1.0 / NY))
    qy = colf - NY * qx
    live = cols[...] < NXY
    far_x, far_y = qx >= 90.0, qy >= 90.0
    kx = jnp.where(live, jnp.where(far_x, NX - qx, qx), 63.0)
    ky = jnp.where(live, jnp.where(far_y, NY - qy, qy), 0.0)
    col = ky + jnp.where(far_x, 2.0 * KB, 0.0) + jnp.where(far_y, 1.0 * KB, 0.0)
    si = lax.broadcasted_iota(jnp.int32, (STK, 128), 0)
    so = lax.rem(lax.broadcasted_iota(jnp.int32, (STK, 128), 1), 32)
    perm = (si == 2 * lax.rem(so, 16) + so // 16).astype(F32)
    kxy = mm(jnp.concatenate([kx, col, jnp.zeros((6, STK), F32)], axis=0), perm)
    code = kxy[0:1, :] * 256.0 + kxy[1:2, :]

    copies[5].wait()
    acc_re = jnp.zeros((16, 128), F32)
    acc_im = jnp.zeros((16, 128), F32)
    for r in range(16):
        lanes = slice(128 * r, 128 * (r + 1))
        p_re, p_im = proj[0, :, lanes], proj[1, :, lanes]
        a, b = m_re[r : r + 1, :], m_im[r : r + 1, :]
        acc_re += a * p_re + b * p_im
        acc_im += b * p_re - a * p_im
    ones = jnp.ones((8, 128), F32)
    part = mm(ones, jnp.concatenate([acc_re, acc_im] * 4, axis=0), NT, HIGHEST)

    field = cosp * d12[:256] + sinp * d12[256:]
    group = lax.broadcasted_iota(jnp.int32, (64, 128), 1) // 32
    odd = lax.rem(lax.broadcasted_iota(jnp.int32, (64, 128), 0), 2) == 1
    message = jnp.where(
        group == 0,
        field[0:64],
        jnp.where(
            group == 1,
            field[64:128],
            jnp.where(
                group == 2,
                jnp.where(odd, jnp.broadcast_to(code, (64, 128)), field[128:192]),
                jnp.where(odd, jnp.broadcast_to(part[0:1, :], (64, 128)), field[192:256]),
            ),
        ),
    )
    for d in range(NF):
        mine[d] = message[2 * d : 2 * d + 2]
    got[0] = mine[me]

    copies[6].wait()
    pool[core, row] = jnp.concatenate([slab[0], slab[1]], axis=0)

    pl.semaphore_wait(barrier, NF - 1 + 4 + 1)

    for dz, dx in OFFSETS:
        to = fft_at(dz, dx)
        pltpu.make_async_remote_copy(
            mine.at[to], got.at[4 * dz + dx], sa, ra.at[dz], device_id={"fft": to}, device_id_type=MESH
        ).start()

    def to_band(src, dst, send, recv, dy):
        return pltpu.make_async_remote_copy(
            src, dst, send, recv, device_id={"band": band_at(dy)}, device_id_type=MESH
        )

    own = pool.at[core, row]
    first_half, second_half = pl.ds(0, 1024), pl.ds(1024, 1024)
    near = [
        to_band(src, src, near_s.at[i], near_r.at[i], dy)
        for i, (src, dy) in enumerate(
            (
                (own.at[:, first_half], 2),
                (own.at[:, second_half], 6),
                (own.at[:, second_half], 2),
                (own.at[:, first_half], 6),
                (own, 1),
                (own, 7),
            )
        )
    ]
    for c in near:
        c.start()

    angles[0] = cosp.T[:STK]
    angles[1] = sinp.T[:STK]

    sr_i = lax.broadcasted_iota(jnp.int32, (16, STK), 1) // 2
    rr_i = lax.broadcasted_iota(jnp.int32, (16, STK), 0)
    s_i = lax.broadcasted_iota(jnp.int32, (STK, 128), 0)
    l_i = lax.broadcasted_iota(jnp.int32, (STK, 128), 1)
    half = (lax.rem(s_i, 2) == l_i // GZ).astype(F32)
    kx16 = mm(jnp.where(sr_i == rr_i, jnp.broadcast_to(kx, (16, STK)), 0.0), half)
    ky16 = mm(jnp.where(sr_i == rr_i, jnp.broadcast_to(ky, (16, STK)), 0.0), half)
    fz = jnp.where(dep16 < NZ // 2, dep16, dep16 - NZ).astype(F32)
    kin = (0.5 / (RADIUS * RADIUS)) * (kx16 * kx16 + ky16 * ky16 + fz * fz)

    for c in copies[7:]:
        c.wait()

    dfull = jnp.zeros((16, 16), F32)
    p_i = lax.broadcasted_iota(jnp.int32, (16, 8), 0)
    for a in range(2):
        owner = (p_i == jnp.broadcast_to(atoms[a : a + 1, :], (16, 8))).astype(F32)
        dfull += mm(mm(owner, coup[a], NN, HIGHEST), owner, NT, HIGHEST)

    field_pot[...] = jnp.zeros_like(field_pot)
    for x in range(NX):
        r = 4 * (x if x <= NX // 2 else U + NX - x)
        field_pot[0, r : r + PLANES, :] = pot[:, NY * x : NY * x + 128]
        field_pot[1, r : r + PLANES, 0 : NY - 128] = pot[:, NY * x + 128 : NY * x + NY]

    ahead = pool.at[core, lax.rem(row + 6, 8)]
    behind = pool.at[core, lax.rem(row + 2, 8)]
    far = [
        to_band(src, src, far_s.at[i], far_r.at[i], dy)
        for i, (src, dy) in enumerate(
            (
                (ahead.at[:, first_half], 2),
                (ahead.at[:, first_half], 1),
                (behind.at[:, second_half], 6),
                (behind.at[:, second_half], 7),
                (ahead.at[:, second_half], 1),
                (behind.at[:, first_half], 7),
            )
        )
    ]
    def arrival(dz):
        block = got.at[pl.ds(1, 3)] if dz == 0 else got.at[pl.ds(4 * dz, 4)]
        return pltpu.make_async_remote_copy(
            block, block, sa, ra.at[dz], device_id={"fft": fft_at(0, 1)}, device_id_type=MESH
        )

    halves = ((0, 1, 7, 2), (6, 3, 5, 4))
    lane = lax.broadcasted_iota(jnp.int32, (4, 128), 1) // 32
    ix = lax.broadcasted_iota(jnp.int32, (KA, 128), 0).astype(F32)
    iy = lax.broadcasted_iota(jnp.int32, (4 * KB, 128), 0).astype(F32)
    grid = jnp.zeros((12 * KA, 4 * KB), F32)
    total = jnp.zeros((1, 128), F32)
    on, wide = [], []
    for half_of in halves:
        for dz in half_of:
            arrival(dz).wait_recv()
        parts = [[None] * 4 for _ in range(2)]
        for h in range(2):
            for b in range(4):
                rows = jnp.concatenate([got[4 * a + b, h : h + 1, :] for a in half_of], axis=0)
                for q in range(4):
                    shift = 32 * ((b - q) % 4)
                    turned = pltpu.roll(rows, shift, 1) if shift else rows
                    parts[h][q] = turned if b == 0 else jnp.where(lane == b, turned, parts[h][q])
        fields = [parts[p // 4][p % 4] for p in range(6)]
        total += jnp.sum(parts[1][3], axis=0, keepdims=True)
        code = parts[1][2]
        kx_at = jnp.floor(code * (1.0 / 256.0))
        col_at = code - 256.0 * kx_at
        his = [f.astype(BF16).astype(F32) for f in fields]
        los = [f - h for f, h in zip(fields, his)]
        here = [ix == kx_at[a : a + 1, :] for a in range(4)]
        hot_y = [(iy == col_at[a : a + 1, :]).astype(F32).astype(BF16) for a in range(4)]
        placed = jnp.concatenate(
            [
                jnp.concatenate(
                    [jnp.where(here[a], values[p][a : a + 1, :], 0.0).astype(BF16) for a in range(4)], axis=1
                )
                for values in (his, los)
                for p in range(6)
            ],
            axis=0,
        )
        hot_half = jnp.concatenate(hot_y, axis=1)
        grid += mm(placed, hot_half, NT)
        on.append(here)
        wide.append(hot_half)
    grid = grid[: 6 * KA] + grid[6 * KA :]

    low = lax.broadcasted_iota(jnp.int32, (KA, 2 * KB), 1) < KB
    rows = []
    for z in range(PLANES):
        real, imag = grid[2 * z * KA : (2 * z + 1) * KA], grid[(2 * z + 1) * KA : (2 * z + 2) * KA]
        pair = []
        for s in range(2):
            re, im = real[:, 128 * s : 128 * (s + 1)], imag[:, 128 * s : 128 * (s + 1)]
            re_t, im_t = pltpu.roll(re, KB, 1), pltpu.roll(im, KB, 1)
            pair.append((jnp.where(low, re + re_t, im - im_t), jnp.where(low, im + im_t, re_t - re)))
        rows += [pair[0][0], pair[1][0], pair[0][1], pair[1][1]]
    hi, lo = split(jnp.concatenate(rows, axis=0))
    inv_y = mm(jnp.concatenate([hi, lo], axis=1), wiy[0:256, :]) + mm(hi, wiy[256:384, :])

    def pass_on(k):
        block = pool.at[core, lax.rem(row + k, 8)]
        pltpu.make_async_remote_copy(block, block, sf, rf, device_id={"band": twin}, device_id_type=MESH).start()

    near[0].wait_recv()
    far[0].start()
    far[1].start()
    near[1].wait_recv()
    far[2].start()
    far[3].start()
    near[2].wait_recv()
    far[4].start()
    near[3].wait_recv()
    far[5].start()
    for k in (0, 2, 6):
        pass_on(k)
    planes = []
    for z in range(PLANES):
        part4 = [inv_y[(4 * z + i) * KA : (4 * z + i + 1) * KA] for i in range(4)]
        even = jnp.concatenate([part4[0] + part4[1], part4[2] + part4[3]], axis=1)
        odd = jnp.concatenate([part4[2] - part4[3], part4[0] - part4[1]], axis=1)
        made = []
        for t, values in enumerate((even, odd)):
            hi, lo = split(values)
            made.append(mm(wix[t], jnp.concatenate([hi, lo, hi], axis=0)))
        value = [
            jnp.concatenate(
                [
                    jnp.concatenate([field_pot[i, pl.ds(32 * x + z, 8, stride=4), :] for i in range(2)], axis=1)
                    for x in range(f * U // 8, (f + 1) * U // 8)
                ],
                axis=0,
            )
            for f in range(2)
        ]
        e_re, e_im, o_im, o_re = made[0][:, :V], made[0][:, V:], made[1][:, :V], made[1][:, V:]
        planes += [
            (e_re - o_im) * value[0],
            (e_re + o_im) * value[1],
            (e_im + o_re) * value[0],
            (e_im - o_re) * value[1],
        ]
    hi, lo = split(jnp.concatenate(planes, axis=0))

    fwd_y = mm(hi, wfy[...])
    fwd_y = fwd_y[:, :128] + (fwd_y[:, 128:] + mm(lo, wfy[:, 0:128]))
    stack = []
    for z in range(PLANES):
        right = jnp.concatenate([fwd_y[4 * z * U : (4 * z + 2) * U], fwd_y[(4 * z + 2) * U : (4 * z + 4) * U]], axis=1)
        hi, lo = split(right)
        all_hi = mm(wfx[...], hi)
        sums = all_hi[: 2 * KA] + (all_hi[2 * KA :] + mm(wfx[0 : 2 * KA, :], lo))
        c_re, c_im, s_re, s_im = sums[:KA, :128], sums[:KA, 128:], sums[KA:, :128], sums[KA:, 128:]
        real, imag = [], []
        for p, q in ((c_re + s_im, c_im - s_re), (c_re - s_im, c_im + s_re)):
            m, n = jnp.where(low, p, q), jnp.where(low, q, -p)
            m_t, n_t = pltpu.roll(m, KB, 1), pltpu.roll(n, KB, 1)
            real.append(jnp.where(low, m + m_t, m_t - m))
            imag.append(jnp.where(low, n + n_t, n_t - n))
        stack += [jnp.concatenate(real, axis=1), jnp.concatenate(imag, axis=1)]
    hi, lo = split(jnp.concatenate(stack, axis=0))
    both_parts = jnp.concatenate([hi, lo], axis=0)
    for half_of, here, hot_half in ((halves[1], on[1], wide[1]), (halves[0], on[0], wide[0])):
        spread = mm(both_parts, hot_half)
        spread = spread[: 6 * KA] + spread[6 * KA :]
        picked = []
        for p in range(6):
            rows = []
            for a in range(4):
                block = spread[p * KA : (p + 1) * KA, 128 * a : 128 * (a + 1)]
                rows.append(jnp.sum(jnp.where(here[a], block, 0.0), axis=0, keepdims=True))
            picked.append(jnp.concatenate(rows, axis=0))
        picked += [jnp.zeros((4, 128), F32)] * 2
        for h in range(2):
            for b in range(4):
                rows = None
                for q in range(4):
                    shift = 32 * ((q - b) % 4)
                    turned = pltpu.roll(picked[4 * h + q], shift, 1) if shift else picked[4 * h + q]
                    rows = turned if q == 0 else jnp.where(lane == q, turned, rows)
                for a in range(4):
                    tiles[4 * half_of[a] + b, h : h + 1, :] = rows[a : a + 1, :]
        for dz, dx in OFFSETS:
            if dz in half_of:
                pltpu.make_async_remote_copy(
                    tiles.at[4 * dz + dx],
                    ret.at[me],
                    sb,
                    rb,
                    device_id={"fft": fft_at(8 - dz, 4 - dx)},
                    device_id_type=MESH,
                ).start()
    ret[me] = tiles[0]

    total = total + pltpu.roll(total, 64, 1)
    total = total + pltpu.roll(total, 32, 1)
    c_re = jnp.sum(dfull * total[:, 0:16], axis=1, keepdims=True)
    c_im = jnp.sum(dfull * total[:, 16:32], axis=1, keepdims=True)
    for r in range(16):
        lanes = slice(128 * r, 128 * (r + 1))
        p_re, p_im = proj[0, :, lanes], proj[1, :, lanes]
        nonl[0, r : r + 1, :] = jnp.sum(c_re * p_re - c_im * p_im, axis=0, keepdims=True)
        nonl[1, r : r + 1, :] = jnp.sum(c_re * p_im + c_im * p_re, axis=0, keepdims=True)

    near[4].wait_recv()
    near[5].wait_recv()
    for k in (1, 7):
        pass_on(k)
    far[1].wait_recv()
    far[4].wait_recv()
    pass_on(5)
    far[3].wait_recv()
    far[5].wait_recv()
    pass_on(3)
    far[0].wait_recv()
    far[2].wait_recv()
    pass_on(4)
    swap = pltpu.make_async_remote_copy(
        pool.at[core], pool.at[core], sf, rf, device_id={"band": twin}, device_id_type=MESH
    )

    def correlate(at, half):
        def step(r4, carry):
            u, w = carry
            for r in range(4):
                block = pool[half, :, :, pl.ds(pl.multiple_of(512 * r4 + 128 * r, 128), 128)]
                u = u + block * vecs[at, pl.ds(4 * r4 + r, 1), :]
                w = w + block * vecs[at + 1, pl.ds(4 * r4 + r, 1), :]
            return u, w

        zero = jnp.zeros((8, 8, 128), F32)
        u, w = lax.fori_loop(0, 4, step, (zero, zero))
        for y in range(8):
            work[at // 2, half, y, 0:4, :] = u[y, 0:4] + w[y, 4:8]
            work[at // 2, half, y, 4:8, :] = w[y, 0:4] - u[y, 4:8]

    def correlate_both(half):
        def step(r4, carry):
            carry = list(carry)
            for r in range(4):
                block = pool[half, :, :, pl.ds(pl.multiple_of(512 * r4 + 128 * r, 128), 128)]
                for i in range(4):
                    carry[i] = carry[i] + block * vecs[i, pl.ds(4 * r4 + r, 1), :]
            return tuple(carry)

        zero = jnp.zeros((8, 8, 128), F32)
        made = lax.fori_loop(0, 4, step, (zero,) * 4)
        for t in range(2):
            u, w = made[2 * t], made[2 * t + 1]
            for y in range(8):
                work[t, half, y, 0:4, :] = u[y, 0:4] + w[y, 4:8]
                work[t, half, y, 4:8, :] = w[y, 0:4] - u[y, 4:8]

    vecs[0] = m_re
    vecs[1] = m_im
    base_re = kin * m_re + nonl[0]
    base_im = kin * m_im + nonl[1]
    correlate(0, core)

    every = pltpu.make_async_remote_copy(
        tiles.at[pl.ds(1, NF - 1)], ret.at[pl.ds(0, NF - 1)], sb, rb, device_id={"fft": fft_at(0, 1)}, device_id_type=MESH
    )
    every.wait_recv()
    came = jnp.concatenate([ret[d] for d in range(NF)], axis=0).T
    came = jnp.concatenate([came[STK * q : STK * (q + 1)] for q in range(4)], axis=1)
    hi, lo = split(jnp.concatenate([came * angles[0], came * angles[1]], axis=1))
    loc = mm(jnp.concatenate([hi, lo], axis=0), tback[...])
    loc = loc[:STK, :128] + (loc[:STK, 128:] + loc[STK:, :128])
    loc_re = jnp.concatenate([loc[0:16, :GZ], loc[16:32, :GZ]], axis=1)
    loc_im = jnp.concatenate([loc[0:16, GZ:], loc[16:32, GZ:]], axis=1)
    a_re = jnp.where(mask, base_re + loc_re, 0.0)
    a_im = jnp.where(mask, base_im + loc_im, 0.0)
    vecs[2] = a_re
    vecs[3] = a_im
    out[0] = a_re
    out[1] = a_im
    correlate(2, core)
    swap.wait_recv()
    correlate_both(1 - core)
    order = [(c, k) for c in range(2) for k in range(16)]
    full = jnp.concatenate(
        [work[t, k % 2, k // 2, 4 * c : 4 * c + 4, :] for t in (1, 0) for c, k in order], axis=0
    )
    hi = full.astype(BF16)
    rest = full - hi.astype(F32)
    mid, lo = split(rest)
    one = jnp.ones((8, 128), BF16)
    sums = mm(one, hi, NT) + (mm(one, mid, NT) + mm(one, lo, NT))
    red[me] = jnp.concatenate([sums[0:1, :128], sums[0:1, 128:]], axis=0)
    for dz, dx in OFFSETS:
        pltpu.make_async_remote_copy(
            red.at[me], red.at[me], sr, rr, device_id={"fft": fft_at(dz, dx)}, device_id_type=MESH
        ).start()

    pltpu.make_async_remote_copy(
        got.at[pl.ds(1, NF - 1)], got.at[pl.ds(1, NF - 1)], sa, ra.at[0], device_id={"fft": fft_at(0, 1)}, device_id_type=MESH
    ).wait_send()
    every.wait_send()
    for c in near:
        c.wait_send()
    for c in far:
        c.wait_send()
    swap.wait_send()
    last = pltpu.make_async_remote_copy(
        red.at[pl.ds(0, NF - 1)], red.at[pl.ds(0, NF - 1)], sr, rr, device_id={"fft": fft_at(0, 1)}, device_id_type=MESH
    )
    last.wait_recv()
    out_sums[...] = jnp.sum(red[...], axis=0)
    last.wait_send()


def finish(applied, sums, out, out_h, out_s):
    out[...] = applied[...]
    for c in range(2):
        out_h[c] = sums[0:1, 64 * c : 64 * (c + 1)]
        out_s[c] = sums[1:2, 64 * c : 64 * (c + 1)]


def shards(orbitals, stick_columns, stick_depths, potential, projectors, atom_projectors, couplings, slab_orbitals):
    args = (
        orbitals.reshape(2, 16, 128),
        stick_columns.reshape(1, STK),
        stick_depths,
        potential,
        projectors,
        atom_projectors,
        couplings,
        slab_orbitals,
    ) + tuple(jnp.asarray(t) for t in tables())
    vmem = pl.BlockSpec(memory_space=pltpu.VMEM)
    hbm = pl.BlockSpec(memory_space=pltpu.HBM)
    dma = pltpu.SemaphoreType.DMA
    applied, sums = pl.pallas_call(
        kernel,
        out_shape=(pltpu.VMEM((2, 16, 128), F32), pltpu.VMEM((2, 128), F32)),
        in_specs=[hbm] * len(args),
        out_specs=(vmem, vmem),
        scratch_shapes=[pltpu.VMEM(a.shape, a.dtype) for a in args]
        + [
            pltpu.VMEM((NF, 2, 128), F32),
            pltpu.VMEM((NF, 2, 128), F32),
            pltpu.VMEM((NF, 2, 128), F32),
            pltpu.VMEM((NF, 2, 128), F32),
            pltpu.VMEM((2, 8, 8, 2048), F32),
            pltpu.VMEM((NF, 2, 128), F32),
            pltpu.VMEM((2, 16, 128), F32),
            pltpu.VMEM((4, 16, 128), F32),
            pltpu.VMEM((2, 8 * U, 128), F32),
            pltpu.VMEM((2, STK, 256), F32),
            pltpu.VMEM((2, 2, 8, 8, 128), F32),
            dma((len(args),)),
        ]
        + [dma, dma((8,)), dma, dma]
        + [dma((6,))] * 4
        + [dma] * 4,
        compiler_params=pltpu.CompilerParams(
            collective_id=0, has_side_effects=True, vmem_limit_bytes=65024 * 1024
        ),
        name="davidson",
    )(*args)
    applied, proj_h, proj_s = pl.pallas_call(
        finish,
        out_shape=(
            jax.ShapeDtypeStruct((2, 16, 128), F32),
            jax.ShapeDtypeStruct((2, 1, 64), F32),
            jax.ShapeDtypeStruct((2, 1, 64), F32),
        ),
        in_specs=[vmem, vmem],
        out_specs=(vmem, vmem, vmem),
        compiler_params=pltpu.CompilerParams(vmem_limit_bytes=1024 * 1024),
        name="finish",
    )(applied, sums)
    return applied.reshape(2, 1, 2048), proj_h, proj_s


def solution(mesh):
    in_specs = (
        P(None, "band", "fft"),
        P("fft"),
        P("fft", None),
        P("fft", None),
        P(None, None, "fft"),
        P(),
        P(),
        P(None, "band", "fft"),
    )
    out_specs = (P(None, "band", "fft"), P(None, "band", None), P(None, "band", None))
    return jax.shard_map(shards, mesh=mesh, in_specs=in_specs, out_specs=out_specs, check_vma=False)
```
